512 devices in a mesh: box: 128 (over z, y, core), sub: 4 (over x).
Axes of the slice: x: 4, y: 8, z: 8, core: 2. Of those that a mesh axis runs over, the one named last changes fastest.
Arguments:
- rhs_points: bfloat16 [131072, 512], P(('box', 'sub')), may hold values from -6 to 6
- interp: bfloat16 [131072, 256], P(('box', 'sub')), may hold values from -0.375 to 0.375
- skel_count: int32 [128], P('box'), may hold values from 128 to 256, as said below
- butterfly: float32 [3, 32768, 512], P(None, 'box'), may hold values from -0.25 to 0.25
- project: float32 [32768, 256], P('box'), may hold values from -0.375 to 0.375
- root_inverse: float32 [256, 256], replicated, may hold values from -0.03125 to 0.03125
Outputs:
- x_points: float32 [131072, 512], P(('box', 'sub'))
The draws below stay inside these ranges and needn't reach their ends.
Inputs may be any that keep to these rules, and one draw needn't show every extreme that they name: `skel_count`: each box has between 128 and 256 live skeleton rows; some box has exactly 256.
All inputs are finite; a program needn't handle non-finite values.
Results may differ from the reference program's by a relative error of at most 0.0028.
Values may be sent and summed in bfloat16 or wider, within the bound.
A program may use at most 64 MiB of HBM per device.

```python
import jax
import jax.numpy as jnp
from jax import lax

S = 256
R = 512
M_DEV = 256
LEVELS = 3
POINTS = 131072
N_BOX = 128
N_SUB = 4
DEVICES = 512


def draw_skel_count(key, part):
    key = jax.random.fold_in(key, 7)
    first_key, second_key = jax.random.split(key)
    counts = jax.random.randint(first_key, (N_BOX,), S // 2, S + 1)
    chosen = jax.random.randint(second_key, (), 0, N_BOX)
    positions = jnp.arange(N_BOX, dtype=jnp.int32)
    return jnp.where(positions == chosen, S, counts).astype(jnp.int32)


def levels(own_key, extent, cuts, least, high):
    loudness = 1.0
    for dim, shards_of in cuts:
        steps = jax.random.uniform(jax.random.fold_in(jax.random.fold_in(own_key, 6), dim), (shards_of,), jnp.float32, least / len(cuts), high / len(cuts))
        loudness = loudness * jnp.repeat(jnp.exp(steps), extent[dim] // shards_of).reshape((-1,) + (1,) * (len(extent) - 1 - dim))
    return loudness


def scatter_about(own_key, dims, spread, most, pieces=(), held_as=jnp.bfloat16):
    gain = levels(own_key, dims, pieces, -0.22, 0.18) if pieces else 1.0
    values = jax.random.normal(own_key, dims, jnp.float32) * spread * gain
    return jnp.minimum(jnp.maximum(values, -most), most).astype(held_as)


def setup_inputs(seed: int = 0) -> dict:
    splits = jax.random.split(jax.random.key(seed), 7)
    return {
        "rhs_points": scatter_about(splits[0], (POINTS, R), 1.0, 6.0, ((0, 512),)),
        "interp": scatter_about(splits[1], (DEVICES * S, M_DEV), M_DEV ** -0.5, 0.375, ((0, 512),)),
        "skel_count": draw_skel_count(jax.random.fold_in(splits[6], 71), 0),
        "butterfly": scatter_about(splits[3], (LEVELS, N_BOX * S, 2 * S), (2 * S) ** -0.5, 0.25, ((1, 128),), jnp.float32),
        "project": scatter_about(splits[4], (N_BOX * S, S), S ** -0.5, 0.375, ((0, 128),), jnp.float32),
        "root_inverse": scatter_about(splits[5], (S, S), (S * N_BOX) ** -0.5, 0.03125, (), jnp.float32),
    }


def partner_of(blocks, bit_index):
    half = 2 ** bit_index
    shaped = blocks.reshape((-1, 2, half) + blocks.shape[1:])
    return shaped[:, ::-1].reshape(blocks.shape)


def reference(rhs_points, interp, skel_count, butterfly, project, root_inverse):
    highest = lax.Precision.HIGHEST
    rhs_blocks = rhs_points.reshape(N_BOX, N_SUB, M_DEV, R).astype(jnp.float32)
    interp_blocks = interp.reshape(N_BOX, N_SUB, S, M_DEV).astype(jnp.float32)
    rows = jnp.arange(S, dtype=jnp.int32)
    live_rows = (rows[None, :, None] < skel_count[:, None, None]).astype(jnp.float32)
    skeleton = jnp.einsum("bcsm,bcmr->bsr", interp_blocks, rhs_blocks, precision=highest)
    upward = skeleton * live_rows
    factors = butterfly.reshape(LEVELS, N_BOX, S, 2 * S)
    top_bit = N_BOX.bit_length() - 1
    for level in range(LEVELS):
        bit_index = top_bit - LEVELS + level
        own_block = factors[level, :, :, :S]
        cross_block = factors[level, :, :, S:]
        partner = partner_of(upward, bit_index)
        upward = (jnp.einsum("bij,bjr->bir", own_block, upward, precision=highest)
                  + jnp.einsum("bij,bjr->bir", cross_block, partner, precision=highest))
    proj_blocks = project.reshape(N_BOX, S, S)
    root_sum = jnp.einsum("bij,bjr->ir", proj_blocks, upward, precision=highest)
    root_solution = jnp.dot(root_inverse, root_sum, precision=highest)
    downward = upward - jnp.einsum("bji,jr->bir", proj_blocks, root_solution, precision=highest)
    for level in reversed(range(LEVELS)):
        bit_index = top_bit - LEVELS + level
        own_block = factors[level, :, :, :S]
        cross_block = factors[level, :, :, S:]
        sending = jnp.einsum("bji,bjr->bir", cross_block, downward, precision=highest)
        downward = jnp.einsum("bji,bjr->bir", own_block, downward, precision=highest) + partner_of(sending, bit_index)
    back = (downward * live_rows).astype(jnp.bfloat16).astype(jnp.float32)
    result = rhs_blocks - jnp.einsum("bcsm,bsr->bcmr", interp_blocks, back, precision=highest)
    return result.reshape(N_BOX * N_SUB * M_DEV, R)
```

```python
import functools

import jax
import jax.numpy as jnp
from jax import lax
from jax.experimental import pallas as pl
from jax.experimental.pallas import tpu as pltpu
from jax.sharding import PartitionSpec as P

F32 = jnp.float32
BF16 = jnp.bfloat16
MESH = pl.DeviceIdType.MESH
CHUNKS = 2
NN = (((1,), (0,)), ((), ()))
NT = (((1,), (1,)), ((), ()))


def halves(value):
    high = value.astype(BF16)
    return high, (value - high.astype(F32)).astype(BF16)


def dot(left, right, dims):
    return lax.dot_general(left, right, dims, preferred_element_type=F32)


def dot_split(value, high, low, dims):
    rows = value.shape[0]
    value_high, value_low = halves(value)
    both = dot(jnp.concatenate([value_high, value_low], axis=0), high, dims)
    return both[:rows] + (both[rows:] + dot(value_high, low, dims))


def kernel(
    n_y, n_z, n_sub, levels,
    rhs_hbm, interp_hbm, count_ref, butterfly_hbm, project_hbm, inverse_hbm, out_hbm,
    rhs, interp, interp_t, butterfly, project, inverse,
    weight_high, weight_low, project_high, project_low, inverse_high, inverse_low,
    leaf, leaf_in, up, up_in, down_out, down_in,
    sweep, sweep_out, sweep_in, root_map,
    root_part, root_core, root_y, root_mine, root_z, root_piece, root_all,
    back, out,
    load_sem, out_sem, leaf_sem, up_sem, down_sem, sweep_sem, map_sem, core_sem, y_sem, z_sem, spread_sem,
    swap_sem, back_sem,
):
    width = interp.shape[0]
    slice_cols = leaf.shape[1]
    half = slice_cols // 2
    chunk = slice_cols // CHUNKS
    root_rows = width // n_sub
    piece = half // n_y

    box = lax.axis_index("box")
    x = lax.axis_index("sub")
    core = box % 2
    y = (box // 2) % n_y
    z = box // (2 * n_y)

    def at_x(k):
        return (box, (x + k) % n_sub)

    def at_y(k):
        return (z * 2 * n_y + ((y + k) % n_y) * 2 + core, x)

    def at_z(k):
        return (((z + k) % n_z) * 2 * n_y + y * 2 + core, x)

    def sibling(level):
        bit = 2 ** level
        return (box + (1 - 2 * ((z // bit) % 2)) * bit * 2 * n_y, x)

    other_core = (box + 1 - 2 * core, x)

    def send(source, target, sems, index, device):
        copy = pltpu.make_async_remote_copy(
            src_ref=source, dst_ref=target, send_sem=sems.at[0, index], recv_sem=sems.at[1, index],
            device_id=device, device_id_type=MESH,
        )
        copy.start()
        started.append(copy)
        return copy

    started = []

    loads = []
    for source, target in (
        (project_hbm, project), (butterfly_hbm.at[2], butterfly.at[2]), (interp_hbm, interp), (rhs_hbm, rhs),
        (butterfly_hbm.at[1], butterfly.at[1]),
        (butterfly_hbm.at[0], butterfly.at[0]), (inverse_hbm, inverse),
    ):
        load = pltpu.make_async_copy(source, target, load_sem.at[len(loads)])
        load.start()
        loads.append(load)

    barrier = pltpu.get_barrier_semaphore()
    peers = ([at_x(k) for k in range(1, n_sub)] + [at_y(k) for k in range(1, n_y)]
             + [at_z(k) for k in range(1, n_z)] + [other_core])
    for peer in peers:
        pl.semaphore_signal(barrier, inc=1, device_id=peer, device_id_type=MESH)

    def split_level(level):
        high, low = halves(butterfly[level])
        weight_high[level] = high
        weight_low[level] = low

    def own(value, level, dims):
        return dot_split(value, weight_high[level, :, :width], weight_low[level, :, :width], dims)

    def cross(value, level, dims):
        return dot_split(value, weight_high[level, :, width:], weight_low[level, :, width:], dims)

    loads[0].wait()
    loads[1].wait()
    split_level(levels - 1)
    sweep[levels] = project[pl.ds(pl.multiple_of(x * root_rows, root_rows), root_rows), :]
    sweep_out[levels - 1] = cross(sweep[levels], levels - 1, NN)

    pl.semaphore_wait(barrier, len(peers))

    sweep_copies = {}

    def sweep_send(level):
        sweep_copies[level] = send(
            sweep_out.at[level], sweep_in.at[level], sweep_sem, level, sibling(level))

    def sweep_take(level):
        sweep[level] = own(sweep[level + 1], level, NN)
        sweep_copies[level].wait_recv()
        sweep[level] = sweep[level] + sweep_in[level]
        if level > 0:
            sweep_out[level - 1] = cross(sweep[level], level - 1, NN)
            sweep_send(level - 1)

    sweep_send(levels - 1)

    loads[2].wait()
    loads[3].wait()
    interp_value = interp[...]
    leaf_order = sorted(range(n_sub), key=lambda k: (k == 0, -min(k, n_sub - k)))
    leaf_copies = {}
    turned = {}
    for k in leaf_order:
        columns = pl.ds(pl.multiple_of(((x + k) % n_sub) * slice_cols, slice_cols), slice_cols)
        turned[k] = rhs[:, columns].T
    for j in range(CHUNKS):
        rows = pl.ds(j * chunk, chunk)
        for k in leaf_order[:-1]:
            leaf[k, rows] = dot(turned[k][j * chunk:(j + 1) * chunk], interp_value, NT)
            leaf_copies[j, k] = send(leaf.at[k, rows], leaf_in.at[k, rows], leaf_sem, j * n_sub + k, at_x(k))
    leaf[0] = dot(turned[0], interp_value, NT)

    for position, level in ((4, 1), (5, 0)):
        loads[position].wait()
        split_level(level)
    project_high[...], project_low[...] = halves(project[...])
    loads[6].wait()
    inverse_high[...], inverse_low[...] = halves(inverse[...])
    interp_t[...] = interp_value.T
    live = lax.broadcasted_iota(jnp.int32, (chunk, width), 1) < count_ref[0]

    up_copies = {}
    up_own = {}

    def up_send(level, j):
        rows = pl.ds(j * chunk, chunk)
        up_copies[level, j] = send(
            up.at[level, rows], up_in.at[level, rows], up_sem, level * CHUNKS + j, sibling(level))

    def up_start(j):
        rows = pl.ds(j * chunk, chunk)
        total = leaf[0, rows]
        for k in leaf_order[:-1][::-1]:
            leaf_copies[j, k].wait_recv()
            total = total + leaf_in[k, rows]
        up[0, rows] = jnp.where(live, total, 0.0)
        up_send(0, j)
        up_own[j] = own(up[0, rows], 0, NT)

    def up_step(level, j):
        rows = pl.ds(j * chunk, chunk)
        up_copies[level, j].wait_recv()
        up[level + 1, rows] = up_own[j] + cross(up_in[level, rows], level, NT)
        if level + 1 < levels:
            up_send(level + 1, j)
            up_own[j] = own(up[level + 1, rows], level + 1, NT)

    down_copies = {}
    down_own = {}

    def down_send(value, level, j):
        rows = pl.ds(j * chunk, chunk)
        down_out[level, rows] = cross(value, level, NN).astype(BF16)
        down_copies[level, j] = send(
            down_out.at[level, rows], down_in.at[level, rows], down_sem, level * CHUNKS + j, sibling(level))
        down_own[j] = own(value, level, NN)

    def down_take(level, j):
        rows = pl.ds(j * chunk, chunk)
        down_copies[level, j].wait_recv()
        value = down_own[j] + down_in[level, rows].astype(F32)
        if level > 0:
            down_send(value, level - 1, j)
        else:
            leaf[0, rows] = value

    sweep_take(2)
    for j in range(CHUNKS):
        up_start(j)
    sweep_take(1)
    for j in range(CHUNKS):
        up_step(0, j)
    sweep_take(0)
    my_rows = pl.ds(pl.multiple_of(x * root_rows, root_rows), root_rows)
    root_map[my_rows] = sweep[0]
    map_copies = [
        send(sweep.at[0], root_map.at[my_rows], map_sem, k, at_x(k)) for k in range(1, n_sub)]
    for j in range(CHUNKS):
        up_step(1, j)
    for j in range(CHUNKS):
        rows = pl.ds(j * chunk, chunk)
        up_step(2, j)
        value = up[levels, rows]
        root_part[rows] = dot_split(value, project_high[...], project_low[...], NT)
        if j == CHUNKS - 1:
            my_half = pl.ds(pl.multiple_of(core * half, half), half)
            other_half = pl.ds(pl.multiple_of((1 - core) * half, half), half)
            core_copy = send(root_part.at[other_half], root_core, core_sem, 0, other_core)
        down_send(value, levels - 1, j)

    def piece_of(k):
        return pl.ds(pl.multiple_of(((y + k) % n_y) * piece, piece), piece)

    def down_part(level, part):
        for j in range(part * CHUNKS // 2, (part + 1) * CHUNKS // 2):
            down_take(level, j)

    core_copy.wait_recv()
    root_core[...] = root_core[...] + root_part[my_half]
    y_copies = [send(root_core.at[piece_of(k)], root_y.at[k], y_sem, k, at_y(k)) for k in range(1, n_y)]
    down_part(2, 0)
    total = root_core[piece_of(0)]
    for k, copy in enumerate(y_copies, 1):
        copy.wait_recv()
        total = total + root_y[k]
    root_mine[...] = total
    z_copies = [send(root_mine, root_z.at[k], z_sem, k, at_z(k)) for k in range(1, n_z)]
    down_part(2, 1)
    for k, copy in enumerate(z_copies, 1):
        copy.wait_recv()
        total = total + root_z[k]
    padded = jnp.concatenate([total, jnp.zeros_like(total)], axis=0)
    solved = dot_split(padded, inverse_high[...], inverse_low[...], NT)[:piece]
    root_piece[...] = solved
    mine = pl.ds(pl.multiple_of(core * half + y * piece, piece), piece)
    root_all[mine] = solved
    spread_copies = [
        send(root_piece, root_all.at[mine], spread_sem, k, at_y(k)) for k in range(1, n_y)]
    down_part(1, 0)
    for copy in spread_copies:
        copy.wait_recv()
    swap_copy = send(root_all.at[my_half], root_all.at[my_half], swap_sem, 0, other_core)
    down_part(1, 1)
    for copy in map_copies:
        copy.wait_recv()
    map_high, map_low = halves(root_map[...])
    swap_copy.wait_recv()
    root_term = dot_split(root_all[...], map_high, map_low, NN)

    back_copies = {}
    for j in range(CHUNKS):
        rows = pl.ds(j * chunk, chunk)
        down_take(0, j)
        value = leaf[0, rows] - root_term[j * chunk:(j + 1) * chunk]
        spot = pl.ds(pl.multiple_of(x * slice_cols + j * chunk, chunk), chunk)
        back[spot] = jnp.where(live, value, 0.0).astype(BF16)
        for k in leaf_order[:-1]:
            back_copies[j, k] = send(back.at[spot], back.at[spot], back_sem, j * n_sub + k, at_x(k))

    out_copies = []
    for k in (0, *leaf_order[:-1][::-1]):
        columns = pl.ds(pl.multiple_of(((x + n_sub - k) % n_sub) * slice_cols, slice_cols), slice_cols)
        if k:
            for j in range(CHUNKS):
                back_copies[j, k].wait_recv()
        out[:, columns] = rhs[:, columns].astype(F32) - dot(interp_t[...], back[columns], NT)
        copy = pltpu.make_async_copy(out.at[:, columns], out_hbm.at[:, columns], out_sem.at[k])
        copy.start()
        out_copies.append(copy)

    for copy in started:
        copy.wait_send()
    for copy in out_copies:
        copy.wait()


def local(n_y, n_z, n_sub, rhs_points, interp, skel_count, butterfly, project, root_inverse):
    points, columns = rhs_points.shape
    width = interp.shape[0]
    levels = butterfly.shape[0]
    slice_cols = columns // n_sub
    half = slice_cols // 2
    piece = half // n_y
    root_rows = width // n_sub
    vmem = pltpu.VMEM
    pair = lambda count: pltpu.SemaphoreType.DMA((2, count))
    scratch = [
        vmem((points, columns), BF16), vmem((width, points), BF16), vmem((points, width), BF16),
        vmem(butterfly.shape, F32), vmem((width, width), F32), vmem((width, width), F32),
        vmem(butterfly.shape, BF16), vmem(butterfly.shape, BF16),
        vmem((width, width), BF16), vmem((width, width), BF16), vmem((width, width), BF16), vmem((width, width), BF16),
        vmem((n_sub, slice_cols, width), F32), vmem((n_sub, slice_cols, width), F32),
        vmem((levels + 1, slice_cols, width), F32), vmem((levels, slice_cols, width), F32),
        vmem((levels, slice_cols, width), BF16), vmem((levels, slice_cols, width), BF16),
        vmem((levels + 1, root_rows, width), F32), vmem((levels, root_rows, width), F32),
        vmem((levels, root_rows, width), F32), vmem((width, width), F32),
        vmem((slice_cols, width), F32), vmem((half, width), F32), vmem((n_y, piece, width), F32),
        vmem((piece, width), F32), vmem((n_z, piece, width), F32), vmem((piece, width), F32),
        vmem((slice_cols, width), F32),
        vmem((columns, width), BF16), vmem((points, columns), F32),
        pltpu.SemaphoreType.DMA((7,)), pltpu.SemaphoreType.DMA((n_sub,)),
        pair(CHUNKS * n_sub), pair(levels * CHUNKS), pair(levels * CHUNKS), pair(levels), pair(n_sub),
        pair(1), pair(n_y), pair(n_z), pair(n_y), pair(1), pair(CHUNKS * n_sub),
    ]
    anywhere = pl.BlockSpec(memory_space=pl.ANY)
    return pl.pallas_call(
        functools.partial(kernel, n_y, n_z, n_sub, levels),
        out_shape=jax.ShapeDtypeStruct((points, columns), F32),
        in_specs=[anywhere, anywhere, pl.BlockSpec(memory_space=pltpu.SMEM), anywhere, anywhere, anywhere],
        out_specs=anywhere,
        scratch_shapes=scratch,
        compiler_params=pltpu.CompilerParams(
            collective_id=0, has_side_effects=True, vmem_limit_bytes=62 * 2**20),
    )(rhs_points, interp, skel_count, butterfly, project, root_inverse)


def solution(mesh):
    n_box, n_sub = mesh.shape["box"], mesh.shape["sub"]
    n_z = 8
    n_y = n_box // (2 * n_z)
    in_specs = (
        P(("box", "sub"), None),
        P(("box", "sub"), None),
        P("box"),
        P(None, "box", None),
        P("box", None),
        P(),
    )
    out_specs = P(("box", "sub"), None)
    return jax.shard_map(
        functools.partial(local, n_y, n_z, n_sub),
        mesh=mesh, in_specs=in_specs, out_specs=out_specs, check_vma=False)
```

```python
import functools

import jax
import jax.numpy as jnp
from jax import lax
from jax.experimental import pallas as pl
from jax.experimental.pallas import tpu as pltpu
from jax.sharding import PartitionSpec as P

F32 = jnp.float32
BF16 = jnp.bfloat16
MESH = pl.DeviceIdType.MESH
CHUNKS = 2
NN = (((1,), (0,)), ((), ()))
NT = (((1,), (1,)), ((), ()))


def halves(value):
    high = value.astype(BF16)
    return high, (value - high.astype(F32)).astype(BF16)


def dot(left, right, dims):
    return lax.dot_general(left, right, dims, preferred_element_type=F32)


def dot_split(value, high, low, dims):
    rows = value.shape[0]
    value_high, value_low = halves(value)
    both = dot(jnp.concatenate([value_high, value_low], axis=0), high, dims)
    return both[:rows] + (both[rows:] + dot(value_high, low, dims))


def kernel(
    n_y, n_z, n_sub, levels,
    rhs_hbm, interp_hbm, count_ref, butterfly_hbm, project_hbm, inverse_hbm, out_hbm,
    rhs, interp, interp_t, butterfly, inverse,
    weight_high, weight_low, inverse_high, inverse_low,
    leaf, leaf_in, up, up_in, down_out, down_in,
    sweep, sweep_out, sweep_in, step_map, root_map,
    root_part, root_core, root_y, root_mine, root_z, root_piece, root_all,
    back, out,
    load_sem, out_sem, leaf_sem, up_sem, down_sem, sweep_sem, step_sem, map_sem, core_sem, y_sem, z_sem, spread_sem,
    swap_sem, back_sem,
):
    width = interp.shape[0]
    slice_cols = leaf.shape[1]
    half = slice_cols // 2
    chunk = slice_cols // CHUNKS
    root_rows = width // n_sub
    piece = half // n_y

    box = lax.axis_index("box")
    x = lax.axis_index("sub")
    core = box % 2
    y = (box // 2) % n_y
    z = box // (2 * n_y)

    def at_x(k):
        return (box, (x + k) % n_sub)

    def at_y(k):
        return (z * 2 * n_y + ((y + k) % n_y) * 2 + core, x)

    def at_z(k):
        return (((z + k) % n_z) * 2 * n_y + y * 2 + core, x)

    def sibling(level):
        bit = 2 ** level
        return (box + (1 - 2 * ((z // bit) % 2)) * bit * 2 * n_y, x)

    other_core = (box + 1 - 2 * core, x)

    def send(source, target, sems, index, device):
        copy = pltpu.make_async_remote_copy(
            src_ref=source, dst_ref=target, send_sem=sems.at[0, index], recv_sem=sems.at[1, index],
            device_id=device, device_id_type=MESH,
        )
        copy.start()
        started.append(copy)
        return copy

    started = []

    my_rows = pl.ds(pl.multiple_of(x * root_rows, root_rows), root_rows)
    loads = []
    for source, target in (
        (interp_hbm, interp), (rhs_hbm, rhs), (project_hbm.at[my_rows], sweep.at[levels]),
        (butterfly_hbm.at[2], butterfly.at[2]), (butterfly_hbm.at[0], butterfly.at[0]),
        (butterfly_hbm.at[1], butterfly.at[1]), (inverse_hbm, inverse),
    ):
        load = pltpu.make_async_copy(source, target, load_sem.at[len(loads)])
        load.start()
        loads.append(load)

    barrier = pltpu.get_barrier_semaphore()
    peers = ([at_x(k) for k in range(1, n_sub)] + [at_y(k) for k in range(1, n_y)]
             + [at_z(k) for k in range(1, n_z)] + [other_core])
    for peer in peers:
        pl.semaphore_signal(barrier, inc=1, device_id=peer, device_id_type=MESH)

    leaf_order = sorted(range(n_sub), key=lambda k: (k == 0, -min(k, n_sub - k)))
    loads[0].wait()
    loads[1].wait()
    interp_value = interp[...]
    for k in leaf_order:
        columns = pl.ds(pl.multiple_of(((x + k) % n_sub) * slice_cols, slice_cols), slice_cols)
        leaf[k] = dot(rhs[:, columns].T, interp_value, NT)

    pl.semaphore_wait(barrier, len(peers))

    leaf_copies = {}
    for j in range(CHUNKS):
        rows = pl.ds(j * chunk, chunk)
        for k in leaf_order[:-1]:
            leaf_copies[j, k] = send(leaf.at[k, rows], leaf_in.at[k, rows], leaf_sem, j * n_sub + k, at_x(k))

    def split_level(level):
        high, low = halves(butterfly[level])
        weight_high[level] = high
        weight_low[level] = low

    def own(value, level, dims):
        return dot_split(value, weight_high[level, :, :width], weight_low[level, :, :width], dims)

    def cross(value, level, dims):
        return dot_split(value, weight_high[level, :, width:], weight_low[level, :, width:], dims)

    sweep_copies = {}

    def sweep_send(level):
        sweep_out[level] = cross(sweep[level + 1], level, NN)
        sweep_copies[level] = send(
            sweep_out.at[level], sweep_in.at[level], sweep_sem, level, sibling(level))
        sweep[level] = own(sweep[level + 1], level, NN)

    def sweep_take(level):
        sweep_copies[level].wait_recv()
        sweep[level] = sweep[level] + sweep_in[level]
        if level > 0:
            sweep_send(level - 1)

    def gather(level, target, sems):
        target[my_rows] = sweep[level]
        return [send(sweep.at[level], target.at[my_rows], sems, k, at_x(k)) for k in range(1, n_sub)]

    loads[2].wait()
    loads[3].wait()
    split_level(2)
    sweep_send(levels - 1)
    for position, level in ((4, 0), (5, 1)):
        loads[position].wait()
        split_level(level)
    loads[6].wait()
    inverse_high[...], inverse_low[...] = halves(inverse[...])
    interp_t[...] = interp_value.T
    live = lax.broadcasted_iota(jnp.int32, (chunk, width), 1) < count_ref[0]

    up_copies = {}
    up_own = {}

    def up_send(level, j):
        rows = pl.ds(j * chunk, chunk)
        up_copies[level, j] = send(
            up.at[level, rows], up_in.at[level, rows], up_sem, level * CHUNKS + j, sibling(level))

    def up_start(j):
        rows = pl.ds(j * chunk, chunk)
        total = leaf[0, rows]
        for k in leaf_order[:-1][::-1]:
            leaf_copies[j, k].wait_recv()
            total = total + leaf_in[k, rows]
        up[0, rows] = jnp.where(live, total, 0.0)
        up_send(0, j)
        up_own[j] = own(up[0, rows], 0, NT)

    def up_step(level, j):
        rows = pl.ds(j * chunk, chunk)
        up_copies[level, j].wait_recv()
        up[level + 1, rows] = up_own[j] + cross(up_in[level, rows], level, NT)
        if level + 1 < levels:
            up_send(level + 1, j)
            up_own[j] = own(up[level + 1, rows], level + 1, NT)

    down_copies = {}
    down_own = {}

    def down_send(value, level, j):
        rows = pl.ds(j * chunk, chunk)
        down_out[level, rows] = cross(value, level, NN).astype(BF16)
        down_copies[level, j] = send(
            down_out.at[level, rows], down_in.at[level, rows], down_sem, level * CHUNKS + j, sibling(level))
        down_own[j] = own(value, level, NN)

    def down_take(level, j):
        rows = pl.ds(j * chunk, chunk)
        down_copies[level, j].wait_recv()
        value = down_own[j] + down_in[level, rows].astype(F32)
        if level > 0:
            down_send(value, level - 1, j)
        else:
            leaf[0, rows] = value

    def up_part(level, part):
        for j in range(part * CHUNKS // 2, (part + 1) * CHUNKS // 2):
            up_step(level, j)
            if level == levels - 1:
                down_send(up[levels, pl.ds(j * chunk, chunk)], levels - 1, j)

    def down_part(level, part):
        for j in range(part * CHUNKS // 2, (part + 1) * CHUNKS // 2):
            down_take(level, j)

    for j in range(CHUNKS):
        up_start(j)
    sweep_take(2)
    step_copies = gather(2, step_map, step_sem)
    up_part(0, 0)
    up_part(0, 1)
    up_part(1, 0)
    sweep_take(1)
    up_part(1, 1)

    for copy in step_copies:
        copy.wait_recv()
    step_high, step_low = halves(step_map[...])
    root_part[...] = dot_split(up[levels - 1], step_high, step_low, NT)
    my_half = pl.ds(pl.multiple_of(core * half, half), half)
    other_half = pl.ds(pl.multiple_of((1 - core) * half, half), half)
    core_copy = send(root_part.at[other_half], root_core, core_sem, 0, other_core)
    sweep_take(0)
    map_copies = gather(0, root_map, map_sem)

    def piece_of(k):
        return pl.ds(pl.multiple_of(((y + k) % n_y) * piece, piece), piece)

    core_copy.wait_recv()
    root_core[...] = root_core[...] + root_part[my_half]
    y_copies = [send(root_core.at[piece_of(k)], root_y.at[k], y_sem, k, at_y(k)) for k in range(1, n_y)]
    up_part(2, 0)
    total = root_core[piece_of(0)]
    for k, copy in enumerate(y_copies, 1):
        copy.wait_recv()
        total = total + root_y[k]
    root_mine[...] = total
    z_copies = [send(root_mine, root_z.at[k], z_sem, k, at_z(k)) for k in range(1, n_z)]
    up_part(2, 1)
    for k, copy in enumerate(z_copies, 1):
        copy.wait_recv()
        total = total + root_z[k]
    padded = jnp.concatenate([total, jnp.zeros_like(total)], axis=0)
    solved = dot_split(padded, inverse_high[...], inverse_low[...], NT)[:piece]
    root_piece[...] = solved
    mine = pl.ds(pl.multiple_of(core * half + y * piece, piece), piece)
    root_all[mine] = solved
    spread_copies = [
        send(root_piece, root_all.at[mine], spread_sem, k, at_y(k)) for k in range(1, n_y)]
    down_part(2, 0)
    down_part(2, 1)
    for copy in spread_copies:
        copy.wait_recv()
    swap_copy = send(root_all.at[my_half], root_all.at[my_half], swap_sem, 0, other_core)
    down_part(1, 0)
    for copy in map_copies:
        copy.wait_recv()
    map_high, map_low = halves(root_map[...])
    swap_copy.wait_recv()
    root_term = dot_split(root_all[...], map_high, map_low, NN)
    down_part(1, 1)

    back_copies = {}
    for j in range(CHUNKS):
        rows = pl.ds(j * chunk, chunk)
        down_take(0, j)
        value = leaf[0, rows] - root_term[j * chunk:(j + 1) * chunk]
        spot = pl.ds(pl.multiple_of(x * slice_cols + j * chunk, chunk), chunk)
        back[spot] = jnp.where(live, value, 0.0).astype(BF16)
        for k in leaf_order[:-1]:
            back_copies[j, k] = send(back.at[spot], back.at[spot], back_sem, j * n_sub + k, at_x(k))

    out_copies = []
    for k in (0, *leaf_order[:-1][::-1]):
        columns = pl.ds(pl.multiple_of(((x + n_sub - k) % n_sub) * slice_cols, slice_cols), slice_cols)
        if k:
            for j in range(CHUNKS):
                back_copies[j, k].wait_recv()
        out[:, columns] = rhs[:, columns].astype(F32) - dot(interp_t[...], back[columns], NT)
        copy = pltpu.make_async_copy(out.at[:, columns], out_hbm.at[:, columns], out_sem.at[k])
        copy.start()
        out_copies.append(copy)

    for copy in started:
        copy.wait_send()
    for copy in out_copies:
        copy.wait()


def local(n_y, n_z, n_sub, rhs_points, interp, skel_count, butterfly, project, root_inverse):
    points, columns = rhs_points.shape
    width = interp.shape[0]
    levels = butterfly.shape[0]
    slice_cols = columns // n_sub
    half = slice_cols // 2
    piece = half // n_y
    root_rows = width // n_sub
    vmem = pltpu.VMEM
    pair = lambda count: pltpu.SemaphoreType.DMA((2, count))
    scratch = [
        vmem((points, columns), BF16), vmem((width, points), BF16), vmem((points, width), BF16),
        vmem(butterfly.shape, F32), vmem((width, width), F32),
        vmem(butterfly.shape, BF16), vmem(butterfly.shape, BF16),
        vmem((width, width), BF16), vmem((width, width), BF16),
        vmem((n_sub, slice_cols, width), F32), vmem((n_sub, slice_cols, width), F32),
        vmem((levels + 1, slice_cols, width), F32), vmem((levels, slice_cols, width), F32),
        vmem((levels, slice_cols, width), BF16), vmem((levels, slice_cols, width), BF16),
        vmem((levels + 1, root_rows, width), F32), vmem((levels, root_rows, width), F32),
        vmem((levels, root_rows, width), F32), vmem((width, width), F32), vmem((width, width), F32),
        vmem((slice_cols, width), F32), vmem((half, width), F32), vmem((n_y, piece, width), F32),
        vmem((piece, width), F32), vmem((n_z, piece, width), F32), vmem((piece, width), F32),
        vmem((slice_cols, width), F32),
        vmem((columns, width), BF16), vmem((points, columns), F32),
        pltpu.SemaphoreType.DMA((7,)), pltpu.SemaphoreType.DMA((n_sub,)),
        pair(CHUNKS * n_sub), pair(levels * CHUNKS), pair(levels * CHUNKS), pair(levels), pair(n_sub), pair(n_sub),
        pair(1), pair(n_y), pair(n_z), pair(n_y), pair(1), pair(CHUNKS * n_sub),
    ]
    hbm = pl.BlockSpec(memory_space=pl.ANY)
    return pl.pallas_call(
        functools.partial(kernel, n_y, n_z, n_sub, levels),
        out_shape=jax.ShapeDtypeStruct((points, columns), F32),
        in_specs=[hbm, hbm, pl.BlockSpec(memory_space=pltpu.SMEM), hbm, hbm, hbm],
        out_specs=pl.BlockSpec(memory_space=pl.ANY),
        scratch_shapes=scratch,
        compiler_params=pltpu.CompilerParams(
            collective_id=0, has_side_effects=True, vmem_limit_bytes=62 * 2**20),
    )(rhs_points, interp, skel_count, butterfly, project, root_inverse)


def solution(mesh):
    n_box, n_sub = mesh.shape["box"], mesh.shape["sub"]
    n_z = 8
    n_y = n_box // (2 * n_z)
    in_specs = (
        P(("box", "sub"), None),
        P(("box", "sub"), None),
        P("box"),
        P(None, "box", None),
        P("box", None),
        P(),
    )
    out_specs = P(("box", "sub"), None)
    return jax.shard_map(
        functools.partial(local, n_y, n_z, n_sub),
        mesh=mesh, in_specs=in_specs, out_specs=out_specs, check_vma=False)
```

```python
import functools

import jax
import jax.numpy as jnp
from jax import lax
from jax.experimental import pallas as pl
from jax.experimental.pallas import tpu as pltpu
from jax.sharding import PartitionSpec as P

F32 = jnp.float32
BF16 = jnp.bfloat16
MESH = pl.DeviceIdType.MESH
CHUNKS = 2
NN = (((1,), (0,)), ((), ()))
NT = (((1,), (1,)), ((), ()))


def halves(value):
    high = value.astype(BF16)
    return high, (value - high.astype(F32)).astype(BF16)


def dot(left, right, dims):
    return lax.dot_general(left, right, dims, preferred_element_type=F32)


def dot_split(value, high, low, dims):
    rows = value.shape[0]
    if value.dtype == BF16:
        return dot(value, high, dims) + dot(value, low, dims)
    value_high, value_low = halves(value)
    both = dot(jnp.concatenate([value_high, value_low], axis=0), high, dims)
    return both[:rows] + (both[rows:] + dot(value_high, low, dims))


def kernel(
    n_y, n_z, n_sub, levels,
    rhs_hbm, interp_hbm, count_ref, butterfly_hbm, project_hbm, inverse_hbm, out_hbm,
    rhs, interp, interp_t, butterfly, inverse,
    weight_high, weight_low, inverse_high, inverse_low,
    leaf, leaf_in, up, up_wide_in, up_out, up_in, down_wide_out, down_wide_in, down_out, down_in,
    sweep, sweep_out, sweep_in, root_map,
    root_part, root_core, root_y, root_mine, root_z, root_piece, root_all,
    back, out,
    load_sem, out_sem, leaf_sem, up_sem, down_sem, sweep_sem, map_sem, core_sem, y_sem, z_sem, spread_sem,
    swap_sem, back_sem,
):
    width = interp.shape[0]
    slice_cols = leaf.shape[1]
    half = slice_cols // 2
    chunk = slice_cols // CHUNKS
    root_rows = width // n_sub
    piece = half // n_y

    box = lax.axis_index("box")
    x = lax.axis_index("sub")
    core = box % 2
    y = (box // 2) % n_y
    z = box // (2 * n_y)

    def at_x(k):
        return (box, (x + k) % n_sub)

    def at_y(k):
        return (z * 2 * n_y + ((y + k) % n_y) * 2 + core, x)

    def at_z(k):
        return (((z + k) % n_z) * 2 * n_y + y * 2 + core, x)

    def sibling(level):
        bit = 2 ** level
        return (box + (1 - 2 * ((z // bit) % 2)) * bit * 2 * n_y, x)

    other_core = (box + 1 - 2 * core, x)

    def send(source, target, sems, index, device):
        copy = pltpu.make_async_remote_copy(
            src_ref=source, dst_ref=target, send_sem=sems.at[0, index], recv_sem=sems.at[1, index],
            device_id=device, device_id_type=MESH,
        )
        copy.start()
        started.append(copy)
        return copy

    started = []

    my_rows = pl.ds(pl.multiple_of(x * root_rows, root_rows), root_rows)
    loads = []
    for source, target in (
        (interp_hbm, interp), (rhs_hbm, rhs), (project_hbm.at[my_rows], sweep.at[1]),
        (butterfly_hbm.at[2], butterfly.at[2]), (butterfly_hbm.at[0], butterfly.at[0]),
        (butterfly_hbm.at[1], butterfly.at[1]), (inverse_hbm, inverse),
    ):
        load = pltpu.make_async_copy(source, target, load_sem.at[len(loads)])
        load.start()
        loads.append(load)

    barrier = pltpu.get_barrier_semaphore()
    peers = ([at_x(k) for k in range(1, n_sub)] + [at_y(k) for k in range(1, n_y)]
             + [at_z(k) for k in range(1, n_z)] + [other_core])
    for peer in peers:
        pl.semaphore_signal(barrier, inc=1, device_id=peer, device_id_type=MESH)

    leaf_order = sorted(range(n_sub), key=lambda k: (k == 0, -min(k, n_sub - k)))
    loads[0].wait()
    loads[1].wait()
    interp_value = interp[...]
    for k in leaf_order:
        columns = pl.ds(pl.multiple_of(((x + k) % n_sub) * slice_cols, slice_cols), slice_cols)
        leaf[k] = dot(rhs[:, columns].T, interp_value, NT)

    pl.semaphore_wait(barrier, len(peers))

    leaf_copies = {}
    for j in range(CHUNKS):
        rows = pl.ds(j * chunk, chunk)
        for k in leaf_order[:-1]:
            leaf_copies[j, k] = send(leaf.at[k, rows], leaf_in.at[k, rows], leaf_sem, j * n_sub + k, at_x(k))

    def split_level(level):
        high, low = halves(butterfly[level])
        weight_high[level] = high
        weight_low[level] = low

    def own(value, level, dims):
        return dot_split(value, weight_high[level, :, :width], weight_low[level, :, :width], dims)

    def cross(value, level, dims):
        return dot_split(value, weight_high[level, :, width:], weight_low[level, :, width:], dims)

    loads[2].wait()
    loads[3].wait()
    split_level(2)
    sweep_out[...] = cross(sweep[1], levels - 1, NN)
    sweep_copy = send(sweep_out, sweep_in, sweep_sem, 0, sibling(levels - 1))
    sweep[0] = own(sweep[1], levels - 1, NN)
    for position, level in ((4, 0), (5, 1)):
        loads[position].wait()
        split_level(level)
    loads[6].wait()
    inverse_high[...], inverse_low[...] = halves(inverse[...])
    interp_t[...] = interp_value.T
    live = lax.broadcasted_iota(jnp.int32, (chunk, width), 1) < count_ref[0]

    up_copies = {}
    up_own = {}

    def up_send(level, j):
        rows = pl.ds(j * chunk, chunk)
        if level == 0:
            source, target = up.at[0, rows], up_wide_in.at[rows]
        else:
            up_out[level, rows] = up[level, rows].astype(BF16)
            source, target = up_out.at[level, rows], up_in.at[level, rows]
        up_copies[level, j] = send(source, target, up_sem, level * CHUNKS + j, sibling(level))
        up_own[j] = own(up[level, rows], level, NT)

    def up_start(j):
        rows = pl.ds(j * chunk, chunk)
        total = leaf[0, rows]
        for k in leaf_order[:-1][::-1]:
            leaf_copies[j, k].wait_recv()
            total = total + leaf_in[k, rows]
        up[0, rows] = jnp.where(live, total, 0.0)
        up_send(0, j)

    def up_step(level, j):
        rows = pl.ds(j * chunk, chunk)
        up_copies[level, j].wait_recv()
        arrived = up_in[level, rows] if level else up_wide_in[rows]
        up[level + 1, rows] = up_own[j] + cross(arrived, level, NT)
        if level + 1 < levels:
            up_send(level + 1, j)
        else:
            down_send(up[levels, rows], level, j)

    down_copies = {}
    down_own = {}

    def down_send(value, level, j):
        rows = pl.ds(j * chunk, chunk)
        if level == 0:
            down_wide_out[rows] = cross(value, level, NN)
            source, target = down_wide_out.at[rows], down_wide_in.at[rows]
        else:
            down_out[level, rows] = cross(value, level, NN).astype(BF16)
            source, target = down_out.at[level, rows], down_in.at[level, rows]
        down_copies[level, j] = send(source, target, down_sem, level * CHUNKS + j, sibling(level))
        down_own[j] = own(value, level, NN)

    def down_value(level, j):
        rows = pl.ds(j * chunk, chunk)
        down_copies[level, j].wait_recv()
        arrived = down_in[level, rows].astype(F32) if level else down_wide_in[rows]
        return down_own[j] + arrived

    for j in range(CHUNKS):
        up_start(j)
    sweep_copy.wait_recv()
    sweep[0] = sweep[0] + sweep_in[...]
    root_map[my_rows] = sweep[0]
    map_copies = [send(sweep.at[0], root_map.at[my_rows], map_sem, k, at_x(k)) for k in range(1, n_sub)]
    for j in range(CHUNKS):
        up_step(0, j)
    for copy in map_copies:
        copy.wait_recv()
    map_high, map_low = halves(root_map[...])

    my_half = pl.ds(pl.multiple_of(core * half, half), half)
    other_half = pl.ds(pl.multiple_of((1 - core) * half, half), half)
    for j in range(CHUNKS):
        rows = pl.ds(j * chunk, chunk)
        up_step(1, j)
        root_part[rows] = dot_split(up[levels - 1, rows], map_high, map_low, NT)
    core_copy = send(root_part.at[other_half], root_core, core_sem, 0, other_core)

    def piece_of(k):
        return pl.ds(pl.multiple_of(((y + k) % n_y) * piece, piece), piece)

    core_copy.wait_recv()
    root_core[...] = root_core[...] + root_part[my_half]
    y_copies = [send(root_core.at[piece_of(k)], root_y.at[k], y_sem, k, at_y(k)) for k in range(1, n_y)]
    total = root_core[piece_of(0)]
    for k, copy in enumerate(y_copies, 1):
        copy.wait_recv()
        total = total + root_y[k]
    root_mine[...] = total
    z_copies = [send(root_mine, root_z.at[k], z_sem, k, at_z(k)) for k in range(1, n_z)]
    for j in range(CHUNKS):
        up_step(2, j)
    for k, copy in enumerate(z_copies, 1):
        copy.wait_recv()
        total = total + root_z[k]
    padded = jnp.concatenate([total, jnp.zeros_like(total)], axis=0)
    solved = dot_split(padded, inverse_high[...], inverse_low[...], NT)[:piece]
    root_piece[...] = solved
    mine = pl.ds(pl.multiple_of(core * half + y * piece, piece), piece)
    root_all[mine] = solved
    spread_copies = [
        send(root_piece, root_all.at[mine], spread_sem, k, at_y(k)) for k in range(1, n_y)]
    for copy in spread_copies:
        copy.wait_recv()
    swap_copy = send(root_all.at[my_half], root_all.at[my_half], swap_sem, 0, other_core)
    swap_copy.wait_recv()
    root_term = dot_split(root_all[...], map_high, map_low, NN)
    for j in range(CHUNKS):
        down_send(down_value(2, j) - root_term[j * chunk:(j + 1) * chunk], 1, j)
    for j in range(CHUNKS):
        down_send(down_value(1, j), 0, j)

    back_copies = {}
    for j in range(CHUNKS):
        value = down_value(0, j)
        spot = pl.ds(pl.multiple_of(x * slice_cols + j * chunk, chunk), chunk)
        back[spot] = jnp.where(live, value, 0.0).astype(BF16)
        for k in leaf_order[:-1]:
            back_copies[j, k] = send(back.at[spot], back.at[spot], back_sem, j * n_sub + k, at_x(k))

    out_copies = []
    for k in (0, *leaf_order[:-1][::-1]):
        columns = pl.ds(pl.multiple_of(((x + n_sub - k) % n_sub) * slice_cols, slice_cols), slice_cols)
        if k:
            for j in range(CHUNKS):
                back_copies[j, k].wait_recv()
        out[:, columns] = rhs[:, columns].astype(F32) - dot(interp_t[...], back[columns], NT)
        copy = pltpu.make_async_copy(out.at[:, columns], out_hbm.at[:, columns], out_sem.at[k])
        copy.start()
        out_copies.append(copy)

    for copy in started:
        copy.wait_send()
    for copy in out_copies:
        copy.wait()


def local(n_y, n_z, n_sub, rhs_points, interp, skel_count, butterfly, project, root_inverse):
    points, columns = rhs_points.shape
    width = interp.shape[0]
    levels = butterfly.shape[0]
    slice_cols = columns // n_sub
    half = slice_cols // 2
    piece = half // n_y
    root_rows = width // n_sub
    vmem = pltpu.VMEM
    pair = lambda count: pltpu.SemaphoreType.DMA((2, count))
    scratch = [
        vmem((points, columns), BF16), vmem((width, points), BF16), vmem((points, width), BF16),
        vmem(butterfly.shape, F32), vmem((width, width), F32),
        vmem(butterfly.shape, BF16), vmem(butterfly.shape, BF16),
        vmem((width, width), BF16), vmem((width, width), BF16),
        vmem((n_sub, slice_cols, width), F32), vmem((n_sub, slice_cols, width), F32),
        vmem((levels + 1, slice_cols, width), F32), vmem((slice_cols, width), F32),
        vmem((levels, slice_cols, width), BF16), vmem((levels, slice_cols, width), BF16),
        vmem((slice_cols, width), F32), vmem((slice_cols, width), F32),
        vmem((levels, slice_cols, width), BF16), vmem((levels, slice_cols, width), BF16),
        vmem((2, root_rows, width), F32), vmem((root_rows, width), F32), vmem((root_rows, width), F32),
        vmem((width, width), F32),
        vmem((slice_cols, width), F32), vmem((half, width), F32), vmem((n_y, piece, width), F32),
        vmem((piece, width), F32), vmem((n_z, piece, width), F32), vmem((piece, width), F32),
        vmem((slice_cols, width), F32),
        vmem((columns, width), BF16), vmem((points, columns), F32),
        pltpu.SemaphoreType.DMA((7,)), pltpu.SemaphoreType.DMA((n_sub,)),
        pair(CHUNKS * n_sub), pair(levels * CHUNKS), pair(levels * CHUNKS), pair(1), pair(n_sub),
        pair(1), pair(n_y), pair(n_z), pair(n_y), pair(1), pair(CHUNKS * n_sub),
    ]
    hbm = pl.BlockSpec(memory_space=pl.ANY)
    return pl.pallas_call(
        functools.partial(kernel, n_y, n_z, n_sub, levels),
        out_shape=jax.ShapeDtypeStruct((points, columns), F32),
        in_specs=[hbm, hbm, pl.BlockSpec(memory_space=pltpu.SMEM), hbm, hbm, hbm],
        out_specs=pl.BlockSpec(memory_space=pl.ANY),
        scratch_shapes=scratch,
        compiler_params=pltpu.CompilerParams(
            collective_id=0, has_side_effects=True, vmem_limit_bytes=62 * 2**20),
    )(rhs_points, interp, skel_count, butterfly, project, root_inverse)


def solution(mesh):
    n_box, n_sub = mesh.shape["box"], mesh.shape["sub"]
    n_z = 8
    n_y = n_box // (2 * n_z)
    in_specs = (
        P(("box", "sub"), None),
        P(("box", "sub"), None),
        P("box"),
        P(None, "box", None),
        P("box", None),
        P(),
    )
    out_specs = P(("box", "sub"), None)
    return jax.shard_map(
        functools.partial(local, n_y, n_z, n_sub),
        mesh=mesh, in_specs=in_specs, out_specs=out_specs, check_vma=False)
```

```python
import functools

import jax
import jax.numpy as jnp
from jax import lax
from jax.experimental import pallas as pl
from jax.experimental.pallas import tpu as pltpu
from jax.sharding import PartitionSpec as P

F32 = jnp.float32
BF16 = jnp.bfloat16
MESH = pl.DeviceIdType.MESH
CHUNKS = 2
NN = (((1,), (0,)), ((), ()))
NT = (((1,), (1,)), ((), ()))


def halves(value):
    high = value.astype(BF16)
    return high, (value - high.astype(F32)).astype(BF16)


def dot(left, right, dims):
    return lax.dot_general(left, right, dims, preferred_element_type=F32)


def dot_split(value, high, low, dims):
    rows = value.shape[0]
    if value.dtype == BF16:
        return dot(value, high, dims) + dot(value, low, dims)
    value_high, value_low = halves(value)
    both = dot(jnp.concatenate([value_high, value_low], axis=0), high, dims)
    return both[:rows] + (both[rows:] + dot(value_high, low, dims))


def kernel(
    n_y, n_z, n_sub, levels,
    rhs_hbm, interp_hbm, count_ref, butterfly_hbm, project_hbm, inverse_hbm, out_hbm,
    rhs, interp, interp_t, butterfly, inverse,
    weight_high, weight_low, inverse_high, inverse_low,
    leaf, leaf_in, up, up_wide_in, up_out, up_in, down_wide_out, down_wide_in, down_out, down_in,
    sweep, sweep_out, sweep_in, step_map, root_map,
    root_part, root_core, root_y, root_mine, root_z, root_piece, root_all,
    back, out,
    load_sem, out_sem, leaf_sem, up_sem, down_sem, sweep_sem, step_sem, map_sem, core_sem, y_sem, z_sem, spread_sem,
    swap_sem, back_sem,
):
    width = interp.shape[0]
    slice_cols = leaf.shape[1]
    half = slice_cols // 2
    chunk = slice_cols // CHUNKS
    root_rows = width // n_sub
    piece = half // n_y

    box = lax.axis_index("box")
    x = lax.axis_index("sub")
    core = box % 2
    y = (box // 2) % n_y
    z = box // (2 * n_y)

    def at_x(k):
        return (box, (x + k) % n_sub)

    def at_y(k):
        return (z * 2 * n_y + ((y + k) % n_y) * 2 + core, x)

    def at_z(k):
        return (((z + k) % n_z) * 2 * n_y + y * 2 + core, x)

    def sibling(level):
        bit = 2 ** level
        return (box + (1 - 2 * ((z // bit) % 2)) * bit * 2 * n_y, x)

    other_core = (box + 1 - 2 * core, x)

    def send(source, target, sems, index, device):
        copy = pltpu.make_async_remote_copy(
            src_ref=source, dst_ref=target, send_sem=sems.at[0, index], recv_sem=sems.at[1, index],
            device_id=device, device_id_type=MESH,
        )
        copy.start()
        started.append(copy)
        return copy

    started = []

    my_rows = pl.ds(pl.multiple_of(x * root_rows, root_rows), root_rows)
    loads = []
    for source, target in (
        (interp_hbm, interp), (rhs_hbm, rhs), (project_hbm.at[my_rows], sweep.at[levels]),
        (butterfly_hbm.at[2], butterfly.at[2]), (butterfly_hbm.at[0], butterfly.at[0]),
        (butterfly_hbm.at[1], butterfly.at[1]), (inverse_hbm, inverse),
    ):
        load = pltpu.make_async_copy(source, target, load_sem.at[len(loads)])
        load.start()
        loads.append(load)

    barrier = pltpu.get_barrier_semaphore()
    peers = ([at_x(k) for k in range(1, n_sub)] + [at_y(k) for k in range(1, n_y)]
             + [at_z(k) for k in range(1, n_z)] + [other_core])
    for peer in peers:
        pl.semaphore_signal(barrier, inc=1, device_id=peer, device_id_type=MESH)

    leaf_order = sorted(range(n_sub), key=lambda k: (k == 0, -min(k, n_sub - k)))
    loads[0].wait()
    loads[1].wait()
    interp_value = interp[...]
    for k in leaf_order:
        columns = pl.ds(pl.multiple_of(((x + k) % n_sub) * slice_cols, slice_cols), slice_cols)
        leaf[k] = dot(rhs[:, columns].T, interp_value, NT)

    pl.semaphore_wait(barrier, len(peers))

    leaf_copies = {}
    for j in range(CHUNKS):
        rows = pl.ds(j * chunk, chunk)
        for k in leaf_order[:-1]:
            leaf_copies[j, k] = send(leaf.at[k, rows], leaf_in.at[k, rows], leaf_sem, j * n_sub + k, at_x(k))

    def split_level(level):
        high, low = halves(butterfly[level])
        weight_high[level] = high
        weight_low[level] = low

    def own(value, level, dims):
        return dot_split(value, weight_high[level, :, :width], weight_low[level, :, :width], dims)

    def cross(value, level, dims):
        return dot_split(value, weight_high[level, :, width:], weight_low[level, :, width:], dims)

    sweep_copies = {}

    def sweep_send(level):
        sweep_out[level] = cross(sweep[level + 1], level, NN)
        sweep_copies[level] = send(
            sweep_out.at[level], sweep_in.at[level], sweep_sem, level, sibling(level))
        sweep[level] = own(sweep[level + 1], level, NN)

    def sweep_take(level):
        sweep_copies[level].wait_recv()
        sweep[level] = sweep[level] + sweep_in[level]
        if level > 0:
            sweep_send(level - 1)

    def gather(level, target, sems):
        target[my_rows] = sweep[level]
        return [send(sweep.at[level], target.at[my_rows], sems, k, at_x(k)) for k in range(1, n_sub)]

    loads[2].wait()
    loads[3].wait()
    split_level(2)
    sweep_send(levels - 1)
    for position, level in ((4, 0), (5, 1)):
        loads[position].wait()
        split_level(level)
    loads[6].wait()
    inverse_high[...], inverse_low[...] = halves(inverse[...])
    interp_t[...] = interp_value.T
    live = lax.broadcasted_iota(jnp.int32, (chunk, width), 1) < count_ref[0]

    up_copies = {}
    up_own = {}

    def up_send(level, j):
        rows = pl.ds(j * chunk, chunk)
        if level == 0:
            source, target = up.at[0, rows], up_wide_in.at[rows]
        else:
            up_out[level, rows] = up[level, rows].astype(BF16)
            source, target = up_out.at[level, rows], up_in.at[level, rows]
        up_copies[level, j] = send(source, target, up_sem, level * CHUNKS + j, sibling(level))
        up_own[j] = own(up[level, rows], level, NT)

    def up_start(j):
        rows = pl.ds(j * chunk, chunk)
        total = leaf[0, rows]
        for k in leaf_order[:-1][::-1]:
            leaf_copies[j, k].wait_recv()
            total = total + leaf_in[k, rows]
        up[0, rows] = jnp.where(live, total, 0.0)
        up_send(0, j)

    def up_step(level, j):
        rows = pl.ds(j * chunk, chunk)
        up_copies[level, j].wait_recv()
        arrived = up_in[level, rows] if level else up_wide_in[rows]
        up[level + 1, rows] = up_own[j] + cross(arrived, level, NT)
        if level + 1 < levels:
            up_send(level + 1, j)
        else:
            down_send(up[levels, rows], level, j)

    down_copies = {}
    down_own = {}

    def down_send(value, level, j):
        rows = pl.ds(j * chunk, chunk)
        if level == 0:
            down_wide_out[rows] = cross(value, level, NN)
            source, target = down_wide_out.at[rows], down_wide_in.at[rows]
        else:
            down_out[level, rows] = cross(value, level, NN).astype(BF16)
            source, target = down_out.at[level, rows], down_in.at[level, rows]
        down_copies[level, j] = send(source, target, down_sem, level * CHUNKS + j, sibling(level))
        down_own[j] = own(value, level, NN)

    def down_value(level, j):
        rows = pl.ds(j * chunk, chunk)
        down_copies[level, j].wait_recv()
        arrived = down_in[level, rows].astype(F32) if level else down_wide_in[rows]
        return down_own[j] + arrived

    def down_step(level, j):
        down_send(down_value(level, j), level - 1, j)

    def parts(step, level, part):
        for j in range(part * CHUNKS // 2, (part + 1) * CHUNKS // 2):
            step(level, j)

    for j in range(CHUNKS):
        up_start(j)
    sweep_take(2)
    step_copies = gather(2, step_map, step_sem)
    parts(up_step, 0, 0)
    parts(up_step, 0, 1)
    for copy in step_copies:
        copy.wait_recv()
    step_high, step_low = halves(step_map[...])

    my_half = pl.ds(pl.multiple_of(core * half, half), half)
    other_half = pl.ds(pl.multiple_of((1 - core) * half, half), half)
    for j in range(CHUNKS):
        rows = pl.ds(j * chunk, chunk)
        up_step(1, j)
        root_part[rows] = dot_split(up[levels - 1, rows], step_high, step_low, NT)
    core_copy = send(root_part.at[other_half], root_core, core_sem, 0, other_core)
    sweep_take(1)

    def piece_of(k):
        return pl.ds(pl.multiple_of(((y + k) % n_y) * piece, piece), piece)

    core_copy.wait_recv()
    root_core[...] = root_core[...] + root_part[my_half]
    y_copies = [send(root_core.at[piece_of(k)], root_y.at[k], y_sem, k, at_y(k)) for k in range(1, n_y)]
    parts(up_step, 2, 0)
    total = root_core[piece_of(0)]
    for k, copy in enumerate(y_copies, 1):
        copy.wait_recv()
        total = total + root_y[k]
    root_mine[...] = total
    z_copies = [send(root_mine, root_z.at[k], z_sem, k, at_z(k)) for k in range(1, n_z)]
    parts(up_step, 2, 1)
    sweep_take(0)
    map_copies = gather(0, root_map, map_sem)
    for k, copy in enumerate(z_copies, 1):
        copy.wait_recv()
        total = total + root_z[k]
    padded = jnp.concatenate([total, jnp.zeros_like(total)], axis=0)
    solved = dot_split(padded, inverse_high[...], inverse_low[...], NT)[:piece]
    root_piece[...] = solved
    mine = pl.ds(pl.multiple_of(core * half + y * piece, piece), piece)
    root_all[mine] = solved
    spread_copies = [
        send(root_piece, root_all.at[mine], spread_sem, k, at_y(k)) for k in range(1, n_y)]
    parts(down_step, 2, 0)
    parts(down_step, 2, 1)
    for copy in spread_copies:
        copy.wait_recv()
    swap_copy = send(root_all.at[my_half], root_all.at[my_half], swap_sem, 0, other_core)
    parts(down_step, 1, 0)
    parts(down_step, 1, 1)
    for copy in map_copies:
        copy.wait_recv()
    map_high, map_low = halves(root_map[...])
    swap_copy.wait_recv()
    root_term = dot_split(root_all[...], map_high, map_low, NN)

    back_copies = {}
    for j in range(CHUNKS):
        value = down_value(0, j) - root_term[j * chunk:(j + 1) * chunk]
        spot = pl.ds(pl.multiple_of(x * slice_cols + j * chunk, chunk), chunk)
        back[spot] = jnp.where(live, value, 0.0).astype(BF16)
        for k in leaf_order[:-1]:
            back_copies[j, k] = send(back.at[spot], back.at[spot], back_sem, j * n_sub + k, at_x(k))

    out_copies = []
    for k in (0, *leaf_order[:-1][::-1]):
        columns = pl.ds(pl.multiple_of(((x + n_sub - k) % n_sub) * slice_cols, slice_cols), slice_cols)
        if k:
            for j in range(CHUNKS):
                back_copies[j, k].wait_recv()
        out[:, columns] = rhs[:, columns].astype(F32) - dot(interp_t[...], back[columns], NT)
        copy = pltpu.make_async_copy(out.at[:, columns], out_hbm.at[:, columns], out_sem.at[k])
        copy.start()
        out_copies.append(copy)

    for copy in started:
        copy.wait_send()
    for copy in out_copies:
        copy.wait()


def local(n_y, n_z, n_sub, rhs_points, interp, skel_count, butterfly, project, root_inverse):
    points, columns = rhs_points.shape
    width = interp.shape[0]
    levels = butterfly.shape[0]
    slice_cols = columns // n_sub
    half = slice_cols // 2
    piece = half // n_y
    root_rows = width // n_sub
    vmem = pltpu.VMEM
    pair = lambda count: pltpu.SemaphoreType.DMA((2, count))
    scratch = [
        vmem((points, columns), BF16), vmem((width, points), BF16), vmem((points, width), BF16),
        vmem(butterfly.shape, F32), vmem((width, width), F32),
        vmem(butterfly.shape, BF16), vmem(butterfly.shape, BF16),
        vmem((width, width), BF16), vmem((width, width), BF16),
        vmem((n_sub, slice_cols, width), F32), vmem((n_sub, slice_cols, width), F32),
        vmem((levels + 1, slice_cols, width), F32), vmem((slice_cols, width), F32),
        vmem((levels, slice_cols, width), BF16), vmem((levels, slice_cols, width), BF16),
        vmem((slice_cols, width), F32), vmem((slice_cols, width), F32),
        vmem((levels, slice_cols, width), BF16), vmem((levels, slice_cols, width), BF16),
        vmem((levels + 1, root_rows, width), F32), vmem((levels, root_rows, width), F32),
        vmem((levels, root_rows, width), F32), vmem((width, width), F32), vmem((width, width), F32),
        vmem((slice_cols, width), F32), vmem((half, width), F32), vmem((n_y, piece, width), F32),
        vmem((piece, width), F32), vmem((n_z, piece, width), F32), vmem((piece, width), F32),
        vmem((slice_cols, width), F32),
        vmem((columns, width), BF16), vmem((points, columns), F32),
        pltpu.SemaphoreType.DMA((7,)), pltpu.SemaphoreType.DMA((n_sub,)),
        pair(CHUNKS * n_sub), pair(levels * CHUNKS), pair(levels * CHUNKS), pair(levels), pair(n_sub), pair(n_sub),
        pair(1), pair(n_y), pair(n_z), pair(n_y), pair(1), pair(CHUNKS * n_sub),
    ]
    hbm = pl.BlockSpec(memory_space=pl.ANY)
    return pl.pallas_call(
        functools.partial(kernel, n_y, n_z, n_sub, levels),
        out_shape=jax.ShapeDtypeStruct((points, columns), F32),
        in_specs=[hbm, hbm, pl.BlockSpec(memory_space=pltpu.SMEM), hbm, hbm, hbm],
        out_specs=pl.BlockSpec(memory_space=pl.ANY),
        scratch_shapes=scratch,
        compiler_params=pltpu.CompilerParams(
            collective_id=0, has_side_effects=True, vmem_limit_bytes=62 * 2**20),
    )(rhs_points, interp, skel_count, butterfly, project, root_inverse)


def solution(mesh):
    n_box, n_sub = mesh.shape["box"], mesh.shape["sub"]
    n_z = 8
    n_y = n_box // (2 * n_z)
    in_specs = (
        P(("box", "sub"), None),
        P(("box", "sub"), None),
        P("box"),
        P(None, "box", None),
        P("box", None),
        P(),
    )
    out_specs = P(("box", "sub"), None)
    return jax.shard_map(
        functools.partial(local, n_y, n_z, n_sub),
        mesh=mesh, in_specs=in_specs, out_specs=out_specs, check_vma=False)
```

```python
import functools

import jax
import jax.numpy as jnp
from jax import lax
from jax.experimental import pallas as pl
from jax.experimental.pallas import tpu as pltpu
from jax.sharding import PartitionSpec as P

F32 = jnp.float32
BF16 = jnp.bfloat16
MESH = pl.DeviceIdType.MESH
CHUNKS = 2
NN = (((1,), (0,)), ((), ()))
NT = (((1,), (1,)), ((), ()))


def halves(value):
    high = value.astype(BF16)
    return high, (value - high.astype(F32)).astype(BF16)


def dot(left, right, dims):
    return lax.dot_general(left, right, dims, preferred_element_type=F32)


def dot_split(value, high, low, dims):
    rows = value.shape[0]
    if value.dtype == BF16:
        return dot(value, high, dims) + dot(value, low, dims)
    value_high, value_low = halves(value)
    both = dot(jnp.concatenate([value_high, value_low], axis=0), high, dims)
    return both[:rows] + (both[rows:] + dot(value_high, low, dims))


def kernel(
    n_plane, n_z, n_sub, levels,
    rhs_hbm, interp_hbm, count_ref, butterfly_hbm, project_hbm, inverse_hbm, out_hbm,
    rhs, interp, interp_t, butterfly, inverse,
    weight_high, weight_low, inverse_high, inverse_low,
    leaf, leaf_in, up, up_wide_in, up_out, up_in, down_wide_out, down_wide_in, down_out, down_in,
    sweep, sweep_out, sweep_in, step_map, root_map,
    root_part, root_plane, root_mine, root_z, root_piece, root_all,
    back, out,
    load_sem, out_sem, leaf_sem, up_sem, down_sem, sweep_sem, step_sem, map_sem, plane_sem, z_sem, spread_sem, back_sem,
):
    width = interp.shape[0]
    slice_cols = leaf.shape[1]
    chunk = slice_cols // CHUNKS
    root_rows = width // n_sub
    piece = slice_cols // n_plane

    box = lax.axis_index("box")
    x = lax.axis_index("sub")
    place = box % n_plane
    z = box // n_plane

    def at_x(k):
        return (box, (x + k) % n_sub)

    def at_place(k):
        return (z * n_plane + (place + k) % n_plane, x)

    def at_z(k):
        return (((z + k) % n_z) * n_plane + place, x)

    def sibling(level):
        bit = 2 ** level
        return (box + (1 - 2 * ((z // bit) % 2)) * bit * n_plane, x)

    def send(source, target, sems, index, device):
        copy = pltpu.make_async_remote_copy(
            src_ref=source, dst_ref=target, send_sem=sems.at[0, index], recv_sem=sems.at[1, index],
            device_id=device, device_id_type=MESH,
        )
        copy.start()
        started.append(copy)
        return copy

    started = []

    my_rows = pl.ds(pl.multiple_of(x * root_rows, root_rows), root_rows)
    loads = []
    for source, target in (
        (interp_hbm, interp), (rhs_hbm, rhs), (project_hbm.at[my_rows], sweep.at[levels]),
        (butterfly_hbm.at[2], butterfly.at[2]), (butterfly_hbm.at[0], butterfly.at[0]),
        (butterfly_hbm.at[1], butterfly.at[1]), (inverse_hbm, inverse),
    ):
        load = pltpu.make_async_copy(source, target, load_sem.at[len(loads)])
        load.start()
        loads.append(load)

    barrier = pltpu.get_barrier_semaphore()
    peers = ([at_x(k) for k in range(1, n_sub)] + [at_place(k) for k in range(1, n_plane)]
             + [at_z(k) for k in range(1, n_z)])
    for peer in peers:
        pl.semaphore_signal(barrier, inc=1, device_id=peer, device_id_type=MESH)

    leaf_order = sorted(range(n_sub), key=lambda k: (k == 0, -min(k, n_sub - k)))
    leaf_copies = {}

    def leaf_send(j, k):
        rows = pl.ds(j * chunk, chunk)
        leaf_copies[j, k] = send(leaf.at[k, rows], leaf_in.at[k, rows], leaf_sem, j * n_sub + k, at_x(k))

    loads[0].wait()
    loads[1].wait()
    pl.semaphore_wait(barrier, len(peers))
    interp_value = interp[...]
    for k in leaf_order:
        columns = pl.ds(pl.multiple_of(((x + k) % n_sub) * slice_cols, slice_cols), slice_cols)
        leaf[k] = dot(rhs[:, columns].T, interp_value, NT)
        if k:
            leaf_send(0, k)
    for j in range(1, CHUNKS):
        for k in leaf_order[:-1]:
            leaf_send(j, k)

    def split_level(level):
        high, low = halves(butterfly[level])
        weight_high[level] = high
        weight_low[level] = low

    def own(value, level, dims):
        return dot_split(value, weight_high[level, :, :width], weight_low[level, :, :width], dims)

    def cross(value, level, dims):
        return dot_split(value, weight_high[level, :, width:], weight_low[level, :, width:], dims)

    sweep_copies = {}

    def sweep_send(level):
        sweep_out[level] = cross(sweep[level + 1], level, NN)
        sweep_copies[level] = send(
            sweep_out.at[level], sweep_in.at[level], sweep_sem, level, sibling(level))
        sweep[level] = own(sweep[level + 1], level, NN)

    def sweep_take(level):
        sweep_copies[level].wait_recv()
        sweep[level] = sweep[level] + sweep_in[level]
        if level > 0:
            sweep_send(level - 1)

    def gather(level, target, sems):
        target[my_rows] = sweep[level]
        return [send(sweep.at[level], target.at[my_rows], sems, k, at_x(k)) for k in range(1, n_sub)]

    loads[2].wait()
    loads[3].wait()
    split_level(2)
    sweep_send(levels - 1)
    for position, level in ((4, 0), (5, 1)):
        loads[position].wait()
        split_level(level)
    loads[6].wait()
    inverse_high[...], inverse_low[...] = halves(inverse[...])
    interp_t[...] = interp_value.T
    live = lax.broadcasted_iota(jnp.int32, (chunk, width), 1) < count_ref[0]

    up_copies = {}
    up_own = {}

    def up_send(level, j):
        rows = pl.ds(j * chunk, chunk)
        if level == 0:
            source, target = up.at[0, rows], up_wide_in.at[rows]
        else:
            up_out[level, rows] = up[level, rows].astype(BF16)
            source, target = up_out.at[level, rows], up_in.at[level, rows]
        up_copies[level, j] = send(source, target, up_sem, level * CHUNKS + j, sibling(level))
        up_own[j] = own(up[level, rows], level, NT)

    def up_start(j):
        rows = pl.ds(j * chunk, chunk)
        total = leaf[0, rows]
        for k in leaf_order[:-1][::-1]:
            leaf_copies[j, k].wait_recv()
            total = total + leaf_in[k, rows]
        up[0, rows] = jnp.where(live, total, 0.0)
        up_send(0, j)

    def up_step(level, j):
        rows = pl.ds(j * chunk, chunk)
        up_copies[level, j].wait_recv()
        arrived = up_in[level, rows] if level else up_wide_in[rows]
        up[level + 1, rows] = up_own[j] + cross(arrived, level, NT)
        if level + 1 < levels:
            up_send(level + 1, j)
        else:
            down_send(up[levels, rows], level, j)

    down_copies = {}
    down_own = {}

    def down_send(value, level, j):
        rows = pl.ds(j * chunk, chunk)
        if level == 0:
            down_wide_out[rows] = cross(value, level, NN)
            source, target = down_wide_out.at[rows], down_wide_in.at[rows]
        else:
            down_out[level, rows] = cross(value, level, NN).astype(BF16)
            source, target = down_out.at[level, rows], down_in.at[level, rows]
        down_copies[level, j] = send(source, target, down_sem, level * CHUNKS + j, sibling(level))
        down_own[j] = own(value, level, NN)

    def down_value(level, j):
        rows = pl.ds(j * chunk, chunk)
        down_copies[level, j].wait_recv()
        arrived = down_in[level, rows].astype(F32) if level else down_wide_in[rows]
        return down_own[j] + arrived

    def down_step(level, j):
        down_send(down_value(level, j), level - 1, j)

    def parts(step, level, part):
        for j in range(part * CHUNKS // 2, (part + 1) * CHUNKS // 2):
            step(level, j)

    for j in range(CHUNKS):
        up_start(j)
    sweep_take(2)
    step_copies = gather(2, step_map, step_sem)
    parts(up_step, 0, 0)
    parts(up_step, 0, 1)
    for copy in step_copies:
        copy.wait_recv()
    step_high, step_low = halves(step_map[...])

    for j in range(CHUNKS):
        rows = pl.ds(j * chunk, chunk)
        up_step(1, j)
        root_part[rows] = dot_split(up[levels - 1, rows], step_high, step_low, NT)

    def piece_of(k):
        return pl.ds(pl.multiple_of(((place + k) % n_plane) * piece, piece), piece)

    plane_copies = [
        send(root_part.at[piece_of(k)], root_plane.at[k], plane_sem, k, at_place(k)) for k in range(1, n_plane)]
    sweep_take(1)
    parts(up_step, 2, 0)
    total = root_part[piece_of(0)]
    for k, copy in enumerate(plane_copies, 1):
        copy.wait_recv()
        total = total + root_plane[k]
    root_mine[...] = total
    z_copies = [send(root_mine, root_z.at[k], z_sem, k, at_z(k)) for k in range(1, n_z)]
    parts(up_step, 2, 1)
    sweep_take(0)
    map_copies = gather(0, root_map, map_sem)
    parts(down_step, 2, 0)
    for k, copy in enumerate(z_copies, 1):
        copy.wait_recv()
        total = total + root_z[k]
    padded = jnp.concatenate([total, jnp.zeros_like(total)], axis=0)
    solved = dot_split(padded, inverse_high[...], inverse_low[...], NT)[:piece]
    root_piece[...] = solved
    root_all[piece_of(0)] = solved
    spread_copies = [
        send(root_piece, root_all.at[piece_of(0)], spread_sem, k, at_place(k)) for k in range(1, n_plane)]
    parts(down_step, 2, 1)
    parts(down_step, 1, 0)
    parts(down_step, 1, 1)
    for copy in map_copies:
        copy.wait_recv()
    map_high, map_low = halves(root_map[...])
    for copy in spread_copies:
        copy.wait_recv()
    root_term = dot_split(root_all[...], map_high, map_low, NN)

    back_copies = {}
    for j in range(CHUNKS):
        value = down_value(0, j) - root_term[j * chunk:(j + 1) * chunk]
        spot = pl.ds(pl.multiple_of(x * slice_cols + j * chunk, chunk), chunk)
        back[spot] = jnp.where(live, value, 0.0).astype(BF16)
        for k in leaf_order[:-1]:
            back_copies[j, k] = send(back.at[spot], back.at[spot], back_sem, j * n_sub + k, at_x(k))

    out_copies = []
    for k in (0, *leaf_order[:-1][::-1]):
        columns = pl.ds(pl.multiple_of(((x + n_sub - k) % n_sub) * slice_cols, slice_cols), slice_cols)
        if k:
            for j in range(CHUNKS):
                back_copies[j, k].wait_recv()
        out[:, columns] = rhs[:, columns].astype(F32) - dot(interp_t[...], back[columns], NT)
        copy = pltpu.make_async_copy(out.at[:, columns], out_hbm.at[:, columns], out_sem.at[k])
        copy.start()
        out_copies.append(copy)

    for copy in started:
        copy.wait_send()
    for copy in out_copies:
        copy.wait()


def local(n_plane, n_z, n_sub, rhs_points, interp, skel_count, butterfly, project, root_inverse):
    points, columns = rhs_points.shape
    width = interp.shape[0]
    levels = butterfly.shape[0]
    slice_cols = columns // n_sub
    piece = slice_cols // n_plane
    root_rows = width // n_sub
    vmem = pltpu.VMEM
    pair = lambda count: pltpu.SemaphoreType.DMA((2, count))
    scratch = [
        vmem((points, columns), BF16), vmem((width, points), BF16), vmem((points, width), BF16),
        vmem(butterfly.shape, F32), vmem((width, width), F32),
        vmem(butterfly.shape, BF16), vmem(butterfly.shape, BF16),
        vmem((width, width), BF16), vmem((width, width), BF16),
        vmem((n_sub, slice_cols, width), F32), vmem((n_sub, slice_cols, width), F32),
        vmem((levels + 1, slice_cols, width), F32), vmem((slice_cols, width), F32),
        vmem((levels, slice_cols, width), BF16), vmem((levels, slice_cols, width), BF16),
        vmem((slice_cols, width), F32), vmem((slice_cols, width), F32),
        vmem((levels, slice_cols, width), BF16), vmem((levels, slice_cols, width), BF16),
        vmem((levels + 1, root_rows, width), F32), vmem((levels, root_rows, width), F32),
        vmem((levels, root_rows, width), F32), vmem((width, width), F32), vmem((width, width), F32),
        vmem((slice_cols, width), F32), vmem((n_plane, piece, width), F32),
        vmem((piece, width), F32), vmem((n_z, piece, width), F32), vmem((piece, width), F32),
        vmem((slice_cols, width), F32),
        vmem((columns, width), BF16), vmem((points, columns), F32),
        pltpu.SemaphoreType.DMA((7,)), pltpu.SemaphoreType.DMA((n_sub,)),
        pair(CHUNKS * n_sub), pair(levels * CHUNKS), pair(levels * CHUNKS), pair(levels), pair(n_sub), pair(n_sub),
        pair(n_plane), pair(n_z), pair(n_plane), pair(CHUNKS * n_sub),
    ]
    hbm = pl.BlockSpec(memory_space=pl.ANY)
    return pl.pallas_call(
        functools.partial(kernel, n_plane, n_z, n_sub, levels),
        out_shape=jax.ShapeDtypeStruct((points, columns), F32),
        in_specs=[hbm, hbm, pl.BlockSpec(memory_space=pltpu.SMEM), hbm, hbm, hbm],
        out_specs=pl.BlockSpec(memory_space=pl.ANY),
        scratch_shapes=scratch,
        compiler_params=pltpu.CompilerParams(
            collective_id=0, has_side_effects=True, vmem_limit_bytes=62 * 2**20),
    )(rhs_points, interp, skel_count, butterfly, project, root_inverse)


def solution(mesh):
    n_box, n_sub = mesh.shape["box"], mesh.shape["sub"]
    n_z = 8
    in_specs = (
        P(("box", "sub"), None),
        P(("box", "sub"), None),
        P("box"),
        P(None, "box", None),
        P("box", None),
        P(),
    )
    out_specs = P(("box", "sub"), None)
    return jax.shard_map(
        functools.partial(local, n_box // n_z, n_z, n_sub),
        mesh=mesh, in_specs=in_specs, out_specs=out_specs, check_vma=False)
```

```python
import functools

import jax
import jax.numpy as jnp
from jax import lax
from jax.experimental import pallas as pl
from jax.experimental.pallas import tpu as pltpu
from jax.sharding import PartitionSpec as P

F32 = jnp.float32
BF16 = jnp.bfloat16
MESH = pl.DeviceIdType.MESH
CHUNKS = 4
NN = (((1,), (0,)), ((), ()))
NT = (((1,), (1,)), ((), ()))


def halves(value):
    high = value.astype(BF16)
    return high, (value - high.astype(F32)).astype(BF16)


def dot(left, right, dims):
    return lax.dot_general(left, right, dims, preferred_element_type=F32)


def dot_split(value, high, low, dims):
    rows = value.shape[0]
    if value.dtype == BF16:
        return dot(value, high, dims) + dot(value, low, dims)
    value_high, value_low = halves(value)
    both = dot(jnp.concatenate([value_high, value_low], axis=0), high, dims)
    return both[:rows] + (both[rows:] + dot(value_high, low, dims))


def kernel(
    n_plane, n_z, n_sub, levels,
    rhs_hbm, interp_hbm, count_ref, butterfly_hbm, project_hbm, inverse_hbm, out_hbm,
    rhs, interp, interp_t, butterfly, inverse,
    weight_high, weight_low, inverse_high, inverse_low,
    leaf, leaf_in, up, up_wide_in, up_out, up_in, down_wide_out, down_wide_in, down_out, down_in,
    sweep, sweep_out, sweep_in, step_map, root_map,
    root_part, root_plane, root_mine, root_z, root_piece, root_all,
    back, out,
    load_sem, out_sem, leaf_sem, up_sem, down_sem, sweep_sem, step_sem, map_sem, plane_sem, z_sem, spread_sem, back_sem,
):
    width = interp.shape[0]
    slice_cols = leaf.shape[1]
    chunk = slice_cols // CHUNKS
    root_rows = width // n_sub
    piece = slice_cols // n_plane

    box = lax.axis_index("box")
    x = lax.axis_index("sub")
    place = box % n_plane
    z = box // n_plane

    def at_x(k):
        return (box, (x + k) % n_sub)

    def at_place(k):
        return (z * n_plane + (place + k) % n_plane, x)

    def at_z(k):
        return (((z + k) % n_z) * n_plane + place, x)

    def sibling(level):
        bit = 2 ** level
        return (box + (1 - 2 * ((z // bit) % 2)) * bit * n_plane, x)

    def send(source, target, sems, index, device):
        copy = pltpu.make_async_remote_copy(
            src_ref=source, dst_ref=target, send_sem=sems.at[0, index], recv_sem=sems.at[1, index],
            device_id=device, device_id_type=MESH,
        )
        copy.start()
        started.append(copy)
        return copy

    started = []

    my_rows = pl.ds(pl.multiple_of(x * root_rows, root_rows), root_rows)
    loads = []
    for source, target in (
        (interp_hbm, interp), (rhs_hbm, rhs), (project_hbm.at[my_rows], sweep.at[levels]),
        (butterfly_hbm.at[2], butterfly.at[2]), (butterfly_hbm.at[0], butterfly.at[0]),
        (butterfly_hbm.at[1], butterfly.at[1]), (inverse_hbm, inverse),
    ):
        load = pltpu.make_async_copy(source, target, load_sem.at[len(loads)])
        load.start()
        loads.append(load)

    barrier = pltpu.get_barrier_semaphore()
    peers = ([at_x(k) for k in range(1, n_sub)] + [at_place(k) for k in range(1, n_plane)]
             + [at_z(k) for k in range(1, n_z)])
    for peer in peers:
        pl.semaphore_signal(barrier, inc=1, device_id=peer, device_id_type=MESH)

    leaf_order = sorted(range(n_sub), key=lambda k: (k == 0, -min(k, n_sub - k)))
    leaf_copies = {}

    def leaf_send(j, k):
        rows = pl.ds(j * chunk, chunk)
        leaf_copies[j, k] = send(leaf.at[k, rows], leaf_in.at[k, rows], leaf_sem, j * n_sub + k, at_x(k))

    loads[0].wait()
    loads[1].wait()
    pl.semaphore_wait(barrier, len(peers))
    interp_value = interp[...]
    for k in leaf_order:
        columns = pl.ds(pl.multiple_of(((x + k) % n_sub) * slice_cols, slice_cols), slice_cols)
        leaf[k] = dot(rhs[:, columns].T, interp_value, NT)
        if k:
            leaf_send(0, k)
    for j in range(1, CHUNKS):
        for k in leaf_order[:-1]:
            leaf_send(j, k)

    def split_level(level):
        high, low = halves(butterfly[level])
        weight_high[level] = high
        weight_low[level] = low

    def own(value, level, dims):
        return dot_split(value, weight_high[level, :, :width], weight_low[level, :, :width], dims)

    def cross(value, level, dims):
        return dot_split(value, weight_high[level, :, width:], weight_low[level, :, width:], dims)

    sweep_copies = {}

    def sweep_send(level):
        sweep_out[level] = cross(sweep[level + 1], level, NN)
        sweep_copies[level] = send(
            sweep_out.at[level], sweep_in.at[level], sweep_sem, level, sibling(level))
        sweep[level] = own(sweep[level + 1], level, NN)

    def sweep_take(level):
        sweep_copies[level].wait_recv()
        sweep[level] = sweep[level] + sweep_in[level]
        if level > 0:
            sweep_send(level - 1)

    def gather(level, target, sems):
        target[my_rows] = sweep[level]
        return [send(sweep.at[level], target.at[my_rows], sems, k, at_x(k)) for k in range(1, n_sub)]

    loads[2].wait()
    loads[3].wait()
    split_level(2)
    sweep_send(levels - 1)
    for position, level in ((4, 0), (5, 1)):
        loads[position].wait()
        split_level(level)
    loads[6].wait()
    inverse_high[...], inverse_low[...] = halves(inverse[...])
    interp_t[...] = interp_value.T
    live = lax.broadcasted_iota(jnp.int32, (chunk, width), 1) < count_ref[0]

    up_copies = {}
    up_own = {}

    def up_send(level, j):
        rows = pl.ds(j * chunk, chunk)
        if level == 0:
            source, target = up.at[0, rows], up_wide_in.at[rows]
        else:
            up_out[level, rows] = up[level, rows].astype(BF16)
            source, target = up_out.at[level, rows], up_in.at[level, rows]
        up_copies[level, j] = send(source, target, up_sem, level * CHUNKS + j, sibling(level))
        up_own[j] = own(up[level, rows], level, NT)

    def up_start(j):
        rows = pl.ds(j * chunk, chunk)
        total = leaf[0, rows]
        for k in leaf_order[:-1][::-1]:
            leaf_copies[j, k].wait_recv()
            total = total + leaf_in[k, rows]
        up[0, rows] = jnp.where(live, total, 0.0)
        up_send(0, j)

    def up_step(level, j):
        rows = pl.ds(j * chunk, chunk)
        up_copies[level, j].wait_recv()
        arrived = up_in[level, rows] if level else up_wide_in[rows]
        up[level + 1, rows] = up_own[j] + cross(arrived, level, NT)
        if level + 1 < levels:
            up_send(level + 1, j)
        else:
            down_send(up[levels, rows], level, j)

    down_copies = {}
    down_own = {}

    def down_send(value, level, j):
        rows = pl.ds(j * chunk, chunk)
        if level == 0:
            down_wide_out[rows] = cross(value, level, NN)
            source, target = down_wide_out.at[rows], down_wide_in.at[rows]
        else:
            down_out[level, rows] = cross(value, level, NN).astype(BF16)
            source, target = down_out.at[level, rows], down_in.at[level, rows]
        down_copies[level, j] = send(source, target, down_sem, level * CHUNKS + j, sibling(level))
        down_own[j] = own(value, level, NN)

    def down_value(level, j):
        rows = pl.ds(j * chunk, chunk)
        down_copies[level, j].wait_recv()
        arrived = down_in[level, rows].astype(F32) if level else down_wide_in[rows]
        return down_own[j] + arrived

    def down_step(level, j):
        down_send(down_value(level, j), level - 1, j)

    def parts(step, level, part):
        for j in range(part * CHUNKS // 2, (part + 1) * CHUNKS // 2):
            step(level, j)

    for j in range(CHUNKS):
        up_start(j)
    sweep_take(2)
    step_copies = gather(2, step_map, step_sem)
    parts(up_step, 0, 0)
    parts(up_step, 0, 1)
    for copy in step_copies:
        copy.wait_recv()
    step_high, step_low = halves(step_map[...])

    for j in range(CHUNKS):
        rows = pl.ds(j * chunk, chunk)
        up_step(1, j)
        root_part[rows] = dot_split(up[levels - 1, rows], step_high, step_low, NT)

    def piece_of(k):
        return pl.ds(pl.multiple_of(((place + k) % n_plane) * piece, piece), piece)

    plane_copies = [
        send(root_part.at[piece_of(k)], root_plane.at[k], plane_sem, k, at_place(k)) for k in range(1, n_plane)]
    sweep_take(1)
    parts(up_step, 2, 0)
    total = root_part[piece_of(0)]
    for k, copy in enumerate(plane_copies, 1):
        copy.wait_recv()
        total = total + root_plane[k]
    root_mine[...] = total
    z_copies = [send(root_mine, root_z.at[k], z_sem, k, at_z(k)) for k in range(1, n_z)]
    parts(up_step, 2, 1)
    sweep_take(0)
    map_copies = gather(0, root_map, map_sem)
    parts(down_step, 2, 0)
    for k, copy in enumerate(z_copies, 1):
        copy.wait_recv()
        total = total + root_z[k]
    padded = jnp.concatenate([total, jnp.zeros_like(total)], axis=0)
    solved = dot_split(padded, inverse_high[...], inverse_low[...], NT)[:piece]
    root_piece[...] = solved
    root_all[piece_of(0)] = solved
    spread_copies = [
        send(root_piece, root_all.at[piece_of(0)], spread_sem, k, at_place(k)) for k in range(1, n_plane)]
    parts(down_step, 2, 1)
    parts(down_step, 1, 0)
    parts(down_step, 1, 1)
    for copy in map_copies:
        copy.wait_recv()
    map_high, map_low = halves(root_map[...])
    for copy in spread_copies:
        copy.wait_recv()
    root_term = dot_split(root_all[...], map_high, map_low, NN)

    back_copies = {}
    for j in range(CHUNKS):
        value = down_value(0, j) - root_term[j * chunk:(j + 1) * chunk]
        spot = pl.ds(pl.multiple_of(x * slice_cols + j * chunk, chunk), chunk)
        back[spot] = jnp.where(live, value, 0.0).astype(BF16)
        for k in leaf_order[:-1]:
            back_copies[j, k] = send(back.at[spot], back.at[spot], back_sem, j * n_sub + k, at_x(k))

    out_copies = []
    for k in (0, *leaf_order[:-1][::-1]):
        columns = pl.ds(pl.multiple_of(((x + n_sub - k) % n_sub) * slice_cols, slice_cols), slice_cols)
        if k:
            for j in range(CHUNKS):
                back_copies[j, k].wait_recv()
        out[:, columns] = rhs[:, columns].astype(F32) - dot(interp_t[...], back[columns], NT)
        copy = pltpu.make_async_copy(out.at[:, columns], out_hbm.at[:, columns], out_sem.at[k])
        copy.start()
        out_copies.append(copy)

    for copy in started:
        copy.wait_send()
    for copy in out_copies:
        copy.wait()


def local(n_plane, n_z, n_sub, rhs_points, interp, skel_count, butterfly, project, root_inverse):
    points, columns = rhs_points.shape
    width = interp.shape[0]
    levels = butterfly.shape[0]
    slice_cols = columns // n_sub
    piece = slice_cols // n_plane
    root_rows = width // n_sub
    vmem = pltpu.VMEM
    pair = lambda count: pltpu.SemaphoreType.DMA((2, count))
    scratch = [
        vmem((points, columns), BF16), vmem((width, points), BF16), vmem((points, width), BF16),
        vmem(butterfly.shape, F32), vmem((width, width), F32),
        vmem(butterfly.shape, BF16), vmem(butterfly.shape, BF16),
        vmem((width, width), BF16), vmem((width, width), BF16),
        vmem((n_sub, slice_cols, width), F32), vmem((n_sub, slice_cols, width), F32),
        vmem((levels + 1, slice_cols, width), F32), vmem((slice_cols, width), F32),
        vmem((levels, slice_cols, width), BF16), vmem((levels, slice_cols, width), BF16),
        vmem((slice_cols, width), F32), vmem((slice_cols, width), F32),
        vmem((levels, slice_cols, width), BF16), vmem((levels, slice_cols, width), BF16),
        vmem((levels + 1, root_rows, width), F32), vmem((levels, root_rows, width), F32),
        vmem((levels, root_rows, width), F32), vmem((width, width), F32), vmem((width, width), F32),
        vmem((slice_cols, width), F32), vmem((n_plane, piece, width), F32),
        vmem((piece, width), F32), vmem((n_z, piece, width), F32), vmem((piece, width), F32),
        vmem((slice_cols, width), F32),
        vmem((columns, width), BF16), vmem((points, columns), F32),
        pltpu.SemaphoreType.DMA((7,)), pltpu.SemaphoreType.DMA((n_sub,)),
        pair(CHUNKS * n_sub), pair(levels * CHUNKS), pair(levels * CHUNKS), pair(levels), pair(n_sub), pair(n_sub),
        pair(n_plane), pair(n_z), pair(n_plane), pair(CHUNKS * n_sub),
    ]
    hbm = pl.BlockSpec(memory_space=pl.ANY)
    return pl.pallas_call(
        functools.partial(kernel, n_plane, n_z, n_sub, levels),
        out_shape=jax.ShapeDtypeStruct((points, columns), F32),
        in_specs=[hbm, hbm, pl.BlockSpec(memory_space=pltpu.SMEM), hbm, hbm, hbm],
        out_specs=pl.BlockSpec(memory_space=pl.ANY),
        scratch_shapes=scratch,
        compiler_params=pltpu.CompilerParams(
            collective_id=0, has_side_effects=True, vmem_limit_bytes=62 * 2**20),
    )(rhs_points, interp, skel_count, butterfly, project, root_inverse)


def solution(mesh):
    n_box, n_sub = mesh.shape["box"], mesh.shape["sub"]
    n_z = 8
    in_specs = (
        P(("box", "sub"), None),
        P(("box", "sub"), None),
        P("box"),
        P(None, "box", None),
        P("box", None),
        P(),
    )
    out_specs = P(("box", "sub"), None)
    return jax.shard_map(
        functools.partial(local, n_box // n_z, n_z, n_sub),
        mesh=mesh, in_specs=in_specs, out_specs=out_specs, check_vma=False)
```

```python
import functools

import jax
import jax.numpy as jnp
from jax import lax
from jax.experimental import pallas as pl
from jax.experimental.pallas import tpu as pltpu
from jax.sharding import PartitionSpec as P

F32 = jnp.float32
BF16 = jnp.bfloat16
MESH = pl.DeviceIdType.MESH
CHUNKS = 2
NN = (((1,), (0,)), ((), ()))
NT = (((1,), (1,)), ((), ()))


def halves(value):
    high = value.astype(BF16)
    return high, (value - high.astype(F32)).astype(BF16)


def dot(left, right, dims):
    return lax.dot_general(left, right, dims, preferred_element_type=F32)


def dot_split(value, high, low, dims):
    rows = value.shape[0]
    if value.dtype == BF16:
        return dot(value, high, dims) + dot(value, low, dims)
    value_high, value_low = halves(value)
    both = dot(jnp.concatenate([value_high, value_low], axis=0), high, dims)
    return both[:rows] + (both[rows:] + dot(value_high, low, dims))


def kernel(
    n_plane, n_z, n_sub, levels,
    rhs_hbm, interp_hbm, count_ref, butterfly_hbm, project_hbm, inverse_hbm, out_hbm,
    rhs, interp, interp_t, butterfly, inverse,
    weight_high, weight_low, inverse_high, inverse_low,
    leaf, leaf_in, relay_in, relay_out, up, up_wide_in, up_out, up_in, down_wide_out, down_wide_in, down_out, down_in,
    sweep, sweep_out, sweep_in, step_map, root_map,
    root_part, root_plane, root_mine, root_z, root_piece, root_all,
    back, out,
    load_sem, out_sem, leaf_sem, relay_sem, up_sem, down_sem, sweep_sem, step_sem, map_sem, plane_sem, z_sem, spread_sem, back_sem,
):
    width = interp.shape[0]
    slice_cols = leaf.shape[1]
    chunk = slice_cols // CHUNKS
    root_rows = width // n_sub
    piece = slice_cols // n_plane

    box = lax.axis_index("box")
    x = lax.axis_index("sub")
    place = box % n_plane
    z = box // n_plane

    def at_x(k):
        return (box, (x + k) % n_sub)

    def at_place(k):
        return (z * n_plane + (place + k) % n_plane, x)

    def at_z(k):
        return (((z + k) % n_z) * n_plane + place, x)

    def sibling(level):
        bit = 2 ** level
        return (box + (1 - 2 * ((z // bit) % 2)) * bit * n_plane, x)

    def send(source, target, sems, index, device):
        copy = pltpu.make_async_remote_copy(
            src_ref=source, dst_ref=target, send_sem=sems.at[0, index], recv_sem=sems.at[1, index],
            device_id=device, device_id_type=MESH,
        )
        copy.start()
        started.append(copy)
        return copy

    started = []

    my_rows = pl.ds(pl.multiple_of(x * root_rows, root_rows), root_rows)
    loads = []
    for source, target in (
        (interp_hbm, interp), (rhs_hbm, rhs), (project_hbm.at[my_rows], sweep.at[levels]),
        (butterfly_hbm.at[2], butterfly.at[2]), (butterfly_hbm.at[0], butterfly.at[0]),
        (butterfly_hbm.at[1], butterfly.at[1]), (inverse_hbm, inverse),
    ):
        load = pltpu.make_async_copy(source, target, load_sem.at[len(loads)])
        load.start()
        loads.append(load)

    barrier = pltpu.get_barrier_semaphore()
    peers = ([at_x(k) for k in range(1, n_sub)] + [at_place(k) for k in range(1, n_plane)]
             + [at_z(k) for k in range(1, n_z)])
    for peer in peers:
        pl.semaphore_signal(barrier, inc=1, device_id=peer, device_id_type=MESH)

    ahead, behind, across = 1, n_sub - 1, n_sub // 2
    leaf_copies = {}

    def rows_of(j):
        return pl.ds(j * chunk, chunk)

    def leaf_send(j, k, source):
        leaf_copies[j, k] = send(source, leaf_in.at[k, rows_of(j)], leaf_sem, j * n_sub + k, at_x(k))

    def leaf_term(k):
        columns = pl.ds(pl.multiple_of(((x + k) % n_sub) * slice_cols, slice_cols), slice_cols)
        leaf[k] = dot(rhs[:, columns].T, interp_value, NT)

    loads[0].wait()
    loads[1].wait()
    pl.semaphore_wait(barrier, len(peers))
    interp_value = interp[...]
    leaf_term(across)
    relay_copies = [
        send(leaf.at[across, rows_of(j)], relay_in.at[j], relay_sem, j, at_x(k)) for j, k in enumerate((ahead, behind))]
    leaf_term(behind)
    leaf_send(0, behind, leaf.at[behind, rows_of(0)])
    leaf_term(ahead)
    leaf_send(1, ahead, leaf.at[ahead, rows_of(1)])
    leaf_term(0)

    def split_level(level):
        high, low = halves(butterfly[level])
        weight_high[level] = high
        weight_low[level] = low

    def own(value, level, dims):
        return dot_split(value, weight_high[level, :, :width], weight_low[level, :, :width], dims)

    def cross(value, level, dims):
        return dot_split(value, weight_high[level, :, width:], weight_low[level, :, width:], dims)

    sweep_copies = {}

    def sweep_send(level):
        sweep_out[level] = cross(sweep[level + 1], level, NN)
        sweep_copies[level] = send(
            sweep_out.at[level], sweep_in.at[level], sweep_sem, level, sibling(level))
        sweep[level] = own(sweep[level + 1], level, NN)

    def sweep_take(level):
        sweep_copies[level].wait_recv()
        sweep[level] = sweep[level] + sweep_in[level]
        if level > 0:
            sweep_send(level - 1)

    def gather(level, target, sems):
        target[my_rows] = sweep[level]
        return [send(sweep.at[level], target.at[my_rows], sems, k, at_x(k)) for k in range(1, n_sub)]

    loads[2].wait()
    loads[3].wait()
    split_level(2)
    sweep_send(levels - 1)
    for j, k in enumerate((ahead, behind)):
        relay_copies[j].wait_recv()
        relay_out[j] = leaf[k, rows_of(j)] + relay_in[j]
        leaf_send(j, k, relay_out.at[j])
    for position, level in ((4, 0), (5, 1)):
        loads[position].wait()
        split_level(level)
    loads[6].wait()
    inverse_high[...], inverse_low[...] = halves(inverse[...])
    interp_t[...] = interp_value.T
    live = lax.broadcasted_iota(jnp.int32, (chunk, width), 1) < count_ref[0]

    up_copies = {}
    up_own = {}

    def up_send(level, j):
        rows = pl.ds(j * chunk, chunk)
        if level == 0:
            source, target = up.at[0, rows], up_wide_in.at[rows]
        else:
            up_out[level, rows] = up[level, rows].astype(BF16)
            source, target = up_out.at[level, rows], up_in.at[level, rows]
        up_copies[level, j] = send(source, target, up_sem, level * CHUNKS + j, sibling(level))
        up_own[j] = own(up[level, rows], level, NT)

    def up_start(j):
        rows = pl.ds(j * chunk, chunk)
        total = leaf[0, rows]
        for k in ((behind, ahead), (ahead, behind))[j]:
            leaf_copies[j, k].wait_recv()
            total = total + leaf_in[k, rows]
        up[0, rows] = jnp.where(live, total, 0.0)
        up_send(0, j)

    def up_step(level, j):
        rows = pl.ds(j * chunk, chunk)
        up_copies[level, j].wait_recv()
        arrived = up_in[level, rows] if level else up_wide_in[rows]
        up[level + 1, rows] = up_own[j] + cross(arrived, level, NT)
        if level + 1 < levels:
            up_send(level + 1, j)
        else:
            down_send(up[levels, rows], level, j)

    down_copies = {}
    down_own = {}

    def down_send(value, level, j):
        rows = pl.ds(j * chunk, chunk)
        if level == 0:
            down_wide_out[rows] = cross(value, level, NN)
            source, target = down_wide_out.at[rows], down_wide_in.at[rows]
        else:
            down_out[level, rows] = cross(value, level, NN).astype(BF16)
            source, target = down_out.at[level, rows], down_in.at[level, rows]
        down_copies[level, j] = send(source, target, down_sem, level * CHUNKS + j, sibling(level))
        down_own[j] = own(value, level, NN)

    def down_value(level, j):
        rows = pl.ds(j * chunk, chunk)
        down_copies[level, j].wait_recv()
        arrived = down_in[level, rows].astype(F32) if level else down_wide_in[rows]
        return down_own[j] + arrived

    def down_step(level, j):
        down_send(down_value(level, j), level - 1, j)

    def parts(step, level, part):
        for j in range(part * CHUNKS // 2, (part + 1) * CHUNKS // 2):
            step(level, j)

    for j in range(CHUNKS):
        up_start(j)
    sweep_take(2)
    step_copies = gather(2, step_map, step_sem)
    parts(up_step, 0, 0)
    parts(up_step, 0, 1)
    for copy in step_copies:
        copy.wait_recv()
    step_high, step_low = halves(step_map[...])

    for j in range(CHUNKS):
        rows = pl.ds(j * chunk, chunk)
        up_step(1, j)
        root_part[rows] = dot_split(up[levels - 1, rows], step_high, step_low, NT)

    def piece_of(k):
        return pl.ds(pl.multiple_of(((place + k) % n_plane) * piece, piece), piece)

    plane_copies = [
        send(root_part.at[piece_of(k)], root_plane.at[k], plane_sem, k, at_place(k)) for k in range(1, n_plane)]
    sweep_take(1)
    parts(up_step, 2, 0)
    total = root_part[piece_of(0)]
    for k, copy in enumerate(plane_copies, 1):
        copy.wait_recv()
        total = total + root_plane[k]
    root_mine[...] = total
    z_copies = [send(root_mine, root_z.at[k], z_sem, k, at_z(k)) for k in range(1, n_z)]
    parts(up_step, 2, 1)
    sweep_take(0)
    map_copies = gather(0, root_map, map_sem)
    parts(down_step, 2, 0)
    for k, copy in enumerate(z_copies, 1):
        copy.wait_recv()
        total = total + root_z[k]
    padded = jnp.concatenate([total, jnp.zeros_like(total)], axis=0)
    solved = dot_split(padded, inverse_high[...], inverse_low[...], NT)[:piece]
    root_piece[...] = solved
    root_all[piece_of(0)] = solved
    spread_copies = [
        send(root_piece, root_all.at[piece_of(0)], spread_sem, k, at_place(k)) for k in range(1, n_plane)]
    parts(down_step, 2, 1)
    parts(down_step, 1, 0)
    parts(down_step, 1, 1)
    for copy in map_copies:
        copy.wait_recv()
    map_high, map_low = halves(root_map[...])
    for copy in spread_copies:
        copy.wait_recv()
    root_term = dot_split(root_all[...], map_high, map_low, NN)

    back_copies = {}
    for j in range(CHUNKS):
        value = down_value(0, j) - root_term[j * chunk:(j + 1) * chunk]
        spot = pl.ds(pl.multiple_of(x * slice_cols + j * chunk, chunk), chunk)
        back[spot] = jnp.where(live, value, 0.0).astype(BF16)
        for k in (ahead, behind):
            back_copies[j, k] = send(back.at[spot], back.at[spot], back_sem, j * n_sub + k, at_x(k))

    def place_of(k):
        return ((x + n_sub - k) % n_sub) * slice_cols

    out_copies = []

    def update(k):
        columns = pl.ds(pl.multiple_of(place_of(k), slice_cols), slice_cols)
        out[:, columns] = rhs[:, columns].astype(F32) - dot(interp_t[...], back[columns], NT)
        copy = pltpu.make_async_copy(out.at[:, columns], out_hbm.at[:, columns], out_sem.at[k])
        copy.start()
        out_copies.append(copy)

    passed = []
    update(0)
    for j, k in enumerate((ahead, behind)):
        back_copies[j, k].wait_recv()
        spot = pl.ds(pl.multiple_of(place_of(k) + j * chunk, chunk), chunk)
        passed.append(send(back.at[spot], back.at[spot], back_sem, j * n_sub + across, at_x(k)))
    for j, k in ((1, ahead), (0, behind)):
        back_copies[j, k].wait_recv()
        update(k)
    for copy in passed:
        copy.wait_recv()
    update(across)

    for copy in started:
        copy.wait_send()
    for copy in out_copies:
        copy.wait()


def local(n_plane, n_z, n_sub, rhs_points, interp, skel_count, butterfly, project, root_inverse):
    points, columns = rhs_points.shape
    width = interp.shape[0]
    levels = butterfly.shape[0]
    slice_cols = columns // n_sub
    piece = slice_cols // n_plane
    root_rows = width // n_sub
    vmem = pltpu.VMEM
    pair = lambda count: pltpu.SemaphoreType.DMA((2, count))
    scratch = [
        vmem((points, columns), BF16), vmem((width, points), BF16), vmem((points, width), BF16),
        vmem(butterfly.shape, F32), vmem((width, width), F32),
        vmem(butterfly.shape, BF16), vmem(butterfly.shape, BF16),
        vmem((width, width), BF16), vmem((width, width), BF16),
        vmem((n_sub, slice_cols, width), F32), vmem((n_sub, slice_cols, width), F32),
        vmem((CHUNKS, slice_cols // CHUNKS, width), F32), vmem((CHUNKS, slice_cols // CHUNKS, width), F32),
        vmem((levels + 1, slice_cols, width), F32), vmem((slice_cols, width), F32),
        vmem((levels, slice_cols, width), BF16), vmem((levels, slice_cols, width), BF16),
        vmem((slice_cols, width), F32), vmem((slice_cols, width), F32),
        vmem((levels, slice_cols, width), BF16), vmem((levels, slice_cols, width), BF16),
        vmem((levels + 1, root_rows, width), F32), vmem((levels, root_rows, width), F32),
        vmem((levels, root_rows, width), F32), vmem((width, width), F32), vmem((width, width), F32),
        vmem((slice_cols, width), F32), vmem((n_plane, piece, width), F32),
        vmem((piece, width), F32), vmem((n_z, piece, width), F32), vmem((piece, width), F32),
        vmem((slice_cols, width), F32),
        vmem((columns, width), BF16), vmem((points, columns), F32),
        pltpu.SemaphoreType.DMA((7,)), pltpu.SemaphoreType.DMA((n_sub,)),
        pair(CHUNKS * n_sub), pair(CHUNKS), pair(levels * CHUNKS), pair(levels * CHUNKS), pair(levels), pair(n_sub), pair(n_sub),
        pair(n_plane), pair(n_z), pair(n_plane), pair(CHUNKS * n_sub),
    ]
    hbm = pl.BlockSpec(memory_space=pl.ANY)
    return pl.pallas_call(
        functools.partial(kernel, n_plane, n_z, n_sub, levels),
        out_shape=jax.ShapeDtypeStruct((points, columns), F32),
        in_specs=[hbm, hbm, pl.BlockSpec(memory_space=pltpu.SMEM), hbm, hbm, hbm],
        out_specs=pl.BlockSpec(memory_space=pl.ANY),
        scratch_shapes=scratch,
        compiler_params=pltpu.CompilerParams(
            collective_id=0, has_side_effects=True, vmem_limit_bytes=62 * 2**20),
    )(rhs_points, interp, skel_count, butterfly, project, root_inverse)


def solution(mesh):
    n_box, n_sub = mesh.shape["box"], mesh.shape["sub"]
    n_z = 8
    in_specs = (
        P(("box", "sub"), None),
        P(("box", "sub"), None),
        P("box"),
        P(None, "box", None),
        P("box", None),
        P(),
    )
    out_specs = P(("box", "sub"), None)
    return jax.shard_map(
        functools.partial(local, n_box // n_z, n_z, n_sub),
        mesh=mesh, in_specs=in_specs, out_specs=out_specs, check_vma=False)
```

```python
import functools

import jax
import jax.numpy as jnp
from jax import lax
from jax.experimental import pallas as pl
from jax.experimental.pallas import tpu as pltpu
from jax.sharding import PartitionSpec as P

F32 = jnp.float32
BF16 = jnp.bfloat16
MESH = pl.DeviceIdType.MESH
CHUNKS = 2
NN = (((1,), (0,)), ((), ()))
NT = (((1,), (1,)), ((), ()))


def halves(value):
    high = value.astype(BF16)
    return high, (value - high.astype(F32)).astype(BF16)


def dot(left, right, dims):
    return lax.dot_general(left, right, dims, preferred_element_type=F32)


def dot_split(value, high, low, dims):
    rows = value.shape[0]
    if value.dtype == BF16:
        return dot(value, high, dims) + dot(value, low, dims)
    value_high, value_low = halves(value)
    both = dot(jnp.concatenate([value_high, value_low], axis=0), high, dims)
    return both[:rows] + (both[rows:] + dot(value_high, low, dims))


def kernel(
    n_plane, n_z, n_sub, levels,
    rhs_hbm, interp_hbm, count_ref, butterfly_hbm, project_hbm, inverse_hbm, out_hbm,
    rhs, interp, interp_t, butterfly, inverse,
    weight_high, weight_low, turned_high, turned_low, inverse_high, inverse_low,
    leaf, leaf_in, up, up_wide_in, up_out, up_in, down_wide_out, down_wide_in, down_out, down_in,
    sweep, sweep_out, sweep_in, step_map, root_map,
    root_part, root_plane, root_mine, root_z, root_piece, root_all,
    back, out,
    load_sem, out_sem, leaf_sem, up_sem, down_sem, sweep_sem, step_sem, map_sem, plane_sem, z_sem, spread_sem, back_sem,
):
    width = interp.shape[0]
    slice_cols = leaf.shape[1]
    chunk = slice_cols // CHUNKS
    root_rows = width // n_sub
    piece = slice_cols // n_plane

    box = lax.axis_index("box")
    x = lax.axis_index("sub")
    place = box % n_plane
    z = box // n_plane

    def at_x(k):
        return (box, (x + k) % n_sub)

    def at_place(k):
        return (z * n_plane + (place + k) % n_plane, x)

    def at_z(k):
        return (((z + k) % n_z) * n_plane + place, x)

    def sibling(level):
        bit = 2 ** level
        return (box + (1 - 2 * ((z // bit) % 2)) * bit * n_plane, x)

    def send(source, target, sems, index, device):
        copy = pltpu.make_async_remote_copy(
            src_ref=source, dst_ref=target, send_sem=sems.at[0, index], recv_sem=sems.at[1, index],
            device_id=device, device_id_type=MESH,
        )
        copy.start()
        started.append(copy)
        return copy

    started = []

    barrier = pltpu.get_barrier_semaphore()
    peers = ([at_x(k) for k in range(1, n_sub)] + [at_place(k) for k in range(1, n_plane)]
             + [at_z(k) for k in range(1, n_z)])
    for peer in peers:
        pl.semaphore_signal(barrier, inc=1, device_id=peer, device_id_type=MESH)

    my_rows = pl.ds(pl.multiple_of(x * root_rows, root_rows), root_rows)
    loads = []
    for source, target in (
        (interp_hbm, interp), (rhs_hbm, rhs), (project_hbm.at[my_rows], sweep.at[levels]),
        (butterfly_hbm.at[2], butterfly.at[2]), (butterfly_hbm.at[0], butterfly.at[0]),
        (butterfly_hbm.at[1], butterfly.at[1]), (inverse_hbm, inverse),
    ):
        load = pltpu.make_async_copy(source, target, load_sem.at[len(loads)])
        load.start()
        loads.append(load)

    leaf_order = sorted(range(n_sub), key=lambda k: (k == 0, -min(k, n_sub - k)))
    leaf_copies = {}

    def leaf_send(j, k):
        rows = pl.ds(j * chunk, chunk)
        leaf_copies[j, k] = send(leaf.at[k, rows], leaf_in.at[k, rows], leaf_sem, j * n_sub + k, at_x(k))

    loads[0].wait()
    loads[1].wait()
    pl.semaphore_wait(barrier, len(peers))
    interp_value = interp[...]
    for k in leaf_order:
        columns = pl.ds(pl.multiple_of(((x + k) % n_sub) * slice_cols, slice_cols), slice_cols)
        leaf[k] = dot(rhs[:, columns].T, interp_value, NT)
        if k:
            leaf_send(0, k)
    for j in range(1, CHUNKS):
        for k in leaf_order[:-1]:
            leaf_send(j, k)

    def split_level(level):
        high, low = halves(butterfly[level])
        weight_high[level] = high
        weight_low[level] = low

    def turn_level(level):
        turned_high[level] = weight_high[level].T
        turned_low[level] = weight_low[level].T

    def own(value, level):
        return dot_split(value, weight_high[level, :, :width], weight_low[level, :, :width], NN)

    def cross(value, level):
        return dot_split(value, weight_high[level, :, width:], weight_low[level, :, width:], NN)

    def own_turned(value, level):
        return dot_split(value, turned_high[level, :width], turned_low[level, :width], NN)

    def cross_turned(value, level):
        return dot_split(value, turned_high[level, width:], turned_low[level, width:], NN)

    sweep_copies = {}

    def sweep_send(level):
        sweep_out[level] = cross(sweep[level + 1], level)
        sweep_copies[level] = send(
            sweep_out.at[level], sweep_in.at[level], sweep_sem, level, sibling(level))
        sweep[level] = own(sweep[level + 1], level)

    def sweep_take(level):
        sweep_copies[level].wait_recv()
        sweep[level] = sweep[level] + sweep_in[level]
        if level > 0:
            sweep_send(level - 1)

    def gather(level, target, sems):
        target[my_rows] = sweep[level]
        return [send(sweep.at[level], target.at[my_rows], sems, k, at_x(k)) for k in range(1, n_sub)]

    loads[2].wait()
    loads[3].wait()
    split_level(2)
    sweep_send(levels - 1)
    for position, level in ((4, 0), (5, 1)):
        loads[position].wait()
        split_level(level)
        turn_level(level)
    turn_level(levels - 1)
    loads[6].wait()
    inverse_high[...], inverse_low[...] = halves(inverse[...].T)
    interp_t[...] = interp_value.T
    live = lax.broadcasted_iota(jnp.int32, (chunk, width), 1) < count_ref[0]

    up_copies = {}
    up_own = {}

    def up_send(level, j):
        rows = pl.ds(j * chunk, chunk)
        if level == 0:
            source, target = up.at[0, rows], up_wide_in.at[rows]
        else:
            up_out[level, rows] = up[level, rows].astype(BF16)
            source, target = up_out.at[level, rows], up_in.at[level, rows]
        up_copies[level, j] = send(source, target, up_sem, level * CHUNKS + j, sibling(level))
        up_own[j] = own_turned(up[level, rows], level)

    def up_start(j):
        rows = pl.ds(j * chunk, chunk)
        total = leaf[0, rows]
        for k in leaf_order[:-1][::-1]:
            leaf_copies[j, k].wait_recv()
            total = total + leaf_in[k, rows]
        up[0, rows] = jnp.where(live, total, 0.0)
        up_send(0, j)

    def up_step(level, j):
        rows = pl.ds(j * chunk, chunk)
        up_copies[level, j].wait_recv()
        arrived = up_in[level, rows] if level else up_wide_in[rows]
        up[level + 1, rows] = up_own[j] + cross_turned(arrived, level)
        if level + 1 < levels:
            up_send(level + 1, j)
        else:
            down_send(up[levels, rows], level, j)

    down_copies = {}
    down_own = {}

    def down_send(value, level, j):
        rows = pl.ds(j * chunk, chunk)
        if level == 0:
            down_wide_out[rows] = cross(value, level)
            source, target = down_wide_out.at[rows], down_wide_in.at[rows]
        else:
            down_out[level, rows] = cross(value, level).astype(BF16)
            source, target = down_out.at[level, rows], down_in.at[level, rows]
        down_copies[level, j] = send(source, target, down_sem, level * CHUNKS + j, sibling(level))
        down_own[j] = own(value, level)

    def down_value(level, j):
        rows = pl.ds(j * chunk, chunk)
        down_copies[level, j].wait_recv()
        arrived = down_in[level, rows].astype(F32) if level else down_wide_in[rows]
        return down_own[j] + arrived

    def down_step(level, j):
        down_send(down_value(level, j), level - 1, j)

    def parts(step, level, part):
        for j in range(part * CHUNKS // 2, (part + 1) * CHUNKS // 2):
            step(level, j)

    for j in range(CHUNKS):
        up_start(j)
    sweep_take(2)
    step_copies = gather(2, step_map, step_sem)
    parts(up_step, 0, 0)
    parts(up_step, 0, 1)
    for copy in step_copies:
        copy.wait_recv()
    step_high, step_low = halves(step_map[...].T)

    for j in range(CHUNKS):
        rows = pl.ds(j * chunk, chunk)
        up_step(1, j)
        root_part[rows] = dot_split(up[levels - 1, rows], step_high, step_low, NN)

    def piece_of(k):
        return pl.ds(pl.multiple_of(((place + k) % n_plane) * piece, piece), piece)

    plane_copies = [
        send(root_part.at[piece_of(k)], root_plane.at[k], plane_sem, k, at_place(k)) for k in range(1, n_plane)]
    sweep_take(1)
    parts(up_step, 2, 0)
    total = root_part[piece_of(0)]
    for k, copy in enumerate(plane_copies, 1):
        copy.wait_recv()
        total = total + root_plane[k]
    root_mine[...] = total
    z_copies = [send(root_mine, root_z.at[k], z_sem, k, at_z(k)) for k in range(1, n_z)]
    parts(up_step, 2, 1)
    sweep_take(0)
    map_copies = gather(0, root_map, map_sem)
    parts(down_step, 2, 0)
    for k, copy in enumerate(z_copies, 1):
        copy.wait_recv()
        total = total + root_z[k]
    padded = jnp.concatenate([total, jnp.zeros_like(total)], axis=0)
    solved = dot_split(padded, inverse_high[...], inverse_low[...], NN)[:piece]
    root_piece[...] = solved
    root_all[piece_of(0)] = solved
    spread_copies = [
        send(root_piece, root_all.at[piece_of(0)], spread_sem, k, at_place(k)) for k in range(1, n_plane)]
    parts(down_step, 2, 1)
    parts(down_step, 1, 0)
    parts(down_step, 1, 1)
    for copy in map_copies:
        copy.wait_recv()
    map_high, map_low = halves(root_map[...])
    for copy in spread_copies:
        copy.wait_recv()
    root_term = dot_split(root_all[...], map_high, map_low, NN)

    back_copies = {}
    for j in range(CHUNKS):
        value = down_value(0, j) - root_term[j * chunk:(j + 1) * chunk]
        spot = pl.ds(pl.multiple_of(x * slice_cols + j * chunk, chunk), chunk)
        back[spot] = jnp.where(live, value, 0.0).astype(BF16)
        for k in leaf_order[:-1]:
            back_copies[j, k] = send(back.at[spot], back.at[spot], back_sem, j * n_sub + k, at_x(k))

    out_copies = []
    for k in (0, *leaf_order[:-1][::-1]):
        columns = pl.ds(pl.multiple_of(((x + n_sub - k) % n_sub) * slice_cols, slice_cols), slice_cols)
        if k:
            for j in range(CHUNKS):
                back_copies[j, k].wait_recv()
        out[:, columns] = rhs[:, columns].astype(F32) - dot(interp_t[...], back[columns], NT)
        copy = pltpu.make_async_copy(out.at[:, columns], out_hbm.at[:, columns], out_sem.at[k])
        copy.start()
        out_copies.append(copy)

    for copy in started:
        copy.wait_send()
    for copy in out_copies:
        copy.wait()


def local(n_plane, n_z, n_sub, rhs_points, interp, skel_count, butterfly, project, root_inverse):
    points, columns = rhs_points.shape
    width = interp.shape[0]
    levels = butterfly.shape[0]
    slice_cols = columns // n_sub
    piece = slice_cols // n_plane
    root_rows = width // n_sub
    vmem = pltpu.VMEM
    pair = lambda count: pltpu.SemaphoreType.DMA((2, count))
    scratch = [
        vmem((points, columns), BF16), vmem((width, points), BF16), vmem((points, width), BF16),
        vmem(butterfly.shape, F32), vmem((width, width), F32),
        vmem(butterfly.shape, BF16), vmem(butterfly.shape, BF16),
        vmem((levels, 2 * width, width), BF16), vmem((levels, 2 * width, width), BF16),
        vmem((width, width), BF16), vmem((width, width), BF16),
        vmem((n_sub, slice_cols, width), F32), vmem((n_sub, slice_cols, width), F32),
        vmem((levels + 1, slice_cols, width), F32), vmem((slice_cols, width), F32),
        vmem((levels, slice_cols, width), BF16), vmem((levels, slice_cols, width), BF16),
        vmem((slice_cols, width), F32), vmem((slice_cols, width), F32),
        vmem((levels, slice_cols, width), BF16), vmem((levels, slice_cols, width), BF16),
        vmem((levels + 1, root_rows, width), F32), vmem((levels, root_rows, width), F32),
        vmem((levels, root_rows, width), F32), vmem((width, width), F32), vmem((width, width), F32),
        vmem((slice_cols, width), F32), vmem((n_plane, piece, width), F32),
        vmem((piece, width), F32), vmem((n_z, piece, width), F32), vmem((piece, width), F32),
        vmem((slice_cols, width), F32),
        vmem((columns, width), BF16), vmem((points, columns), F32),
        pltpu.SemaphoreType.DMA((7,)), pltpu.SemaphoreType.DMA((n_sub,)),
        pair(CHUNKS * n_sub), pair(levels * CHUNKS), pair(levels * CHUNKS), pair(levels), pair(n_sub), pair(n_sub),
        pair(n_plane), pair(n_z), pair(n_plane), pair(CHUNKS * n_sub),
    ]
    hbm = pl.BlockSpec(memory_space=pl.ANY)
    return pl.pallas_call(
        functools.partial(kernel, n_plane, n_z, n_sub, levels),
        out_shape=jax.ShapeDtypeStruct((points, columns), F32),
        in_specs=[hbm, hbm, pl.BlockSpec(memory_space=pltpu.SMEM), hbm, hbm, hbm],
        out_specs=pl.BlockSpec(memory_space=pl.ANY),
        scratch_shapes=scratch,
        compiler_params=pltpu.CompilerParams(
            collective_id=0, has_side_effects=True, vmem_limit_bytes=62 * 2**20),
    )(rhs_points, interp, skel_count, butterfly, project, root_inverse)


def solution(mesh):
    n_box, n_sub = mesh.shape["box"], mesh.shape["sub"]
    n_z = 8
    in_specs = (
        P(("box", "sub"), None),
        P(("box", "sub"), None),
        P("box"),
        P(None, "box", None),
        P("box", None),
        P(),
    )
    out_specs = P(("box", "sub"), None)
    return jax.shard_map(
        functools.partial(local, n_box // n_z, n_z, n_sub),
        mesh=mesh, in_specs=in_specs, out_specs=out_specs, check_vma=False)
```

```python
import functools

import jax
import jax.numpy as jnp
from jax import lax
from jax.experimental import pallas as pl
from jax.experimental.pallas import tpu as pltpu
from jax.sharding import PartitionSpec as P

F32 = jnp.float32
BF16 = jnp.bfloat16
MESH = pl.DeviceIdType.MESH
CHUNKS = 2
NN = (((1,), (0,)), ((), ()))
NT = (((1,), (1,)), ((), ()))


def halves(value):
    high = value.astype(BF16)
    return high, (value - high.astype(F32)).astype(BF16)


def dot(left, right, dims):
    return lax.dot_general(left, right, dims, preferred_element_type=F32)


def dot_split(value, high, low, dims):
    rows = value.shape[0]
    if value.dtype == BF16:
        return dot(value, high, dims) + dot(value, low, dims)
    value_high, value_low = halves(value)
    both = dot(jnp.concatenate([value_high, value_low], axis=0), high, dims)
    return both[:rows] + (both[rows:] + dot(value_high, low, dims))


def kernel(
    n_plane, n_z, n_sub, levels,
    rhs_hbm, interp_hbm, count_ref, butterfly_hbm, project_hbm, inverse_hbm, out_hbm,
    rhs, interp, interp_t, butterfly, inverse,
    weight_high, weight_low, turned_high, turned_low, inverse_high, inverse_low,
    leaf, leaf_in, up, up_wide_in, up_out, up_in, down_wide_out, down_wide_in, down_out, down_in,
    sweep, sweep_wide_out, sweep_wide_in, sweep_out, sweep_in, step_map, root_map,
    root_part, root_plane, root_mine, root_z, root_piece, root_all,
    back, out,
    load_sem, out_sem, leaf_sem, up_sem, down_sem, sweep_sem, step_sem, map_sem, plane_sem, z_sem, spread_sem, back_sem,
):
    width = interp.shape[0]
    slice_cols = leaf.shape[1]
    chunk = slice_cols // CHUNKS
    root_rows = width // n_sub
    piece = slice_cols // n_plane

    box = lax.axis_index("box")
    x = lax.axis_index("sub")
    place = box % n_plane
    z = box // n_plane

    def at_x(k):
        return (box, (x + k) % n_sub)

    def at_place(k):
        return (z * n_plane + (place + k) % n_plane, x)

    def at_z(k):
        return (((z + k) % n_z) * n_plane + place, x)

    def sibling(level):
        bit = 2 ** level
        return (box + (1 - 2 * ((z // bit) % 2)) * bit * n_plane, x)

    def send(source, target, sems, index, device):
        copy = pltpu.make_async_remote_copy(
            src_ref=source, dst_ref=target, send_sem=sems.at[0, index], recv_sem=sems.at[1, index],
            device_id=device, device_id_type=MESH,
        )
        copy.start()
        started.append(copy)
        return copy

    started = []

    barrier = pltpu.get_barrier_semaphore()
    peers = ([at_x(k) for k in range(1, n_sub)] + [at_place(k) for k in range(1, n_plane)]
             + [at_z(k) for k in range(1, n_z)])
    for peer in peers:
        pl.semaphore_signal(barrier, inc=1, device_id=peer, device_id_type=MESH)

    my_rows = pl.ds(pl.multiple_of(x * root_rows, root_rows), root_rows)
    loads = []
    for source, target in (
        (interp_hbm, interp), (rhs_hbm, rhs), (project_hbm.at[my_rows], sweep.at[levels]),
        (butterfly_hbm.at[2], butterfly.at[2]), (butterfly_hbm.at[0], butterfly.at[0]),
        (butterfly_hbm.at[1], butterfly.at[1]), (inverse_hbm, inverse),
    ):
        load = pltpu.make_async_copy(source, target, load_sem.at[len(loads)])
        load.start()
        loads.append(load)

    leaf_order = sorted(range(n_sub), key=lambda k: (k == 0, -min(k, n_sub - k)))
    leaf_copies = {}

    def leaf_send(j, k):
        rows = pl.ds(j * chunk, chunk)
        leaf_copies[j, k] = send(leaf.at[k, rows], leaf_in.at[k, rows], leaf_sem, j * n_sub + k, at_x(k))

    loads[0].wait()
    loads[1].wait()
    pl.semaphore_wait(barrier, len(peers))
    interp_value = interp[...]
    for k in leaf_order:
        columns = pl.ds(pl.multiple_of(((x + k) % n_sub) * slice_cols, slice_cols), slice_cols)
        leaf[k] = dot(rhs[:, columns].T, interp_value, NT)
        if k:
            leaf_send(0, k)
    for j in range(1, CHUNKS):
        for k in leaf_order[:-1]:
            leaf_send(j, k)

    def split_level(level):
        high, low = halves(butterfly[level])
        weight_high[level] = high
        weight_low[level] = low

    def turn_level(level):
        turned_high[level] = weight_high[level].T
        turned_low[level] = weight_low[level].T

    def own(value, level):
        return dot_split(value, weight_high[level, :, :width], weight_low[level, :, :width], NN)

    def cross(value, level):
        return dot_split(value, weight_high[level, :, width:], weight_low[level, :, width:], NN)

    def own_turned(value, level):
        return dot_split(value, turned_high[level, :width], turned_low[level, :width], NN)

    def cross_turned(value, level):
        return dot_split(value, turned_high[level, width:], turned_low[level, width:], NN)

    sweep_copies = {}

    def sweep_send(level):
        term = cross(sweep[level + 1], level)
        if level == levels - 1:
            sweep_wide_out[...] = term
            source, target = sweep_wide_out, sweep_wide_in
        else:
            sweep_out[level] = term.astype(BF16)
            source, target = sweep_out.at[level], sweep_in.at[level]
        sweep_copies[level] = send(source, target, sweep_sem, level, sibling(level))
        sweep[level] = own(sweep[level + 1], level)

    def sweep_take(level):
        sweep_copies[level].wait_recv()
        arrived = sweep_wide_in[...] if level == levels - 1 else sweep_in[level].astype(F32)
        sweep[level] = sweep[level] + arrived
        if level > 0:
            sweep_send(level - 1)

    def gather(level, target, sems):
        target[my_rows] = sweep[level]
        return [send(sweep.at[level], target.at[my_rows], sems, k, at_x(k)) for k in range(1, n_sub)]

    loads[2].wait()
    loads[3].wait()
    split_level(2)
    sweep_send(levels - 1)
    for position, level in ((4, 0), (5, 1)):
        loads[position].wait()
        split_level(level)
        turn_level(level)
    turn_level(levels - 1)
    loads[6].wait()
    inverse_high[...], inverse_low[...] = halves(inverse[...].T)
    interp_t[...] = interp_value.T
    live = lax.broadcasted_iota(jnp.int32, (chunk, width), 1) < count_ref[0]

    up_copies = {}
    up_own = {}

    def up_send(level, j):
        rows = pl.ds(j * chunk, chunk)
        if level == 0:
            source, target = up.at[0, rows], up_wide_in.at[rows]
        else:
            up_out[level, rows] = up[level, rows].astype(BF16)
            source, target = up_out.at[level, rows], up_in.at[level, rows]
        up_copies[level, j] = send(source, target, up_sem, level * CHUNKS + j, sibling(level))
        up_own[j] = own_turned(up[level, rows], level)

    def up_start(j):
        rows = pl.ds(j * chunk, chunk)
        total = leaf[0, rows]
        for k in leaf_order[:-1][::-1]:
            leaf_copies[j, k].wait_recv()
            total = total + leaf_in[k, rows]
        up[0, rows] = jnp.where(live, total, 0.0)
        up_send(0, j)

    def up_step(level, j):
        rows = pl.ds(j * chunk, chunk)
        up_copies[level, j].wait_recv()
        arrived = up_in[level, rows] if level else up_wide_in[rows]
        up[level + 1, rows] = up_own[j] + cross_turned(arrived, level)
        if level + 1 < levels:
            up_send(level + 1, j)
        else:
            down_send(up[levels, rows], level, j)

    down_copies = {}
    down_own = {}

    def down_send(value, level, j):
        rows = pl.ds(j * chunk, chunk)
        if level == 0:
            down_wide_out[rows] = cross(value, level)
            source, target = down_wide_out.at[rows], down_wide_in.at[rows]
        else:
            down_out[level, rows] = cross(value, level).astype(BF16)
            source, target = down_out.at[level, rows], down_in.at[level, rows]
        down_copies[level, j] = send(source, target, down_sem, level * CHUNKS + j, sibling(level))
        down_own[j] = own(value, level)

    def down_value(level, j):
        rows = pl.ds(j * chunk, chunk)
        down_copies[level, j].wait_recv()
        arrived = down_in[level, rows].astype(F32) if level else down_wide_in[rows]
        return down_own[j] + arrived

    def down_step(level, j):
        down_send(down_value(level, j), level - 1, j)

    def parts(step, level, part):
        for j in range(part * CHUNKS // 2, (part + 1) * CHUNKS // 2):
            step(level, j)

    for j in range(CHUNKS):
        up_start(j)
    sweep_take(2)
    step_copies = gather(2, step_map, step_sem)
    parts(up_step, 0, 0)
    parts(up_step, 0, 1)
    parts(up_step, 1, 0)
    parts(up_step, 1, 1)

    for copy in step_copies:
        copy.wait_recv()
    step_high, step_low = halves(step_map[...].T)
    root_part[...] = dot_split(up[levels - 1], step_high, step_low, NN)

    def piece_of(k):
        return pl.ds(pl.multiple_of(((place + k) % n_plane) * piece, piece), piece)

    plane_copies = [
        send(root_part.at[piece_of(k)], root_plane.at[k], plane_sem, k, at_place(k)) for k in range(1, n_plane)]
    sweep_take(1)
    parts(up_step, 2, 0)
    total = root_part[piece_of(0)]
    for k, copy in enumerate(plane_copies, 1):
        copy.wait_recv()
        total = total + root_plane[k]
    root_mine[...] = total
    z_copies = [send(root_mine, root_z.at[k], z_sem, k, at_z(k)) for k in range(1, n_z)]
    parts(up_step, 2, 1)
    sweep_take(0)
    map_copies = gather(0, root_map, map_sem)
    parts(down_step, 2, 0)
    for k, copy in enumerate(z_copies, 1):
        copy.wait_recv()
        total = total + root_z[k]
    padded = jnp.concatenate([total, jnp.zeros_like(total)], axis=0)
    solved = dot_split(padded, inverse_high[...], inverse_low[...], NN)[:piece]
    root_piece[...] = solved
    root_all[piece_of(0)] = solved
    spread_copies = [
        send(root_piece, root_all.at[piece_of(0)], spread_sem, k, at_place(k)) for k in range(1, n_plane)]
    parts(down_step, 2, 1)
    parts(down_step, 1, 0)
    parts(down_step, 1, 1)
    for copy in map_copies:
        copy.wait_recv()
    map_high, map_low = halves(root_map[...])
    for copy in spread_copies:
        copy.wait_recv()
    root_term = dot_split(root_all[...], map_high, map_low, NN)

    back_copies = {}
    for j in range(CHUNKS):
        value = down_value(0, j) - root_term[j * chunk:(j + 1) * chunk]
        spot = pl.ds(pl.multiple_of(x * slice_cols + j * chunk, chunk), chunk)
        back[spot] = jnp.where(live, value, 0.0).astype(BF16)
        for k in leaf_order[:-1]:
            back_copies[j, k] = send(back.at[spot], back.at[spot], back_sem, j * n_sub + k, at_x(k))

    out_copies = []
    for k in (0, *leaf_order[:-1][::-1]):
        columns = pl.ds(pl.multiple_of(((x + n_sub - k) % n_sub) * slice_cols, slice_cols), slice_cols)
        if k:
            for j in range(CHUNKS):
                back_copies[j, k].wait_recv()
        out[:, columns] = rhs[:, columns].astype(F32) - dot(interp_t[...], back[columns], NT)
        copy = pltpu.make_async_copy(out.at[:, columns], out_hbm.at[:, columns], out_sem.at[k])
        copy.start()
        out_copies.append(copy)

    for copy in started:
        copy.wait_send()
    for copy in out_copies:
        copy.wait()


def local(n_plane, n_z, n_sub, rhs_points, interp, skel_count, butterfly, project, root_inverse):
    points, columns = rhs_points.shape
    width = interp.shape[0]
    levels = butterfly.shape[0]
    slice_cols = columns // n_sub
    piece = slice_cols // n_plane
    root_rows = width // n_sub
    vmem = pltpu.VMEM
    pair = lambda count: pltpu.SemaphoreType.DMA((2, count))
    scratch = [
        vmem((points, columns), BF16), vmem((width, points), BF16), vmem((points, width), BF16),
        vmem(butterfly.shape, F32), vmem((width, width), F32),
        vmem(butterfly.shape, BF16), vmem(butterfly.shape, BF16),
        vmem((levels, 2 * width, width), BF16), vmem((levels, 2 * width, width), BF16),
        vmem((width, width), BF16), vmem((width, width), BF16),
        vmem((n_sub, slice_cols, width), F32), vmem((n_sub, slice_cols, width), F32),
        vmem((levels + 1, slice_cols, width), F32), vmem((slice_cols, width), F32),
        vmem((levels, slice_cols, width), BF16), vmem((levels, slice_cols, width), BF16),
        vmem((slice_cols, width), F32), vmem((slice_cols, width), F32),
        vmem((levels, slice_cols, width), BF16), vmem((levels, slice_cols, width), BF16),
        vmem((levels + 1, root_rows, width), F32), vmem((root_rows, width), F32), vmem((root_rows, width), F32),
        vmem((levels, root_rows, width), BF16), vmem((levels, root_rows, width), BF16),
        vmem((width, width), F32), vmem((width, width), F32),
        vmem((slice_cols, width), F32), vmem((n_plane, piece, width), F32),
        vmem((piece, width), F32), vmem((n_z, piece, width), F32), vmem((piece, width), F32),
        vmem((slice_cols, width), F32),
        vmem((columns, width), BF16), vmem((points, columns), F32),
        pltpu.SemaphoreType.DMA((7,)), pltpu.SemaphoreType.DMA((n_sub,)),
        pair(CHUNKS * n_sub), pair(levels * CHUNKS), pair(levels * CHUNKS), pair(levels), pair(n_sub), pair(n_sub),
        pair(n_plane), pair(n_z), pair(n_plane), pair(CHUNKS * n_sub),
    ]
    hbm = pl.BlockSpec(memory_space=pl.ANY)
    return pl.pallas_call(
        functools.partial(kernel, n_plane, n_z, n_sub, levels),
        out_shape=jax.ShapeDtypeStruct((points, columns), F32),
        in_specs=[hbm, hbm, pl.BlockSpec(memory_space=pltpu.SMEM), hbm, hbm, hbm],
        out_specs=pl.BlockSpec(memory_space=pl.ANY),
        scratch_shapes=scratch,
        compiler_params=pltpu.CompilerParams(
            collective_id=0, has_side_effects=True, vmem_limit_bytes=62 * 2**20),
    )(rhs_points, interp, skel_count, butterfly, project, root_inverse)


def solution(mesh):
    n_box, n_sub = mesh.shape["box"], mesh.shape["sub"]
    n_z = 8
    in_specs = (
        P(("box", "sub"), None),
        P(("box", "sub"), None),
        P("box"),
        P(None, "box", None),
        P("box", None),
        P(),
    )
    out_specs = P(("box", "sub"), None)
    return jax.shard_map(
        functools.partial(local, n_box // n_z, n_z, n_sub),
        mesh=mesh, in_specs=in_specs, out_specs=out_specs, check_vma=False)
```

```python
import functools

import jax
import jax.numpy as jnp
from jax import lax
from jax.experimental import pallas as pl
from jax.experimental.pallas import tpu as pltpu
from jax.sharding import PartitionSpec as P

F32 = jnp.float32
BF16 = jnp.bfloat16
MESH = pl.DeviceIdType.MESH
CHUNKS = 4
NN = (((1,), (0,)), ((), ()))
NT = (((1,), (1,)), ((), ()))


def halves(value):
    high = value.astype(BF16)
    return high, (value - high.astype(F32)).astype(BF16)


def dot(left, right, dims):
    return lax.dot_general(left, right, dims, preferred_element_type=F32)


def dot_split(value, high, low, dims):
    rows = value.shape[0]
    if value.dtype == BF16:
        return dot(value, high, dims) + dot(value, low, dims)
    value_high, value_low = halves(value)
    both = dot(jnp.concatenate([value_high, value_low], axis=0), high, dims)
    return both[:rows] + (both[rows:] + dot(value_high, low, dims))


def kernel(
    n_plane, n_z, n_sub, levels,
    rhs_hbm, interp_hbm, count_ref, butterfly_hbm, project_hbm, inverse_hbm, out_hbm,
    rhs, interp, interp_t, butterfly, inverse,
    weight_high, weight_low, turned_high, turned_low, inverse_high, inverse_low,
    leaf, leaf_in, up, up_wide_in, up_out, up_in, down_wide_out, down_wide_in, down_out, down_in, down,
    sweep, sweep_out, sweep_in, step_map, root_map,
    root_part, root_plane, root_mine, root_z, root_piece, root_all,
    back, out,
    load_sem, out_sem, leaf_sem, up_sem, down_sem, sweep_sem, step_sem, map_sem, plane_sem, z_sem, spread_sem, back_sem,
):
    width = interp.shape[0]
    slice_cols = leaf.shape[1]
    chunk = slice_cols // CHUNKS
    root_rows = width // n_sub
    piece = slice_cols // n_plane

    box = lax.axis_index("box")
    x = lax.axis_index("sub")
    place = box % n_plane
    z = box // n_plane

    def at_x(k):
        return (box, (x + k) % n_sub)

    def at_place(k):
        return (z * n_plane + (place + k) % n_plane, x)

    def at_z(k):
        return (((z + k) % n_z) * n_plane + place, x)

    def sibling(level):
        bit = 2 ** level
        return (box + (1 - 2 * ((z // bit) % 2)) * bit * n_plane, x)

    def send(source, target, sems, index, device):
        copy = pltpu.make_async_remote_copy(
            src_ref=source, dst_ref=target, send_sem=sems.at[0, index], recv_sem=sems.at[1, index],
            device_id=device, device_id_type=MESH,
        )
        copy.start()
        started.append(copy)
        return copy

    started = []

    barrier = pltpu.get_barrier_semaphore()
    peers = ([at_x(k) for k in range(1, n_sub)] + [at_place(k) for k in range(1, n_plane)]
             + [at_z(k) for k in range(1, n_z)])
    for peer in peers:
        pl.semaphore_signal(barrier, inc=1, device_id=peer, device_id_type=MESH)

    my_rows = pl.ds(pl.multiple_of(x * root_rows, root_rows), root_rows)
    loads = []
    for source, target in (
        (interp_hbm, interp), (rhs_hbm, rhs), (project_hbm.at[my_rows], sweep.at[levels]),
        (butterfly_hbm.at[2], butterfly.at[2]), (butterfly_hbm.at[0], butterfly.at[0]),
        (butterfly_hbm.at[1], butterfly.at[1]), (inverse_hbm, inverse),
    ):
        load = pltpu.make_async_copy(source, target, load_sem.at[len(loads)])
        load.start()
        loads.append(load)

    leaf_order = sorted(range(n_sub), key=lambda k: (k == 0, -min(k, n_sub - k)))
    leaf_copies = {}

    def leaf_send(j, k):
        rows = pl.ds(j * chunk, chunk)
        leaf_copies[j, k] = send(leaf.at[k, rows], leaf_in.at[k, rows], leaf_sem, j * n_sub + k, at_x(k))

    loads[0].wait()
    loads[1].wait()
    pl.semaphore_wait(barrier, len(peers))
    interp_value = interp[...]
    for k in leaf_order:
        columns = pl.ds(pl.multiple_of(((x + k) % n_sub) * slice_cols, slice_cols), slice_cols)
        leaf[k] = dot(rhs[:, columns].T, interp_value, NT)
        if k:
            leaf_send(0, k)
    for j in range(1, CHUNKS):
        for k in leaf_order[:-1]:
            leaf_send(j, k)

    def split_level(level):
        high, low = halves(butterfly[level])
        weight_high[level] = high
        weight_low[level] = low

    def turn_level(level):
        turned_high[level] = weight_high[level].T
        turned_low[level] = weight_low[level].T

    def own(value, level):
        return dot_split(value, weight_high[level, :, :width], weight_low[level, :, :width], NN)

    def cross(value, level):
        return dot_split(value, weight_high[level, :, width:], weight_low[level, :, width:], NN)

    def own_turned(value, level):
        return dot_split(value, turned_high[level, :width], turned_low[level, :width], NN)

    def cross_turned(value, level):
        return dot_split(value, turned_high[level, width:], turned_low[level, width:], NN)

    sweep_copies = {}

    def sweep_send(level):
        sweep_out[level] = cross(sweep[level + 1], level)
        sweep_copies[level] = send(
            sweep_out.at[level], sweep_in.at[level], sweep_sem, level, sibling(level))
        sweep[level] = own(sweep[level + 1], level)

    def sweep_take(level):
        sweep_copies[level].wait_recv()
        sweep[level] = sweep[level] + sweep_in[level]
        if level > 0:
            sweep_send(level - 1)

    def gather(level, target, sems):
        target[my_rows] = sweep[level]
        return [send(sweep.at[level], target.at[my_rows], sems, k, at_x(k)) for k in range(1, n_sub)]

    loads[2].wait()
    loads[3].wait()
    split_level(2)
    sweep_send(levels - 1)
    for position, level in ((4, 0), (5, 1)):
        loads[position].wait()
        split_level(level)
        turn_level(level)
    turn_level(levels - 1)
    loads[6].wait()
    inverse_high[...], inverse_low[...] = halves(inverse[...].T)
    interp_t[...] = interp_value.T
    live = lax.broadcasted_iota(jnp.int32, (chunk, width), 1) < count_ref[0]

    up_copies = {}

    def rows_of(j):
        return pl.ds(j * chunk, chunk)

    def up_send(level, j):
        rows = rows_of(j)
        if level == 0:
            source, target = up.at[0, rows], up_wide_in.at[rows]
        else:
            up_out[level, rows] = up[level, rows].astype(BF16)
            source, target = up_out.at[level, rows], up_in.at[level, rows]
        up_copies[level, j] = send(source, target, up_sem, level * CHUNKS + j, sibling(level))

    def up_start(j):
        rows = rows_of(j)
        total = leaf[0, rows]
        for k in leaf_order[:-1][::-1]:
            leaf_copies[j, k].wait_recv()
            total = total + leaf_in[k, rows]
        up[0, rows] = jnp.where(live, total, 0.0)
        up_send(0, j)

    def up_step(level, j):
        rows = rows_of(j)
        up_copies[level, j].wait_recv()
        arrived = up_in[level, rows] if level else up_wide_in[rows]
        up[level + 1, rows] = up[level + 1, rows] + cross_turned(arrived, level)
        if level + 1 < levels:
            up_send(level + 1, j)
        else:
            down_send(up[levels, rows], level, j)

    def up_own(level):
        up[level + 1] = own_turned(up[level], level)

    down_copies = {}

    def down_send(value, level, j):
        rows = rows_of(j)
        if level == 0:
            down_wide_out[rows] = cross(value, level)
            source, target = down_wide_out.at[rows], down_wide_in.at[rows]
        else:
            down_out[level, rows] = cross(value, level).astype(BF16)
            source, target = down_out.at[level, rows], down_in.at[level, rows]
        down_copies[level, j] = send(source, target, down_sem, level * CHUNKS + j, sibling(level))

    def down_value(level, j):
        rows = rows_of(j)
        down_copies[level, j].wait_recv()
        arrived = down_in[level, rows].astype(F32) if level else down_wide_in[rows]
        return down[level, rows] + arrived

    def down_step(level, j):
        value = down_value(level, j)
        down[level, rows_of(j)] = value
        down_send(value, level - 1, j)

    def every(step, level, part=range(CHUNKS)):
        for j in part:
            step(level, j)

    for j in range(CHUNKS):
        up_start(j)
    up_own(0)
    sweep_take(2)
    step_copies = gather(2, step_map, step_sem)
    every(up_step, 0)
    up_own(1)
    every(up_step, 1)

    for copy in step_copies:
        copy.wait_recv()
    step_high, step_low = halves(step_map[...].T)
    root_part[...] = dot_split(up[levels - 1], step_high, step_low, NN)

    def piece_of(k):
        return pl.ds(pl.multiple_of(((place + k) % n_plane) * piece, piece), piece)

    plane_copies = [
        send(root_part.at[piece_of(k)], root_plane.at[k], plane_sem, k, at_place(k)) for k in range(1, n_plane)]
    up_own(2)
    sweep_take(1)
    every(up_step, 2)
    total = root_part[piece_of(0)]
    for k, copy in enumerate(plane_copies, 1):
        copy.wait_recv()
        total = total + root_plane[k]
    root_mine[...] = total
    z_copies = [send(root_mine, root_z.at[k], z_sem, k, at_z(k)) for k in range(1, n_z)]
    down[2] = own(up[levels], 2)
    sweep_take(0)
    map_copies = gather(0, root_map, map_sem)
    every(down_step, 2, range(CHUNKS // 2))
    for k, copy in enumerate(z_copies, 1):
        copy.wait_recv()
        total = total + root_z[k]
    padded = jnp.concatenate([total, jnp.zeros_like(total)], axis=0)
    solved = dot_split(padded, inverse_high[...], inverse_low[...], NN)[:piece]
    root_piece[...] = solved
    root_all[piece_of(0)] = solved
    spread_copies = [
        send(root_piece, root_all.at[piece_of(0)], spread_sem, k, at_place(k)) for k in range(1, n_plane)]
    every(down_step, 2, range(CHUNKS // 2, CHUNKS))
    down[1] = own(down[2], 1)
    every(down_step, 1)
    down[0] = own(down[1], 0)
    for copy in map_copies:
        copy.wait_recv()
    map_high, map_low = halves(root_map[...])
    for copy in spread_copies:
        copy.wait_recv()
    root_term = dot_split(root_all[...], map_high, map_low, NN)

    back_copies = {}
    for j in range(CHUNKS):
        value = down_value(0, j) - root_term[j * chunk:(j + 1) * chunk]
        spot = pl.ds(pl.multiple_of(x * slice_cols + j * chunk, chunk), chunk)
        back[spot] = jnp.where(live, value, 0.0).astype(BF16)
        for k in leaf_order[:-1]:
            back_copies[j, k] = send(back.at[spot], back.at[spot], back_sem, j * n_sub + k, at_x(k))

    out_copies = []
    for k in (0, *leaf_order[:-1][::-1]):
        columns = pl.ds(pl.multiple_of(((x + n_sub - k) % n_sub) * slice_cols, slice_cols), slice_cols)
        if k:
            for j in range(CHUNKS):
                back_copies[j, k].wait_recv()
        out[:, columns] = rhs[:, columns].astype(F32) - dot(interp_t[...], back[columns], NT)
        copy = pltpu.make_async_copy(out.at[:, columns], out_hbm.at[:, columns], out_sem.at[k])
        copy.start()
        out_copies.append(copy)

    for copy in started:
        copy.wait_send()
    for copy in out_copies:
        copy.wait()


def local(n_plane, n_z, n_sub, rhs_points, interp, skel_count, butterfly, project, root_inverse):
    points, columns = rhs_points.shape
    width = interp.shape[0]
    levels = butterfly.shape[0]
    slice_cols = columns // n_sub
    piece = slice_cols // n_plane
    root_rows = width // n_sub
    vmem = pltpu.VMEM
    pair = lambda count: pltpu.SemaphoreType.DMA((2, count))
    scratch = [
        vmem((points, columns), BF16), vmem((width, points), BF16), vmem((points, width), BF16),
        vmem(butterfly.shape, F32), vmem((width, width), F32),
        vmem(butterfly.shape, BF16), vmem(butterfly.shape, BF16),
        vmem((levels, 2 * width, width), BF16), vmem((levels, 2 * width, width), BF16),
        vmem((width, width), BF16), vmem((width, width), BF16),
        vmem((n_sub, slice_cols, width), F32), vmem((n_sub, slice_cols, width), F32),
        vmem((levels + 1, slice_cols, width), F32), vmem((slice_cols, width), F32),
        vmem((levels, slice_cols, width), BF16), vmem((levels, slice_cols, width), BF16),
        vmem((slice_cols, width), F32), vmem((slice_cols, width), F32),
        vmem((levels, slice_cols, width), BF16), vmem((levels, slice_cols, width), BF16),
        vmem((levels, slice_cols, width), F32),
        vmem((levels + 1, root_rows, width), F32), vmem((levels, root_rows, width), F32),
        vmem((levels, root_rows, width), F32), vmem((width, width), F32), vmem((width, width), F32),
        vmem((slice_cols, width), F32), vmem((n_plane, piece, width), F32),
        vmem((piece, width), F32), vmem((n_z, piece, width), F32), vmem((piece, width), F32),
        vmem((slice_cols, width), F32),
        vmem((columns, width), BF16), vmem((points, columns), F32),
        pltpu.SemaphoreType.DMA((7,)), pltpu.SemaphoreType.DMA((n_sub,)),
        pair(CHUNKS * n_sub), pair(levels * CHUNKS), pair(levels * CHUNKS), pair(levels), pair(n_sub), pair(n_sub),
        pair(n_plane), pair(n_z), pair(n_plane), pair(CHUNKS * n_sub),
    ]
    hbm = pl.BlockSpec(memory_space=pl.ANY)
    return pl.pallas_call(
        functools.partial(kernel, n_plane, n_z, n_sub, levels),
        out_shape=jax.ShapeDtypeStruct((points, columns), F32),
        in_specs=[hbm, hbm, pl.BlockSpec(memory_space=pltpu.SMEM), hbm, hbm, hbm],
        out_specs=pl.BlockSpec(memory_space=pl.ANY),
        scratch_shapes=scratch,
        compiler_params=pltpu.CompilerParams(
            collective_id=0, has_side_effects=True, vmem_limit_bytes=62 * 2**20),
    )(rhs_points, interp, skel_count, butterfly, project, root_inverse)


def solution(mesh):
    n_box, n_sub = mesh.shape["box"], mesh.shape["sub"]
    n_z = 8
    in_specs = (
        P(("box", "sub"), None),
        P(("box", "sub"), None),
        P("box"),
        P(None, "box", None),
        P("box", None),
        P(),
    )
    out_specs = P(("box", "sub"), None)
    return jax.shard_map(
        functools.partial(local, n_box // n_z, n_z, n_sub),
        mesh=mesh, in_specs=in_specs, out_specs=out_specs, check_vma=False)
```

```python
import functools

import jax
import jax.numpy as jnp
from jax import lax
from jax.experimental import pallas as pl
from jax.experimental.pallas import tpu as pltpu
from jax.sharding import PartitionSpec as P

F32 = jnp.float32
BF16 = jnp.bfloat16
MESH = pl.DeviceIdType.MESH
CHUNKS = 2
NN = (((1,), (0,)), ((), ()))
NT = (((1,), (1,)), ((), ()))


def halves(value):
    high = value.astype(BF16)
    return high, (value - high.astype(F32)).astype(BF16)


def dot(left, right, dims):
    return lax.dot_general(left, right, dims, preferred_element_type=F32)


def dot_split(value, high, low, dims):
    rows = value.shape[0]
    if value.dtype == BF16:
        return dot(value, high, dims) + dot(value, low, dims)
    value_high, value_low = halves(value)
    both = dot(jnp.concatenate([value_high, value_low], axis=0), high, dims)
    return both[:rows] + (both[rows:] + dot(value_high, low, dims))


def kernel(
    n_plane, n_z, n_sub, levels,
    rhs_hbm, interp_hbm, count_ref, butterfly_hbm, project_hbm, inverse_hbm, out_hbm,
    rhs, interp, interp_t, butterfly, inverse,
    weight_high, weight_low, turned_high, turned_low, inverse_turned,
    leaf, leaf_in, up, up_wide_in, up_out, up_in, down_wide_out, down_wide_in, down_out, down_in, down,
    sweep, sweep_out, sweep_in, step_map, root_map,
    root_part, root_out, root_plane, root_mine, root_z, root_piece, root_all,
    back, out,
    load_sem, out_sem, leaf_sem, up_sem, down_sem, sweep_sem, step_sem, map_sem, plane_sem, z_sem, spread_sem, back_sem,
):
    width = interp.shape[0]
    slice_cols = leaf.shape[1]
    chunk = slice_cols // CHUNKS
    root_rows = width // n_sub
    piece = (2 * slice_cols // n_plane, width // 2)

    box = lax.axis_index("box")
    x = lax.axis_index("sub")
    place = box % n_plane
    z = box // n_plane

    def at_x(k):
        return (box, (x + k) % n_sub)

    def at_place(k):
        return (z * n_plane + (place + k) % n_plane, x)

    def at_z(k):
        return (((z + k) % n_z) * n_plane + place, x)

    def sibling(level):
        bit = 2 ** level
        return (box + (1 - 2 * ((z // bit) % 2)) * bit * n_plane, x)

    def send(source, target, sems, index, device):
        copy = pltpu.make_async_remote_copy(
            src_ref=source, dst_ref=target, send_sem=sems.at[0, index], recv_sem=sems.at[1, index],
            device_id=device, device_id_type=MESH,
        )
        copy.start()
        started.append(copy)
        return copy

    started = []

    barrier = pltpu.get_barrier_semaphore()
    peers = ([at_x(k) for k in range(1, n_sub)] + [at_place(k) for k in range(1, n_plane)]
             + [at_z(k) for k in range(1, n_z)])
    for peer in peers:
        pl.semaphore_signal(barrier, inc=1, device_id=peer, device_id_type=MESH)

    my_rows = pl.ds(pl.multiple_of(x * root_rows, root_rows), root_rows)
    loads = []
    for source, target in (
        (interp_hbm, interp), (rhs_hbm, rhs), (project_hbm.at[my_rows], sweep.at[levels]),
        (butterfly_hbm.at[2], butterfly.at[2]), (butterfly_hbm.at[0], butterfly.at[0]),
        (butterfly_hbm.at[1], butterfly.at[1]), (inverse_hbm, inverse),
    ):
        load = pltpu.make_async_copy(source, target, load_sem.at[len(loads)])
        load.start()
        loads.append(load)

    leaf_order = sorted(range(n_sub), key=lambda k: (k == 0, -min(k, n_sub - k)))
    leaf_copies = {}

    def leaf_send(j, k):
        rows = pl.ds(j * chunk, chunk)
        leaf_copies[j, k] = send(leaf.at[k, rows], leaf_in.at[k, rows], leaf_sem, j * n_sub + k, at_x(k))

    loads[0].wait()
    loads[1].wait()
    pl.semaphore_wait(barrier, len(peers))
    interp_value = interp[...]
    for k in leaf_order:
        columns = pl.ds(pl.multiple_of(((x + k) % n_sub) * slice_cols, slice_cols), slice_cols)
        leaf[k] = dot(rhs[:, columns].T, interp_value, NT)
        if k:
            leaf_send(0, k)
    for j in range(1, CHUNKS):
        for k in leaf_order[:-1]:
            leaf_send(j, k)

    def split_level(level):
        high, low = halves(butterfly[level])
        weight_high[level] = high
        weight_low[level] = low

    def turn_level(level):
        turned_high[level] = weight_high[level].T
        turned_low[level] = weight_low[level].T

    def own(value, level):
        return dot_split(value, weight_high[level, :, :width], weight_low[level, :, :width], NN)

    def cross(value, level):
        return dot_split(value, weight_high[level, :, width:], weight_low[level, :, width:], NN)

    def own_turned(value, level):
        return dot_split(value, turned_high[level, :width], turned_low[level, :width], NN)

    def cross_turned(value, level):
        return dot_split(value, turned_high[level, width:], turned_low[level, width:], NN)

    sweep_copies = {}

    def sweep_send(level):
        sweep_out[level] = cross(sweep[level + 1], level)
        sweep_copies[level] = send(
            sweep_out.at[level], sweep_in.at[level], sweep_sem, level, sibling(level))
        sweep[level] = own(sweep[level + 1], level)

    def sweep_take(level):
        sweep_copies[level].wait_recv()
        sweep[level] = sweep[level] + sweep_in[level]
        if level > 0:
            sweep_send(level - 1)

    def gather(level, target, sems):
        target[my_rows] = sweep[level]
        return [send(sweep.at[level], target.at[my_rows], sems, k, at_x(k)) for k in range(1, n_sub)]

    loads[2].wait()
    loads[3].wait()
    split_level(2)
    sweep_send(levels - 1)
    for position, level in ((4, 0), (5, 1)):
        loads[position].wait()
        split_level(level)
        turn_level(level)
    turn_level(levels - 1)
    loads[6].wait()
    inverse_turned[...] = inverse[...].T
    interp_t[...] = interp_value.T
    live = lax.broadcasted_iota(jnp.int32, (chunk, width), 1) < count_ref[0]

    up_copies = {}

    def rows_of(j):
        return pl.ds(j * chunk, chunk)

    def up_send(level, j):
        rows = rows_of(j)
        if level == 0:
            source, target = up.at[0, rows], up_wide_in.at[rows]
        else:
            up_out[level, rows] = up[level, rows].astype(BF16)
            source, target = up_out.at[level, rows], up_in.at[level, rows]
        up_copies[level, j] = send(source, target, up_sem, level * CHUNKS + j, sibling(level))

    def up_start(j):
        rows = rows_of(j)
        total = leaf[0, rows]
        for k in leaf_order[:-1][::-1]:
            leaf_copies[j, k].wait_recv()
            total = total + leaf_in[k, rows]
        up[0, rows] = jnp.where(live, total, 0.0)
        up_send(0, j)

    def up_step(level, j):
        rows = rows_of(j)
        up_copies[level, j].wait_recv()
        arrived = up_in[level, rows] if level else up_wide_in[rows]
        up[level + 1, rows] = up[level + 1, rows] + cross_turned(arrived, level)
        if level + 1 < levels:
            up_send(level + 1, j)
        else:
            down_send(up[levels, rows], level, j)

    def up_own(level):
        up[level + 1] = own_turned(up[level], level)

    down_copies = {}

    def down_send(value, level, j):
        rows = rows_of(j)
        term = cross(value, level)
        if level == levels - 1:
            down_out[rows] = term.astype(BF16)
            source, target = down_out.at[rows], down_in.at[rows]
        else:
            down_wide_out[level, rows] = term
            source, target = down_wide_out.at[level, rows], down_wide_in.at[level, rows]
        down_copies[level, j] = send(source, target, down_sem, level * CHUNKS + j, sibling(level))

    def down_value(level, j):
        rows = rows_of(j)
        down_copies[level, j].wait_recv()
        arrived = down_in[rows].astype(F32) if level == levels - 1 else down_wide_in[level, rows]
        return down[level, rows] + arrived

    def down_step(level, j):
        value = down_value(level, j)
        down[level, rows_of(j)] = value
        down_send(value, level - 1, j)

    def every(step, level, part=range(CHUNKS)):
        for j in part:
            step(level, j)

    for j in range(CHUNKS):
        up_start(j)
    up_own(0)
    sweep_take(2)
    step_copies = gather(2, step_map, step_sem)
    every(up_step, 0)
    up_own(1)
    every(up_step, 1, range(CHUNKS // 2))
    for copy in step_copies:
        copy.wait_recv()
    step_high, step_low = halves(step_map[...].T)
    every(up_step, 1, range(CHUNKS // 2, CHUNKS))

    root_part[...] = dot_split(up[levels - 1], step_high, step_low, NN)
    root_out[...] = root_part[...].astype(BF16)

    def piece_of(k):
        index = (place + k) % n_plane
        rows = pl.ds(pl.multiple_of(index // 2 * piece[0], piece[0]), piece[0])
        return rows, pl.ds(pl.multiple_of(index % 2 * piece[1], piece[1]), piece[1])

    plane_copies = [
        send(root_out.at[piece_of(k)], root_plane.at[k], plane_sem, k, at_place(k)) for k in range(1, n_plane)]
    up_own(2)
    sweep_take(1)
    total = root_part[piece_of(0)]
    for k, copy in enumerate(plane_copies, 1):
        copy.wait_recv()
        total = total + root_plane[k].astype(F32)
    root_mine[...] = total.astype(BF16)
    z_copies = [send(root_mine, root_z.at[k], z_sem, k, at_z(k)) for k in range(1, n_z)]
    every(up_step, 2)
    down[2] = own(up[levels], 2)
    sweep_take(0)
    map_copies = gather(0, root_map, map_sem)
    for k, copy in enumerate(z_copies, 1):
        copy.wait_recv()
        total = total + root_z[k].astype(F32)
    root_piece[...] = total.astype(BF16)
    root_all[piece_of(0)] = total.astype(BF16)
    spread_copies = [
        send(root_piece, root_all.at[piece_of(0)], spread_sem, k, at_place(k)) for k in range(1, n_plane)]
    every(down_step, 2)
    down[1] = own(down[2], 1)
    for copy in map_copies:
        copy.wait_recv()
    map_high, map_low = halves(root_map[...])
    map_high, map_low = halves(dot_split(inverse_turned[...], map_high, map_low, NN))
    every(down_step, 1)
    down[0] = own(down[1], 0)
    for copy in spread_copies:
        copy.wait_recv()
    root_term = dot_split(root_all[...], map_high, map_low, NN)

    back_copies = {}
    for j in range(CHUNKS):
        value = down_value(0, j) - root_term[j * chunk:(j + 1) * chunk]
        spot = pl.ds(pl.multiple_of(x * slice_cols + j * chunk, chunk), chunk)
        back[spot] = jnp.where(live, value, 0.0).astype(BF16)
        for k in leaf_order[:-1]:
            back_copies[j, k] = send(back.at[spot], back.at[spot], back_sem, j * n_sub + k, at_x(k))

    out_copies = []
    for k in (0, *leaf_order[:-1][::-1]):
        columns = pl.ds(pl.multiple_of(((x + n_sub - k) % n_sub) * slice_cols, slice_cols), slice_cols)
        if k:
            for j in range(CHUNKS):
                back_copies[j, k].wait_recv()
        out[:, columns] = rhs[:, columns].astype(F32) - dot(interp_t[...], back[columns], NT)
        copy = pltpu.make_async_copy(out.at[:, columns], out_hbm.at[:, columns], out_sem.at[k])
        copy.start()
        out_copies.append(copy)

    for copy in started:
        copy.wait_send()
    for copy in out_copies:
        copy.wait()


def local(n_plane, n_z, n_sub, rhs_points, interp, skel_count, butterfly, project, root_inverse):
    points, columns = rhs_points.shape
    width = interp.shape[0]
    levels = butterfly.shape[0]
    slice_cols = columns // n_sub
    piece = (2 * slice_cols // n_plane, width // 2)
    root_rows = width // n_sub
    vmem = pltpu.VMEM
    pair = lambda count: pltpu.SemaphoreType.DMA((2, count))
    scratch = [
        vmem((points, columns), BF16), vmem((width, points), BF16), vmem((points, width), BF16),
        vmem(butterfly.shape, F32), vmem((width, width), F32),
        vmem(butterfly.shape, BF16), vmem(butterfly.shape, BF16),
        vmem((levels, 2 * width, width), BF16), vmem((levels, 2 * width, width), BF16),
        vmem((width, width), F32),
        vmem((n_sub, slice_cols, width), F32), vmem((n_sub, slice_cols, width), F32),
        vmem((levels + 1, slice_cols, width), F32), vmem((slice_cols, width), F32),
        vmem((levels, slice_cols, width), BF16), vmem((levels, slice_cols, width), BF16),
        vmem((levels - 1, slice_cols, width), F32), vmem((levels - 1, slice_cols, width), F32),
        vmem((slice_cols, width), BF16), vmem((slice_cols, width), BF16),
        vmem((levels, slice_cols, width), F32),
        vmem((levels + 1, root_rows, width), F32), vmem((levels, root_rows, width), F32),
        vmem((levels, root_rows, width), F32), vmem((width, width), F32), vmem((width, width), F32),
        vmem((slice_cols, width), F32), vmem((slice_cols, width), BF16), vmem((n_plane, *piece), BF16),
        vmem(piece, BF16), vmem((n_z, *piece), BF16), vmem(piece, BF16), vmem((slice_cols, width), BF16),
        vmem((columns, width), BF16), vmem((points, columns), F32),
        pltpu.SemaphoreType.DMA((7,)), pltpu.SemaphoreType.DMA((n_sub,)),
        pair(CHUNKS * n_sub), pair(levels * CHUNKS), pair(levels * CHUNKS), pair(levels), pair(n_sub), pair(n_sub),
        pair(n_plane), pair(n_z), pair(n_plane), pair(CHUNKS * n_sub),
    ]
    hbm = pl.BlockSpec(memory_space=pl.ANY)
    return pl.pallas_call(
        functools.partial(kernel, n_plane, n_z, n_sub, levels),
        out_shape=jax.ShapeDtypeStruct((points, columns), F32),
        in_specs=[hbm, hbm, pl.BlockSpec(memory_space=pltpu.SMEM), hbm, hbm, hbm],
        out_specs=pl.BlockSpec(memory_space=pl.ANY),
        scratch_shapes=scratch,
        compiler_params=pltpu.CompilerParams(
            collective_id=0, has_side_effects=True, vmem_limit_bytes=62 * 2**20),
    )(rhs_points, interp, skel_count, butterfly, project, root_inverse)


def solution(mesh):
    n_box, n_sub = mesh.shape["box"], mesh.shape["sub"]
    n_z = 8
    in_specs = (
        P(("box", "sub"), None),
        P(("box", "sub"), None),
        P("box"),
        P(None, "box", None),
        P("box", None),
        P(),
    )
    out_specs = P(("box", "sub"), None)
    return jax.shard_map(
        functools.partial(local, n_box // n_z, n_z, n_sub),
        mesh=mesh, in_specs=in_specs, out_specs=out_specs, check_vma=False)
```

```python
import functools

import jax
import jax.numpy as jnp
from jax import lax
from jax.experimental import pallas as pl
from jax.experimental.pallas import tpu as pltpu
from jax.sharding import PartitionSpec as P

F32 = jnp.float32
BF16 = jnp.bfloat16
MESH = pl.DeviceIdType.MESH
CHUNKS = 2
NN = (((1,), (0,)), ((), ()))
NT = (((1,), (1,)), ((), ()))


def halves(value):
    high = value.astype(BF16)
    return high, (value - high.astype(F32)).astype(BF16)


def dot(left, right, dims):
    return lax.dot_general(left, right, dims, preferred_element_type=F32)


def dot_split(value, high, low, dims):
    rows = value.shape[0]
    if value.dtype == BF16:
        return dot(value, high, dims) + dot(value, low, dims)
    value_high, value_low = halves(value)
    both = dot(jnp.concatenate([value_high, value_low], axis=0), high, dims)
    return both[:rows] + (both[rows:] + dot(value_high, low, dims))


def kernel(
    n_plane, n_z, n_sub, levels,
    rhs_hbm, interp_hbm, count_ref, butterfly_hbm, project_hbm, inverse_hbm, out_hbm,
    rhs, interp, interp_t, butterfly, inverse,
    weight_high, weight_low, turned_high, turned_low, inverse_high, inverse_low,
    leaf, leaf_in, up, up_wide_in, up_out, up_in, down_wide_out, down_wide_in, down_out, down_in, down,
    sweep, sweep_out, sweep_in, step_map, root_map,
    root_part, root_plane, root_mine, root_z, root_piece, root_all,
    back, out,
    load_sem, out_sem, leaf_sem, up_sem, down_sem, sweep_sem, step_sem, map_sem, plane_sem, z_sem, spread_sem, back_sem,
):
    width = interp.shape[0]
    slice_cols = leaf.shape[1]
    chunk = slice_cols // CHUNKS
    root_rows = width // n_sub
    piece = slice_cols // n_plane

    box = lax.axis_index("box")
    x = lax.axis_index("sub")
    place = box % n_plane
    z = box // n_plane

    def at_x(k):
        return (box, (x + k) % n_sub)

    def at_place(k):
        return (z * n_plane + (place + k) % n_plane, x)

    def at_z(k):
        return (((z + k) % n_z) * n_plane + place, x)

    def sibling(level):
        bit = 2 ** level
        return (box + (1 - 2 * ((z // bit) % 2)) * bit * n_plane, x)

    def send(source, target, sems, index, device):
        copy = pltpu.make_async_remote_copy(
            src_ref=source, dst_ref=target, send_sem=sems.at[0, index], recv_sem=sems.at[1, index],
            device_id=device, device_id_type=MESH,
        )
        copy.start()
        started.append(copy)
        return copy

    started = []

    barrier = pltpu.get_barrier_semaphore()
    peers = ([at_x(k) for k in range(1, n_sub)] + [at_place(k) for k in range(1, n_plane)]
             + [at_z(k) for k in range(1, n_z)])
    for peer in peers:
        pl.semaphore_signal(barrier, inc=1, device_id=peer, device_id_type=MESH)

    my_rows = pl.ds(pl.multiple_of(x * root_rows, root_rows), root_rows)
    loads = []
    for source, target in (
        (interp_hbm, interp), (rhs_hbm, rhs), (project_hbm.at[my_rows], sweep.at[levels]),
        (butterfly_hbm.at[2], butterfly.at[2]), (butterfly_hbm.at[0], butterfly.at[0]),
        (butterfly_hbm.at[1], butterfly.at[1]), (inverse_hbm, inverse),
    ):
        load = pltpu.make_async_copy(source, target, load_sem.at[len(loads)])
        load.start()
        loads.append(load)

    leaf_order = sorted(range(n_sub), key=lambda k: (k == 0, -min(k, n_sub - k)))
    leaf_copies = {}

    def leaf_send(j, k):
        rows = pl.ds(j * chunk, chunk)
        leaf_copies[j, k] = send(leaf.at[k, rows], leaf_in.at[k, rows], leaf_sem, j * n_sub + k, at_x(k))

    loads[0].wait()
    loads[1].wait()
    pl.semaphore_wait(barrier, len(peers))
    interp_value = interp[...]
    for k in leaf_order:
        columns = pl.ds(pl.multiple_of(((x + k) % n_sub) * slice_cols, slice_cols), slice_cols)
        leaf[k] = dot(rhs[:, columns].T, interp_value, NT)
        if k:
            leaf_send(0, k)
    for j in range(1, CHUNKS):
        for k in leaf_order[:-1]:
            leaf_send(j, k)

    def split_level(level):
        high, low = halves(butterfly[level])
        weight_high[level] = high
        weight_low[level] = low

    def turn_level(level):
        turned_high[level] = weight_high[level].T
        turned_low[level] = weight_low[level].T

    def own(value, level):
        return dot_split(value, weight_high[level, :, :width], weight_low[level, :, :width], NN)

    def cross(value, level):
        return dot_split(value, weight_high[level, :, width:], weight_low[level, :, width:], NN)

    def own_turned(value, level):
        return dot_split(value, turned_high[level, :width], turned_low[level, :width], NN)

    def cross_turned(value, level):
        return dot_split(value, turned_high[level, width:], turned_low[level, width:], NN)

    sweep_copies = {}

    def sweep_send(level):
        sweep_out[level] = cross(sweep[level + 1], level)
        sweep_copies[level] = send(
            sweep_out.at[level], sweep_in.at[level], sweep_sem, level, sibling(level))
        sweep[level] = own(sweep[level + 1], level)

    def sweep_take(level):
        sweep_copies[level].wait_recv()
        sweep[level] = sweep[level] + sweep_in[level]
        if level > 0:
            sweep_send(level - 1)

    def gather(level, target, sems):
        target[my_rows] = sweep[level]
        return [send(sweep.at[level], target.at[my_rows], sems, k, at_x(k)) for k in range(1, n_sub)]

    loads[2].wait()
    loads[3].wait()
    split_level(2)
    sweep_send(levels - 1)
    for position, level in ((4, 0), (5, 1)):
        loads[position].wait()
        split_level(level)
        turn_level(level)
    turn_level(levels - 1)
    loads[6].wait()
    inverse_high[...], inverse_low[...] = halves(inverse[...].T)
    interp_t[...] = interp_value.T
    live = lax.broadcasted_iota(jnp.int32, (chunk, width), 1) < count_ref[0]

    up_copies = {}

    def rows_of(j):
        return pl.ds(j * chunk, chunk)

    def up_send(level, j):
        rows = rows_of(j)
        if level == 0:
            source, target = up.at[0, rows], up_wide_in.at[rows]
        else:
            up_out[level, rows] = up[level, rows].astype(BF16)
            source, target = up_out.at[level, rows], up_in.at[level, rows]
        up_copies[level, j] = send(source, target, up_sem, level * CHUNKS + j, sibling(level))

    def up_start(j):
        rows = rows_of(j)
        total = leaf[0, rows]
        for k in leaf_order[:-1][::-1]:
            leaf_copies[j, k].wait_recv()
            total = total + leaf_in[k, rows]
        up[0, rows] = jnp.where(live, total, 0.0)
        up_send(0, j)

    def up_step(level, j):
        rows = rows_of(j)
        up_copies[level, j].wait_recv()
        arrived = up_in[level, rows] if level else up_wide_in[rows]
        up[level + 1, rows] = up[level + 1, rows] + cross_turned(arrived, level)
        if level + 1 < levels:
            up_send(level + 1, j)
        else:
            down_send(up[levels, rows], level, j)

    def up_own(level):
        up[level + 1] = own_turned(up[level], level)

    down_copies = {}

    def down_send(value, level, j):
        rows = rows_of(j)
        if level == 0:
            down_wide_out[rows] = cross(value, level)
            source, target = down_wide_out.at[rows], down_wide_in.at[rows]
        else:
            down_out[level, rows] = cross(value, level).astype(BF16)
            source, target = down_out.at[level, rows], down_in.at[level, rows]
        down_copies[level, j] = send(source, target, down_sem, level * CHUNKS + j, sibling(level))

    def down_value(level, j):
        rows = rows_of(j)
        down_copies[level, j].wait_recv()
        arrived = down_in[level, rows].astype(F32) if level else down_wide_in[rows]
        return down[level, rows] + arrived

    def down_step(level, j):
        value = down_value(level, j)
        down[level, rows_of(j)] = value
        down_send(value, level - 1, j)

    def every(step, level, part=range(CHUNKS)):
        for j in part:
            step(level, j)

    for j in range(CHUNKS):
        up_start(j)
    up_own(0)
    sweep_take(2)
    step_copies = gather(2, step_map, step_sem)
    every(up_step, 0)
    up_own(1)
    every(up_step, 1)

    for copy in step_copies:
        copy.wait_recv()
    step_high, step_low = halves(step_map[...].T)
    root_part[...] = dot_split(up[levels - 1], step_high, step_low, NN)

    def piece_of(k):
        return pl.ds(pl.multiple_of(((place + k) % n_plane) * piece, piece), piece)

    plane_copies = [
        send(root_part.at[piece_of(k)], root_plane.at[k], plane_sem, k, at_place(k)) for k in range(1, n_plane)]
    up_own(2)
    sweep_take(1)
    every(up_step, 2)
    total = root_part[piece_of(0)]
    for k, copy in enumerate(plane_copies, 1):
        copy.wait_recv()
        total = total + root_plane[k]
    root_mine[...] = total
    z_copies = [send(root_mine, root_z.at[k], z_sem, k, at_z(k)) for k in range(1, n_z)]
    down[2] = own(up[levels], 2)
    sweep_take(0)
    map_copies = gather(0, root_map, map_sem)
    every(down_step, 2, range(CHUNKS // 2))
    for k, copy in enumerate(z_copies, 1):
        copy.wait_recv()
        total = total + root_z[k]
    padded = jnp.concatenate([total, jnp.zeros_like(total)], axis=0)
    solved = dot_split(padded, inverse_high[...], inverse_low[...], NN)[:piece]
    root_piece[...] = solved
    root_all[piece_of(0)] = solved
    spread_copies = [
        send(root_piece, root_all.at[piece_of(0)], spread_sem, k, at_place(k)) for k in range(1, n_plane)]
    every(down_step, 2, range(CHUNKS // 2, CHUNKS))
    down[1] = own(down[2], 1)
    every(down_step, 1)
    down[0] = own(down[1], 0)
    for copy in map_copies:
        copy.wait_recv()
    map_high, map_low = halves(root_map[...])
    for copy in spread_copies:
        copy.wait_recv()
    root_term = dot_split(root_all[...], map_high, map_low, NN)

    back_copies = {}
    for j in range(CHUNKS):
        value = down_value(0, j) - root_term[j * chunk:(j + 1) * chunk]
        spot = pl.ds(pl.multiple_of(x * slice_cols + j * chunk, chunk), chunk)
        back[spot] = jnp.where(live, value, 0.0).astype(BF16)
        for k in leaf_order[:-1]:
            back_copies[j, k] = send(back.at[spot], back.at[spot], back_sem, j * n_sub + k, at_x(k))

    out_copies = []
    for k in (0, *leaf_order[:-1][::-1]):
        columns = pl.ds(pl.multiple_of(((x + n_sub - k) % n_sub) * slice_cols, slice_cols), slice_cols)
        if k:
            for j in range(CHUNKS):
                back_copies[j, k].wait_recv()
        out[:, columns] = rhs[:, columns].astype(F32) - dot(interp_t[...], back[columns], NT)
        copy = pltpu.make_async_copy(out.at[:, columns], out_hbm.at[:, columns], out_sem.at[k])
        copy.start()
        out_copies.append(copy)

    for copy in started:
        copy.wait_send()
    for copy in out_copies:
        copy.wait()


def local(n_plane, n_z, n_sub, rhs_points, interp, skel_count, butterfly, project, root_inverse):
    points, columns = rhs_points.shape
    width = interp.shape[0]
    levels = butterfly.shape[0]
    slice_cols = columns // n_sub
    piece = slice_cols // n_plane
    root_rows = width // n_sub
    vmem = pltpu.VMEM
    pair = lambda count: pltpu.SemaphoreType.DMA((2, count))
    scratch = [
        vmem((points, columns), BF16), vmem((width, points), BF16), vmem((points, width), BF16),
        vmem(butterfly.shape, F32), vmem((width, width), F32),
        vmem(butterfly.shape, BF16), vmem(butterfly.shape, BF16),
        vmem((levels, 2 * width, width), BF16), vmem((levels, 2 * width, width), BF16),
        vmem((width, width), BF16), vmem((width, width), BF16),
        vmem((n_sub, slice_cols, width), F32), vmem((n_sub, slice_cols, width), F32),
        vmem((levels + 1, slice_cols, width), F32), vmem((slice_cols, width), F32),
        vmem((levels, slice_cols, width), BF16), vmem((levels, slice_cols, width), BF16),
        vmem((slice_cols, width), F32), vmem((slice_cols, width), F32),
        vmem((levels, slice_cols, width), BF16), vmem((levels, slice_cols, width), BF16),
        vmem((levels, slice_cols, width), F32),
        vmem((levels + 1, root_rows, width), F32), vmem((levels, root_rows, width), F32),
        vmem((levels, root_rows, width), F32), vmem((width, width), F32), vmem((width, width), F32),
        vmem((slice_cols, width), F32), vmem((n_plane, piece, width), F32),
        vmem((piece, width), F32), vmem((n_z, piece, width), F32), vmem((piece, width), F32),
        vmem((slice_cols, width), F32),
        vmem((columns, width), BF16), vmem((points, columns), F32),
        pltpu.SemaphoreType.DMA((7,)), pltpu.SemaphoreType.DMA((n_sub,)),
        pair(CHUNKS * n_sub), pair(levels * CHUNKS), pair(levels * CHUNKS), pair(levels), pair(n_sub), pair(n_sub),
        pair(n_plane), pair(n_z), pair(n_plane), pair(CHUNKS * n_sub),
    ]
    in_hbm = lambda array: pltpu.with_memory_space_constraint(array, pltpu.HBM)
    hbm = pl.BlockSpec(memory_space=pl.ANY)
    return pl.pallas_call(
        functools.partial(kernel, n_plane, n_z, n_sub, levels),
        out_shape=jax.ShapeDtypeStruct((points, columns), F32),
        in_specs=[hbm, hbm, pl.BlockSpec(memory_space=pltpu.SMEM), hbm, hbm, hbm],
        out_specs=pl.BlockSpec(memory_space=pl.ANY),
        scratch_shapes=scratch,
        compiler_params=pltpu.CompilerParams(
            collective_id=0, has_side_effects=True, vmem_limit_bytes=40 * 2**20),
    )(in_hbm(rhs_points), in_hbm(interp), skel_count, in_hbm(butterfly), in_hbm(project), in_hbm(root_inverse))


def solution(mesh):
    n_box, n_sub = mesh.shape["box"], mesh.shape["sub"]
    n_z = 8
    in_specs = (
        P(("box", "sub"), None),
        P(("box", "sub"), None),
        P("box"),
        P(None, "box", None),
        P("box", None),
        P(),
    )
    out_specs = P(("box", "sub"), None)
    return jax.shard_map(
        functools.partial(local, n_box // n_z, n_z, n_sub),
        mesh=mesh, in_specs=in_specs, out_specs=out_specs, check_vma=False)
```

```python
import functools

import jax
import jax.numpy as jnp
from jax import lax
from jax.experimental import pallas as pl
from jax.experimental.pallas import tpu as pltpu
from jax.sharding import PartitionSpec as P

F32 = jnp.float32
BF16 = jnp.bfloat16
MESH = pl.DeviceIdType.MESH
CHUNKS = 2
NN = (((1,), (0,)), ((), ()))
NT = (((1,), (1,)), ((), ()))


def halves(value):
    high = value.astype(BF16)
    return high, (value - high.astype(F32)).astype(BF16)


def dot(left, right, dims):
    return lax.dot_general(left, right, dims, preferred_element_type=F32)


def dot_split(value, high, low, dims):
    rows = value.shape[0]
    if value.dtype == BF16:
        return dot(value, high, dims) + dot(value, low, dims)
    value_high, value_low = halves(value)
    both = dot(jnp.concatenate([value_high, value_low], axis=0), high, dims)
    return both[:rows] + (both[rows:] + dot(value_high, low, dims))


def kernel(
    n_plane, n_z, n_sub, levels,
    rhs_hbm, interp_hbm, count_ref, butterfly_hbm, project_hbm, inverse_hbm, out,
    rhs, interp, interp_t, butterfly, inverse,
    weight_high, weight_low, turned_high, turned_low, inverse_high, inverse_low,
    leaf, leaf_in, far_out, far_in, up, up_wide_in, up_out, up_in, down_wide_out, down_wide_in, down_out, down_in, down,
    sweep, sweep_out, sweep_in, step_map, root_map,
    root_part, root_plane, root_mine, root_z, root_piece, root_all,
    back,
    load_sem, leaf_sem, up_sem, down_sem, sweep_sem, step_sem, map_sem, plane_sem, z_sem, spread_sem, back_sem,
):
    width = interp.shape[0]
    slice_cols = leaf.shape[1]
    chunk = slice_cols // CHUNKS
    root_rows = width // n_sub
    piece = slice_cols // n_plane

    box = lax.axis_index("box")
    x = lax.axis_index("sub")
    place = box % n_plane
    z = box // n_plane

    def at_x(k):
        return (box, (x + k) % n_sub)

    def at_place(k):
        return (z * n_plane + (place + k) % n_plane, x)

    def at_z(k):
        return (((z + k) % n_z) * n_plane + place, x)

    def sibling(level):
        bit = 2 ** level
        return (box + (1 - 2 * ((z // bit) % 2)) * bit * n_plane, x)

    def send(source, target, sems, index, device):
        copy = pltpu.make_async_remote_copy(
            src_ref=source, dst_ref=target, send_sem=sems.at[0, index], recv_sem=sems.at[1, index],
            device_id=device, device_id_type=MESH,
        )
        copy.start()
        started.append(copy)
        return copy

    started = []

    barrier = pltpu.get_barrier_semaphore()
    peers = ([at_x(k) for k in range(1, n_sub)] + [at_place(k) for k in range(1, n_plane)]
             + [at_z(k) for k in range(1, n_z)])
    for peer in peers:
        pl.semaphore_signal(barrier, inc=1, device_id=peer, device_id_type=MESH)

    my_rows = pl.ds(pl.multiple_of(x * root_rows, root_rows), root_rows)
    loads = []
    for source, target in (
        (interp_hbm, interp), (rhs_hbm, rhs), (project_hbm.at[my_rows], sweep.at[levels]),
        (butterfly_hbm.at[2], butterfly.at[2]), (butterfly_hbm.at[0], butterfly.at[0]),
        (butterfly_hbm.at[1], butterfly.at[1]), (inverse_hbm, inverse),
    ):
        load = pltpu.make_async_copy(source, target, load_sem.at[len(loads)])
        load.start()
        loads.append(load)

    leaf_order = sorted(range(n_sub), key=lambda k: (k == 0, -min(k, n_sub - k)))
    leaf_copies = {}

    across = n_sub // 2

    def leaf_send(j, k):
        rows = pl.ds(j * chunk, chunk)
        if k == across:
            source, target = far_out.at[rows], far_in.at[rows]
        else:
            source, target = leaf.at[k, rows], leaf_in.at[k, rows]
        leaf_copies[j, k] = send(source, target, leaf_sem, j * n_sub + k, at_x(k))

    loads[0].wait()
    loads[1].wait()
    pl.semaphore_wait(barrier, len(peers))
    interp_value = interp[...]
    for k in leaf_order:
        columns = pl.ds(pl.multiple_of(((x + k) % n_sub) * slice_cols, slice_cols), slice_cols)
        term = dot(rhs[:, columns].T, interp_value, NT)
        if k == across:
            far_out[...] = term.astype(BF16)
        else:
            leaf[k] = term
        if k:
            leaf_send(0, k)
    for j in range(1, CHUNKS):
        for k in leaf_order[:-1]:
            leaf_send(j, k)

    def split_level(level):
        high, low = halves(butterfly[level])
        weight_high[level] = high
        weight_low[level] = low

    def turn_level(level):
        turned_high[level] = weight_high[level].T
        turned_low[level] = weight_low[level].T

    def own(value, level):
        return dot_split(value, weight_high[level, :, :width], weight_low[level, :, :width], NN)

    def cross(value, level):
        return dot_split(value, weight_high[level, :, width:], weight_low[level, :, width:], NN)

    def own_turned(value, level):
        return dot_split(value, turned_high[level, :width], turned_low[level, :width], NN)

    def cross_turned(value, level):
        return dot_split(value, turned_high[level, width:], turned_low[level, width:], NN)

    sweep_copies = {}

    def sweep_send(level):
        sweep_out[level] = cross(sweep[level + 1], level)
        sweep_copies[level] = send(
            sweep_out.at[level], sweep_in.at[level], sweep_sem, level, sibling(level))
        sweep[level] = own(sweep[level + 1], level)

    def sweep_take(level):
        sweep_copies[level].wait_recv()
        sweep[level] = sweep[level] + sweep_in[level]
        if level > 0:
            sweep_send(level - 1)

    def gather(level, target, sems):
        target[my_rows] = sweep[level]
        return [send(sweep.at[level], target.at[my_rows], sems, k, at_x(k)) for k in range(1, n_sub)]

    loads[2].wait()
    loads[3].wait()
    split_level(2)
    sweep_send(levels - 1)
    for position, level in ((4, 0), (5, 1)):
        loads[position].wait()
        split_level(level)
        turn_level(level)
    turn_level(levels - 1)
    loads[6].wait()
    inverse_high[...], inverse_low[...] = halves(inverse[...].T)
    interp_t[...] = interp_value.T
    live = lax.broadcasted_iota(jnp.int32, (chunk, width), 1) < count_ref[0]

    up_copies = {}

    def rows_of(j):
        return pl.ds(j * chunk, chunk)

    def up_send(level, j):
        rows = rows_of(j)
        if level == 0:
            source, target = up.at[0, rows], up_wide_in.at[rows]
        else:
            up_out[level, rows] = up[level, rows].astype(BF16)
            source, target = up_out.at[level, rows], up_in.at[level, rows]
        up_copies[level, j] = send(source, target, up_sem, level * CHUNKS + j, sibling(level))

    def up_start(j):
        rows = rows_of(j)
        total = leaf[0, rows]
        for k in leaf_order[:-1][::-1]:
            leaf_copies[j, k].wait_recv()
            total = total + (far_in[rows].astype(F32) if k == across else leaf_in[k, rows])
        up[0, rows] = jnp.where(live, total, 0.0)
        up_send(0, j)

    def up_step(level, j):
        rows = rows_of(j)
        up_copies[level, j].wait_recv()
        arrived = up_in[level, rows] if level else up_wide_in[rows]
        up[level + 1, rows] = up[level + 1, rows] + cross_turned(arrived, level)
        if level + 1 < levels:
            up_send(level + 1, j)
        else:
            down_send(up[levels, rows], level, j)

    def up_own(level):
        up[level + 1] = own_turned(up[level], level)

    down_copies = {}

    def down_send(value, level, j):
        rows = rows_of(j)
        if level == 0:
            down_wide_out[rows] = cross(value, level)
            source, target = down_wide_out.at[rows], down_wide_in.at[rows]
        else:
            down_out[level, rows] = cross(value, level).astype(BF16)
            source, target = down_out.at[level, rows], down_in.at[level, rows]
        down_copies[level, j] = send(source, target, down_sem, level * CHUNKS + j, sibling(level))

    def down_value(level, j):
        rows = rows_of(j)
        down_copies[level, j].wait_recv()
        arrived = down_in[level, rows].astype(F32) if level else down_wide_in[rows]
        return down[level, rows] + arrived

    def down_step(level, j):
        value = down_value(level, j)
        down[level, rows_of(j)] = value
        down_send(value, level - 1, j)

    def every(step, level, part=range(CHUNKS)):
        for j in part:
            step(level, j)

    for j in range(CHUNKS):
        up_start(j)
    up_own(0)
    sweep_take(2)
    step_copies = gather(2, step_map, step_sem)
    every(up_step, 0)
    up_own(1)
    every(up_step, 1)

    for copy in step_copies:
        copy.wait_recv()
    step_high, step_low = halves(step_map[...].T)
    root_part[...] = dot_split(up[levels - 1], step_high, step_low, NN)

    def piece_of(k):
        return pl.ds(pl.multiple_of(((place + k) % n_plane) * piece, piece), piece)

    plane_copies = [
        send(root_part.at[piece_of(k)], root_plane.at[k], plane_sem, k, at_place(k)) for k in range(1, n_plane)]
    up_own(2)
    sweep_take(1)
    every(up_step, 2)
    total = root_part[piece_of(0)]
    for k, copy in enumerate(plane_copies, 1):
        copy.wait_recv()
        total = total + root_plane[k]
    root_mine[...] = total
    z_copies = [send(root_mine, root_z.at[k], z_sem, k, at_z(k)) for k in range(1, n_z)]
    down[2] = own(up[levels], 2)
    sweep_take(0)
    map_copies = gather(0, root_map, map_sem)
    every(down_step, 2, range(CHUNKS // 2))
    for k, copy in enumerate(z_copies, 1):
        copy.wait_recv()
        total = total + root_z[k]
    padded = jnp.concatenate([total, jnp.zeros_like(total)], axis=0)
    solved = dot_split(padded, inverse_high[...], inverse_low[...], NN)[:piece]
    root_piece[...] = solved
    root_all[piece_of(0)] = solved
    spread_copies = [
        send(root_piece, root_all.at[piece_of(0)], spread_sem, k, at_place(k)) for k in range(1, n_plane)]
    every(down_step, 2, range(CHUNKS // 2, CHUNKS))
    down[1] = own(down[2], 1)
    every(down_step, 1)
    down[0] = own(down[1], 0)
    for copy in map_copies:
        copy.wait_recv()
    map_high, map_low = halves(root_map[...])
    for copy in spread_copies:
        copy.wait_recv()
    root_term = dot_split(root_all[...], map_high, map_low, NN)

    back_copies = {}
    for j in range(CHUNKS):
        value = down_value(0, j) - root_term[j * chunk:(j + 1) * chunk]
        spot = pl.ds(pl.multiple_of(x * slice_cols + j * chunk, chunk), chunk)
        back[spot] = jnp.where(live, value, 0.0).astype(BF16)
        for k in leaf_order[:-1]:
            back_copies[j, k] = send(back.at[spot], back.at[spot], back_sem, j * n_sub + k, at_x(k))

    for k in (0, *leaf_order[:-1][::-1]):
        columns = pl.ds(pl.multiple_of(((x + n_sub - k) % n_sub) * slice_cols, slice_cols), slice_cols)
        if k:
            for j in range(CHUNKS):
                back_copies[j, k].wait_recv()
        out[:, columns] = rhs[:, columns].astype(F32) - dot(interp_t[...], back[columns], NT)

    for copy in started:
        copy.wait_send()


def local(n_plane, n_z, n_sub, rhs_points, interp, skel_count, butterfly, project, root_inverse):
    points, columns = rhs_points.shape
    width = interp.shape[0]
    levels = butterfly.shape[0]
    slice_cols = columns // n_sub
    piece = slice_cols // n_plane
    root_rows = width // n_sub
    vmem = pltpu.VMEM
    pair = lambda count: pltpu.SemaphoreType.DMA((2, count))
    scratch = [
        vmem((points, columns), BF16), vmem((width, points), BF16), vmem((points, width), BF16),
        vmem(butterfly.shape, F32), vmem((width, width), F32),
        vmem(butterfly.shape, BF16), vmem(butterfly.shape, BF16),
        vmem((levels, 2 * width, width), BF16), vmem((levels, 2 * width, width), BF16),
        vmem((width, width), BF16), vmem((width, width), BF16),
        vmem((n_sub, slice_cols, width), F32), vmem((n_sub, slice_cols, width), F32),
        vmem((slice_cols, width), BF16), vmem((slice_cols, width), BF16),
        vmem((levels + 1, slice_cols, width), F32), vmem((slice_cols, width), F32),
        vmem((levels, slice_cols, width), BF16), vmem((levels, slice_cols, width), BF16),
        vmem((slice_cols, width), F32), vmem((slice_cols, width), F32),
        vmem((levels, slice_cols, width), BF16), vmem((levels, slice_cols, width), BF16),
        vmem((levels, slice_cols, width), F32),
        vmem((levels + 1, root_rows, width), F32), vmem((levels, root_rows, width), F32),
        vmem((levels, root_rows, width), F32), vmem((width, width), F32), vmem((width, width), F32),
        vmem((slice_cols, width), F32), vmem((n_plane, piece, width), F32),
        vmem((piece, width), F32), vmem((n_z, piece, width), F32), vmem((piece, width), F32),
        vmem((slice_cols, width), F32),
        vmem((columns, width), BF16),
        pltpu.SemaphoreType.DMA((7,)),
        pair(CHUNKS * n_sub), pair(levels * CHUNKS), pair(levels * CHUNKS), pair(levels), pair(n_sub), pair(n_sub),
        pair(n_plane), pair(n_z), pair(n_plane), pair(CHUNKS * n_sub),
    ]
    in_hbm = lambda array: pltpu.with_memory_space_constraint(array, pltpu.HBM)
    hbm = pl.BlockSpec(memory_space=pl.ANY)
    return pl.pallas_call(
        functools.partial(kernel, n_plane, n_z, n_sub, levels),
        out_shape=pltpu.VMEM((points, columns), F32),
        in_specs=[hbm, hbm, pl.BlockSpec(memory_space=pltpu.SMEM), hbm, hbm, hbm],
        out_specs=pl.BlockSpec(memory_space=pltpu.VMEM),
        scratch_shapes=scratch,
        compiler_params=pltpu.CompilerParams(
            collective_id=0, has_side_effects=True, vmem_limit_bytes=40 * 2**20),
    )(in_hbm(rhs_points), in_hbm(interp), skel_count, in_hbm(butterfly), in_hbm(project), in_hbm(root_inverse))


def solution(mesh):
    n_box, n_sub = mesh.shape["box"], mesh.shape["sub"]
    n_z = 8
    in_specs = (
        P(("box", "sub"), None),
        P(("box", "sub"), None),
        P("box"),
        P(None, "box", None),
        P("box", None),
        P(),
    )
    out_specs = P(("box", "sub"), None)
    return jax.shard_map(
        functools.partial(local, n_box // n_z, n_z, n_sub),
        mesh=mesh, in_specs=in_specs, out_specs=out_specs, check_vma=False)
```

```python
import functools

import jax
import jax.numpy as jnp
from jax import lax
from jax.experimental import pallas as pl
from jax.experimental.pallas import tpu as pltpu
from jax.sharding import PartitionSpec as P

F32 = jnp.float32
BF16 = jnp.bfloat16
MESH = pl.DeviceIdType.MESH
CHUNKS = 2
NN = (((1,), (0,)), ((), ()))
NT = (((1,), (1,)), ((), ()))


def halves(value):
    high = value.astype(BF16)
    return high, (value - high.astype(F32)).astype(BF16)


def dot(left, right, dims):
    return lax.dot_general(left, right, dims, preferred_element_type=F32)


def dot_split(value, high, low, dims):
    rows = value.shape[0]
    if value.dtype == BF16:
        return dot(value, high, dims) + dot(value, low, dims)
    value_high, value_low = halves(value)
    both = dot(jnp.concatenate([value_high, value_low], axis=0), high, dims)
    return both[:rows] + (both[rows:] + dot(value_high, low, dims))


def kernel(
    n_plane, n_z, n_sub, levels,
    rhs_hbm, interp_hbm, count_ref, butterfly_hbm, project_hbm, inverse_hbm, out,
    rhs, interp, interp_t, butterfly, inverse,
    weight_high, weight_low, turned_high, turned_low, inverse_high, inverse_low,
    leaf, leaf_in, far_out, far_in, up, up_wide_in, up_out, up_in, down_wide_out, down_wide_in, down_out, down_in, down,
    sweep, sweep_out, sweep_in, step_map, root_map,
    root_part, root_plane, root_mine, root_z, root_piece, root_all,
    back,
    load_sem, leaf_sem, up_sem, down_sem, sweep_sem, step_sem, map_sem, plane_sem, z_sem, spread_sem, back_sem,
):
    width = interp.shape[0]
    slice_cols = leaf.shape[1]
    chunk = slice_cols // CHUNKS
    root_rows = width // n_sub
    piece = slice_cols // n_plane

    box = lax.axis_index("box")
    x = lax.axis_index("sub")
    place = box % n_plane
    z = box // n_plane

    def at_x(k):
        return (box, (x + k) % n_sub)

    def at_place(k):
        return (z * n_plane + (place + k) % n_plane, x)

    def at_z(k):
        return (((z + k) % n_z) * n_plane + place, x)

    def sibling(level):
        bit = 2 ** level
        return (box + (1 - 2 * ((z // bit) % 2)) * bit * n_plane, x)

    def send(source, target, sems, index, device):
        copy = pltpu.make_async_remote_copy(
            src_ref=source, dst_ref=target, send_sem=sems.at[0, index], recv_sem=sems.at[1, index],
            device_id=device, device_id_type=MESH,
        )
        copy.start()
        started.append(copy)
        return copy

    started = []

    my_rows = pl.ds(pl.multiple_of(x * root_rows, root_rows), root_rows)
    loads = []

    def load(source, target):
        copy = pltpu.make_async_copy(source, target, load_sem.at[len(loads)])
        copy.start()
        loads.append(copy)

    load(interp_hbm, interp)
    load(rhs_hbm, rhs)
    barrier = pltpu.get_barrier_semaphore()
    peers = ([at_x(k) for k in range(1, n_sub)] + [at_place(k) for k in range(1, n_plane)]
             + [at_z(k) for k in range(1, n_z)])
    for peer in peers:
        pl.semaphore_signal(barrier, inc=1, device_id=peer, device_id_type=MESH)
    load(project_hbm.at[my_rows], sweep.at[levels])
    for level in (2, 0, 1):
        load(butterfly_hbm.at[level], butterfly.at[level])
    load(inverse_hbm, inverse)

    leaf_order = sorted(range(n_sub), key=lambda k: (k == 0, -min(k, n_sub - k)))
    leaf_copies = {}

    across = n_sub // 2

    def leaf_send(j, k):
        rows = pl.ds(j * chunk, chunk)
        if k == across:
            source, target = far_out.at[rows], far_in.at[rows]
        else:
            source, target = leaf.at[k, rows], leaf_in.at[k, rows]
        leaf_copies[j, k] = send(source, target, leaf_sem, j * n_sub + k, at_x(k))

    loads[0].wait()
    loads[1].wait()
    interp_value = interp[...]
    for k in leaf_order:
        columns = pl.ds(pl.multiple_of(((x + k) % n_sub) * slice_cols, slice_cols), slice_cols)
        term = dot(rhs[:, columns].T, interp_value, NT)
        if k == across:
            far_out[...] = term.astype(BF16)
        else:
            leaf[k] = term
        if k == leaf_order[0]:
            pl.semaphore_wait(barrier, len(peers))
        if k:
            leaf_send(0, k)
    for j in range(1, CHUNKS):
        for k in leaf_order[:-1]:
            leaf_send(j, k)

    def split_level(level):
        high, low = halves(butterfly[level])
        weight_high[level] = high
        weight_low[level] = low

    def turn_level(level):
        turned_high[level] = weight_high[level].T
        turned_low[level] = weight_low[level].T

    def own(value, level):
        return dot_split(value, weight_high[level, :, :width], weight_low[level, :, :width], NN)

    def cross(value, level):
        return dot_split(value, weight_high[level, :, width:], weight_low[level, :, width:], NN)

    def own_turned(value, level):
        return dot_split(value, turned_high[level, :width], turned_low[level, :width], NN)

    def cross_turned(value, level):
        return dot_split(value, turned_high[level, width:], turned_low[level, width:], NN)

    sweep_copies = {}

    def sweep_send(level):
        sweep_out[level] = cross(sweep[level + 1], level)
        sweep_copies[level] = send(
            sweep_out.at[level], sweep_in.at[level], sweep_sem, level, sibling(level))
        sweep[level] = own(sweep[level + 1], level)

    def sweep_take(level):
        sweep_copies[level].wait_recv()
        sweep[level] = sweep[level] + sweep_in[level]
        if level > 0:
            sweep_send(level - 1)

    def gather(level, target, sems):
        target[my_rows] = sweep[level]
        return [send(sweep.at[level], target.at[my_rows], sems, k, at_x(k)) for k in range(1, n_sub)]

    loads[2].wait()
    loads[3].wait()
    split_level(2)
    sweep_send(levels - 1)
    live = lax.broadcasted_iota(jnp.int32, (chunk, width), 1) < count_ref[0]

    up_copies = {}

    def rows_of(j):
        return pl.ds(j * chunk, chunk)

    def up_send(level, j):
        rows = rows_of(j)
        if level == 0:
            source, target = up.at[0, rows], up_wide_in.at[rows]
        else:
            up_out[level, rows] = up[level, rows].astype(BF16)
            source, target = up_out.at[level, rows], up_in.at[level, rows]
        up_copies[level, j] = send(source, target, up_sem, level * CHUNKS + j, sibling(level))

    def up_start(j):
        rows = rows_of(j)
        total = leaf[0, rows]
        for k in leaf_order[:-1][::-1]:
            leaf_copies[j, k].wait_recv()
            total = total + (far_in[rows].astype(F32) if k == across else leaf_in[k, rows])
        up[0, rows] = jnp.where(live, total, 0.0)
        up_send(0, j)

    def up_step(level, j):
        rows = rows_of(j)
        up_copies[level, j].wait_recv()
        arrived = up_in[level, rows] if level else up_wide_in[rows]
        up[level + 1, rows] = up[level + 1, rows] + cross_turned(arrived, level)
        if level + 1 < levels:
            up_send(level + 1, j)
        else:
            down_send(up[levels, rows], level, j)

    def prepare(position, level):
        loads[position].wait()
        split_level(level)
        turn_level(level)

    def up_own(level):
        up[level + 1] = own_turned(up[level], level)

    down_copies = {}

    def down_send(value, level, j):
        rows = rows_of(j)
        if level == 0:
            down_wide_out[rows] = cross(value, level)
            source, target = down_wide_out.at[rows], down_wide_in.at[rows]
        else:
            down_out[level, rows] = cross(value, level).astype(BF16)
            source, target = down_out.at[level, rows], down_in.at[level, rows]
        down_copies[level, j] = send(source, target, down_sem, level * CHUNKS + j, sibling(level))

    def down_value(level, j):
        rows = rows_of(j)
        down_copies[level, j].wait_recv()
        arrived = down_in[level, rows].astype(F32) if level else down_wide_in[rows]
        return down[level, rows] + arrived

    def down_step(level, j):
        value = down_value(level, j)
        down[level, rows_of(j)] = value
        down_send(value, level - 1, j)

    def every(step, level, part=range(CHUNKS)):
        for j in part:
            step(level, j)

    for j in range(CHUNKS):
        up_start(j)
    prepare(4, 0)
    up_own(0)
    prepare(5, 1)
    sweep_take(2)
    step_copies = gather(2, step_map, step_sem)
    every(up_step, 0)
    up_own(1)
    turn_level(2)
    loads[6].wait()
    inverse_high[...], inverse_low[...] = halves(inverse[...].T)
    interp_t[...] = interp_value.T
    every(up_step, 1)

    for copy in step_copies:
        copy.wait_recv()
    step_high, step_low = halves(step_map[...].T)
    root_part[...] = dot_split(up[levels - 1], step_high, step_low, NN)

    def piece_of(k):
        return pl.ds(pl.multiple_of(((place + k) % n_plane) * piece, piece), piece)

    plane_copies = [
        send(root_part.at[piece_of(k)], root_plane.at[k], plane_sem, k, at_place(k)) for k in range(1, n_plane)]
    up_own(2)
    sweep_take(1)
    every(up_step, 2)
    total = root_part[piece_of(0)]
    for k, copy in enumerate(plane_copies, 1):
        copy.wait_recv()
        total = total + root_plane[k]
    root_mine[...] = total
    z_copies = [send(root_mine, root_z.at[k], z_sem, k, at_z(k)) for k in range(1, n_z)]
    down[2] = own(up[levels], 2)
    sweep_take(0)
    map_copies = gather(0, root_map, map_sem)
    every(down_step, 2, range(CHUNKS // 2))
    for k, copy in enumerate(z_copies, 1):
        copy.wait_recv()
        total = total + root_z[k]
    padded = jnp.concatenate([total, jnp.zeros_like(total)], axis=0)
    solved = dot_split(padded, inverse_high[...], inverse_low[...], NN)[:piece]
    root_piece[...] = solved
    root_all[piece_of(0)] = solved
    spread_copies = [
        send(root_piece, root_all.at[piece_of(0)], spread_sem, k, at_place(k)) for k in range(1, n_plane)]
    every(down_step, 2, range(CHUNKS // 2, CHUNKS))
    down[1] = own(down[2], 1)
    every(down_step, 1)
    down[0] = own(down[1], 0)
    for copy in map_copies:
        copy.wait_recv()
    map_high, map_low = halves(root_map[...])
    for copy in spread_copies:
        copy.wait_recv()
    root_term = dot_split(root_all[...], map_high, map_low, NN)

    back_copies = {}
    for j in range(CHUNKS):
        value = down_value(0, j) - root_term[j * chunk:(j + 1) * chunk]
        spot = pl.ds(pl.multiple_of(x * slice_cols + j * chunk, chunk), chunk)
        back[spot] = jnp.where(live, value, 0.0).astype(BF16)
        for k in leaf_order[:-1]:
            back_copies[j, k] = send(back.at[spot], back.at[spot], back_sem, j * n_sub + k, at_x(k))

    for k in (0, *leaf_order[:-1][::-1]):
        columns = pl.ds(pl.multiple_of(((x + n_sub - k) % n_sub) * slice_cols, slice_cols), slice_cols)
        if k:
            for j in range(CHUNKS):
                back_copies[j, k].wait_recv()
        out[:, columns] = rhs[:, columns].astype(F32) - dot(interp_t[...], back[columns], NT)

    for copy in started:
        copy.wait_send()


def local(n_plane, n_z, n_sub, rhs_points, interp, skel_count, butterfly, project, root_inverse):
    points, columns = rhs_points.shape
    width = interp.shape[0]
    levels = butterfly.shape[0]
    slice_cols = columns // n_sub
    piece = slice_cols // n_plane
    root_rows = width // n_sub
    vmem = pltpu.VMEM
    pair = lambda count: pltpu.SemaphoreType.DMA((2, count))
    scratch = [
        vmem((points, columns), BF16), vmem((width, points), BF16), vmem((points, width), BF16),
        vmem(butterfly.shape, F32), vmem((width, width), F32),
        vmem(butterfly.shape, BF16), vmem(butterfly.shape, BF16),
        vmem((levels, 2 * width, width), BF16), vmem((levels, 2 * width, width), BF16),
        vmem((width, width), BF16), vmem((width, width), BF16),
        vmem((n_sub, slice_cols, width), F32), vmem((n_sub, slice_cols, width), F32),
        vmem((slice_cols, width), BF16), vmem((slice_cols, width), BF16),
        vmem((levels + 1, slice_cols, width), F32), vmem((slice_cols, width), F32),
        vmem((levels, slice_cols, width), BF16), vmem((levels, slice_cols, width), BF16),
        vmem((slice_cols, width), F32), vmem((slice_cols, width), F32),
        vmem((levels, slice_cols, width), BF16), vmem((levels, slice_cols, width), BF16),
        vmem((levels, slice_cols, width), F32),
        vmem((levels + 1, root_rows, width), F32), vmem((levels, root_rows, width), F32),
        vmem((levels, root_rows, width), F32), vmem((width, width), F32), vmem((width, width), F32),
        vmem((slice_cols, width), F32), vmem((n_plane, piece, width), F32),
        vmem((piece, width), F32), vmem((n_z, piece, width), F32), vmem((piece, width), F32),
        vmem((slice_cols, width), F32),
        vmem((columns, width), BF16),
        pltpu.SemaphoreType.DMA((7,)),
        pair(CHUNKS * n_sub), pair(levels * CHUNKS), pair(levels * CHUNKS), pair(levels), pair(n_sub), pair(n_sub),
        pair(n_plane), pair(n_z), pair(n_plane), pair(CHUNKS * n_sub),
    ]
    in_hbm = lambda array: pltpu.with_memory_space_constraint(array, pltpu.HBM)
    hbm = pl.BlockSpec(memory_space=pl.ANY)
    return pl.pallas_call(
        functools.partial(kernel, n_plane, n_z, n_sub, levels),
        out_shape=pltpu.VMEM((points, columns), F32),
        in_specs=[hbm, hbm, pl.BlockSpec(memory_space=pltpu.SMEM), hbm, hbm, hbm],
        out_specs=pl.BlockSpec(memory_space=pltpu.VMEM),
        scratch_shapes=scratch,
        compiler_params=pltpu.CompilerParams(
            collective_id=0, has_side_effects=True, vmem_limit_bytes=40 * 2**20),
    )(in_hbm(rhs_points), in_hbm(interp), skel_count, in_hbm(butterfly), in_hbm(project), in_hbm(root_inverse))


def solution(mesh):
    n_box, n_sub = mesh.shape["box"], mesh.shape["sub"]
    n_z = 8
    in_specs = (
        P(("box", "sub"), None),
        P(("box", "sub"), None),
        P("box"),
        P(None, "box", None),
        P("box", None),
        P(),
    )
    out_specs = P(("box", "sub"), None)
    return jax.shard_map(
        functools.partial(local, n_box // n_z, n_z, n_sub),
        mesh=mesh, in_specs=in_specs, out_specs=out_specs, check_vma=False)
```

```python
import functools

import jax
import jax.numpy as jnp
from jax import lax
from jax.experimental import pallas as pl
from jax.experimental.pallas import tpu as pltpu
from jax.sharding import PartitionSpec as P

F32 = jnp.float32
BF16 = jnp.bfloat16
MESH = pl.DeviceIdType.MESH
CHUNKS = 2
NN = (((1,), (0,)), ((), ()))
NT = (((1,), (1,)), ((), ()))


def halves(value):
    high = value.astype(BF16)
    return high, (value - high.astype(F32)).astype(BF16)


def dot(left, right, dims):
    return lax.dot_general(left, right, dims, preferred_element_type=F32)


def dot_split(value, high, low, dims):
    rows = value.shape[0]
    if value.dtype == BF16:
        return dot(value, high, dims) + dot(value, low, dims)
    value_high, value_low = halves(value)
    both = dot(jnp.concatenate([value_high, value_low], axis=0), high, dims)
    return both[:rows] + (both[rows:] + dot(value_high, low, dims))


def kernel(
    n_plane, n_z, n_sub, levels,
    rhs_hbm, interp_hbm, count_ref, butterfly_hbm, project_hbm, inverse_hbm, out,
    rhs, interp, interp_t, butterfly, inverse,
    weight_high, weight_low, turned_high, turned_low, inverse_high, inverse_low,
    leaf, leaf_in, far_out, far_in, up, up_wide_in, up_out, up_in, down_wide_out, down_wide_in, down_out, down_in, down,
    sweep, sweep_out, sweep_in, step_map, root_map,
    root_part, root_plane, root_mine, root_z, root_piece, root_all,
    back,
    load_sem, leaf_sem, up_sem, down_sem, sweep_sem, step_sem, map_sem, plane_sem, z_sem, spread_sem, back_sem,
):
    width = interp.shape[0]
    slice_cols = leaf.shape[1]
    chunk = slice_cols // CHUNKS
    root_rows = width // n_sub
    piece = slice_cols // n_plane

    box = lax.axis_index("box")
    x = lax.axis_index("sub")
    place = box % n_plane
    z = box // n_plane

    def at_x(k):
        return (box, (x + k) % n_sub)

    def at_place(k):
        return (z * n_plane + (place + k) % n_plane, x)

    def at_z(k):
        return (((z + k) % n_z) * n_plane + place, x)

    def sibling(level):
        bit = 2 ** level
        return (box + (1 - 2 * ((z // bit) % 2)) * bit * n_plane, x)

    def send(source, target, sems, index, device):
        copy = pltpu.make_async_remote_copy(
            src_ref=source, dst_ref=target, send_sem=sems.at[0, index], recv_sem=sems.at[1, index],
            device_id=device, device_id_type=MESH,
        )
        copy.start()
        started.append(copy)
        return copy

    started = []

    barrier = pltpu.get_barrier_semaphore()
    peers = ([at_x(k) for k in range(1, n_sub)] + [at_place(k) for k in range(1, n_plane)]
             + [at_z(k) for k in range(1, n_z)])
    for peer in peers:
        pl.semaphore_signal(barrier, inc=1, device_id=peer, device_id_type=MESH)

    my_rows = pl.ds(pl.multiple_of(x * root_rows, root_rows), root_rows)
    loads = []
    for source, target in (
        (interp_hbm, interp), (rhs_hbm, rhs), (project_hbm.at[my_rows], sweep.at[levels]),
        (butterfly_hbm.at[2], butterfly.at[2]), (butterfly_hbm.at[0], butterfly.at[0]),
        (butterfly_hbm.at[1], butterfly.at[1]), (inverse_hbm, inverse),
    ):
        load = pltpu.make_async_copy(source, target, load_sem.at[len(loads)])
        load.start()
        loads.append(load)

    leaf_order = sorted(range(n_sub), key=lambda k: (k == 0, -min(k, n_sub - k)))
    leaf_copies = {}

    across = n_sub // 2

    def leaf_send(j, k):
        rows = pl.ds(j * chunk, chunk)
        if k == across:
            source, target = far_out.at[rows], far_in.at[rows]
        else:
            source, target = leaf.at[k, rows], leaf_in.at[k, rows]
        leaf_copies[j, k] = send(source, target, leaf_sem, j * n_sub + k, at_x(k))

    loads[0].wait()
    loads[1].wait()
    pl.semaphore_wait(barrier, len(peers))
    interp_value = interp[...]
    for k in leaf_order:
        columns = pl.ds(pl.multiple_of(((x + k) % n_sub) * slice_cols, slice_cols), slice_cols)
        term = dot(rhs[:, columns].T, interp_value, NT)
        if k == across:
            far_out[...] = term.astype(BF16)
        else:
            leaf[k] = term
        if k:
            leaf_send(0, k)
    for j in range(1, CHUNKS):
        for k in leaf_order[:-1]:
            leaf_send(j, k)

    def split_level(level):
        high, low = halves(butterfly[level])
        weight_high[level] = high
        weight_low[level] = low

    def turn_level(level):
        turned_high[level] = weight_high[level].T
        turned_low[level] = weight_low[level].T

    def own(value, level):
        return dot_split(value, weight_high[level, :, :width], weight_low[level, :, :width], NN)

    def cross(value, level):
        return dot_split(value, weight_high[level, :, width:], weight_low[level, :, width:], NN)

    def own_turned(value, level):
        return dot_split(value, turned_high[level, :width], turned_low[level, :width], NN)

    def cross_turned(value, level):
        return dot_split(value, turned_high[level, width:], turned_low[level, width:], NN)

    sweep_copies = {}

    def sweep_send(level):
        sweep_out[level] = cross(sweep[level + 1], level)
        sweep_copies[level] = send(
            sweep_out.at[level], sweep_in.at[level], sweep_sem, level, sibling(level))
        sweep[level] = own(sweep[level + 1], level)

    def sweep_take(level):
        sweep_copies[level].wait_recv()
        sweep[level] = sweep[level] + sweep_in[level]
        if level > 0:
            sweep_send(level - 1)

    def gather(level, target, sems):
        target[my_rows] = sweep[level]
        return [send(sweep.at[level], target.at[my_rows], sems, k, at_x(k)) for k in range(1, n_sub)]

    loads[2].wait()
    loads[3].wait()
    split_level(2)
    sweep_send(levels - 1)
    for position, level in ((4, 0), (5, 1)):
        loads[position].wait()
        split_level(level)
        turn_level(level)
    turn_level(levels - 1)
    loads[6].wait()
    inverse_high[...], inverse_low[...] = halves(inverse[...].T)
    interp_t[...] = interp_value.T
    live = lax.broadcasted_iota(jnp.int32, (chunk, width), 1) < count_ref[0]

    up_copies = {}

    def rows_of(j):
        return pl.ds(j * chunk, chunk)

    def up_send(level, j):
        rows = rows_of(j)
        if level == 0:
            source, target = up.at[0, rows], up_wide_in.at[rows]
        else:
            up_out[level, rows] = up[level, rows].astype(BF16)
            source, target = up_out.at[level, rows], up_in.at[level, rows]
        up_copies[level, j] = send(source, target, up_sem, level * CHUNKS + j, sibling(level))

    def up_start(j):
        rows = rows_of(j)
        total = leaf[0, rows]
        for k in leaf_order[:-1][::-1]:
            leaf_copies[j, k].wait_recv()
            total = total + (far_in[rows].astype(F32) if k == across else leaf_in[k, rows])
        up[0, rows] = jnp.where(live, total, 0.0)
        up_send(0, j)

    def up_step(level, j):
        rows = rows_of(j)
        up_copies[level, j].wait_recv()
        arrived = up_in[level, rows] if level else up_wide_in[rows]
        up[level + 1, rows] = up[level + 1, rows] + cross_turned(arrived, level)
        if level + 1 < levels:
            up_send(level + 1, j)
        else:
            down_send(up[levels, rows], level, j)

    def up_own(level):
        up[level + 1] = own_turned(up[level], level)

    down_copies = {}

    def down_send(value, level, j):
        rows = rows_of(j)
        if level == 0:
            down_wide_out[rows] = cross(value, level)
            source, target = down_wide_out.at[rows], down_wide_in.at[rows]
        else:
            down_out[level, rows] = cross(value, level).astype(BF16)
            source, target = down_out.at[level, rows], down_in.at[level, rows]
        down_copies[level, j] = send(source, target, down_sem, level * CHUNKS + j, sibling(level))

    def down_value(level, j):
        rows = rows_of(j)
        down_copies[level, j].wait_recv()
        arrived = down_in[level, rows].astype(F32) if level else down_wide_in[rows]
        return down[level, rows] + arrived

    def down_step(level, j):
        value = down_value(level, j)
        down[level, rows_of(j)] = value
        down_send(value, level - 1, j)

    def every(step, level, part=range(CHUNKS)):
        for j in part:
            step(level, j)

    for j in range(CHUNKS):
        up_start(j)
    up_own(0)
    sweep_take(2)
    step_copies = gather(2, step_map, step_sem)
    every(up_step, 0)
    up_own(1)
    every(up_step, 1)

    for copy in step_copies:
        copy.wait_recv()
    step_high, step_low = halves(step_map[...].T)
    root_part[...] = dot_split(up[levels - 1], step_high, step_low, NN)

    def piece_of(k):
        return pl.ds(pl.multiple_of(((place + k) % n_plane) * piece, piece), piece)

    plane_copies = [
        send(root_part.at[piece_of(k)], root_plane.at[k], plane_sem, k, at_place(k)) for k in range(1, n_plane)]
    up_own(2)
    sweep_take(1)
    total = root_part[piece_of(0)]
    for k, copy in enumerate(plane_copies, 1):
        copy.wait_recv()
        total = total + root_plane[k]
    root_mine[...] = total
    z_copies = [send(root_mine, root_z.at[k], z_sem, k, at_z(k)) for k in range(1, n_z)]
    every(up_step, 2)
    down[2] = own(up[levels], 2)
    sweep_take(0)
    map_copies = gather(0, root_map, map_sem)
    every(down_step, 2, range(CHUNKS // 2))
    for k, copy in enumerate(z_copies, 1):
        copy.wait_recv()
        total = total + root_z[k]
    padded = jnp.concatenate([total, jnp.zeros_like(total)], axis=0)
    solved = dot_split(padded, inverse_high[...], inverse_low[...], NN)[:piece]
    root_piece[...] = solved
    root_all[piece_of(0)] = solved
    spread_copies = [
        send(root_piece, root_all.at[piece_of(0)], spread_sem, k, at_place(k)) for k in range(1, n_plane)]
    every(down_step, 2, range(CHUNKS // 2, CHUNKS))
    down[1] = own(down[2], 1)
    every(down_step, 1)
    down[0] = own(down[1], 0)
    for copy in map_copies:
        copy.wait_recv()
    map_high, map_low = halves(root_map[...])
    for copy in spread_copies:
        copy.wait_recv()
    root_term = dot_split(root_all[...], map_high, map_low, NN)

    back_copies = {}
    for j in range(CHUNKS):
        value = down_value(0, j) - root_term[j * chunk:(j + 1) * chunk]
        spot = pl.ds(pl.multiple_of(x * slice_cols + j * chunk, chunk), chunk)
        back[spot] = jnp.where(live, value, 0.0).astype(BF16)
        for k in leaf_order[:-1]:
            back_copies[j, k] = send(back.at[spot], back.at[spot], back_sem, j * n_sub + k, at_x(k))

    for k in (0, *leaf_order[:-1][::-1]):
        columns = pl.ds(pl.multiple_of(((x + n_sub - k) % n_sub) * slice_cols, slice_cols), slice_cols)
        if k:
            for j in range(CHUNKS):
                back_copies[j, k].wait_recv()
        out[:, columns] = rhs[:, columns].astype(F32) - dot(interp_t[...], back[columns], NT)

    for copy in started:
        copy.wait_send()


def local(n_plane, n_z, n_sub, rhs_points, interp, skel_count, butterfly, project, root_inverse):
    points, columns = rhs_points.shape
    width = interp.shape[0]
    levels = butterfly.shape[0]
    slice_cols = columns // n_sub
    piece = slice_cols // n_plane
    root_rows = width // n_sub
    vmem = pltpu.VMEM
    pair = lambda count: pltpu.SemaphoreType.DMA((2, count))
    scratch = [
        vmem((points, columns), BF16), vmem((width, points), BF16), vmem((points, width), BF16),
        vmem(butterfly.shape, F32), vmem((width, width), F32),
        vmem(butterfly.shape, BF16), vmem(butterfly.shape, BF16),
        vmem((levels, 2 * width, width), BF16), vmem((levels, 2 * width, width), BF16),
        vmem((width, width), BF16), vmem((width, width), BF16),
        vmem((n_sub, slice_cols, width), F32), vmem((n_sub, slice_cols, width), F32),
        vmem((slice_cols, width), BF16), vmem((slice_cols, width), BF16),
        vmem((levels + 1, slice_cols, width), F32), vmem((slice_cols, width), F32),
        vmem((levels, slice_cols, width), BF16), vmem((levels, slice_cols, width), BF16),
        vmem((slice_cols, width), F32), vmem((slice_cols, width), F32),
        vmem((levels, slice_cols, width), BF16), vmem((levels, slice_cols, width), BF16),
        vmem((levels, slice_cols, width), F32),
        vmem((levels + 1, root_rows, width), F32), vmem((levels, root_rows, width), F32),
        vmem((levels, root_rows, width), F32), vmem((width, width), F32), vmem((width, width), F32),
        vmem((slice_cols, width), F32), vmem((n_plane, piece, width), F32),
        vmem((piece, width), F32), vmem((n_z, piece, width), F32), vmem((piece, width), F32),
        vmem((slice_cols, width), F32),
        vmem((columns, width), BF16),
        pltpu.SemaphoreType.DMA((7,)),
        pair(CHUNKS * n_sub), pair(levels * CHUNKS), pair(levels * CHUNKS), pair(levels), pair(n_sub), pair(n_sub),
        pair(n_plane), pair(n_z), pair(n_plane), pair(CHUNKS * n_sub),
    ]
    in_hbm = lambda array: pltpu.with_memory_space_constraint(array, pltpu.HBM)
    hbm = pl.BlockSpec(memory_space=pl.ANY)
    return pl.pallas_call(
        functools.partial(kernel, n_plane, n_z, n_sub, levels),
        out_shape=pltpu.VMEM((points, columns), F32),
        in_specs=[hbm, hbm, pl.BlockSpec(memory_space=pltpu.SMEM), hbm, hbm, hbm],
        out_specs=pl.BlockSpec(memory_space=pltpu.VMEM),
        scratch_shapes=scratch,
        compiler_params=pltpu.CompilerParams(
            collective_id=0, has_side_effects=True, vmem_limit_bytes=40 * 2**20),
    )(in_hbm(rhs_points), in_hbm(interp), skel_count, in_hbm(butterfly), in_hbm(project), in_hbm(root_inverse))


def solution(mesh):
    n_box, n_sub = mesh.shape["box"], mesh.shape["sub"]
    n_z = 8
    in_specs = (
        P(("box", "sub"), None),
        P(("box", "sub"), None),
        P("box"),
        P(None, "box", None),
        P("box", None),
        P(),
    )
    out_specs = P(("box", "sub"), None)
    return jax.shard_map(
        functools.partial(local, n_box // n_z, n_z, n_sub),
        mesh=mesh, in_specs=in_specs, out_specs=out_specs, check_vma=False)
```

```python
import functools

import jax
import jax.numpy as jnp
from jax import lax
from jax.experimental import pallas as pl
from jax.experimental.pallas import tpu as pltpu
from jax.sharding import PartitionSpec as P

F32 = jnp.float32
BF16 = jnp.bfloat16
MESH = pl.DeviceIdType.MESH
CHUNKS = 4
NN = (((1,), (0,)), ((), ()))
NT = (((1,), (1,)), ((), ()))


def halves(value):
    high = value.astype(BF16)
    return high, (value - high.astype(F32)).astype(BF16)


def dot(left, right, dims):
    return lax.dot_general(left, right, dims, preferred_element_type=F32)


def dot_split(value, high, low, dims):
    rows = value.shape[0]
    if value.dtype == BF16:
        return dot(value, high, dims) + dot(value, low, dims)
    value_high, value_low = halves(value)
    both = dot(jnp.concatenate([value_high, value_low], axis=0), high, dims)
    return both[:rows] + (both[rows:] + dot(value_high, low, dims))


def kernel(
    n_plane, n_z, n_sub, levels,
    rhs_hbm, interp_hbm, count_ref, butterfly_hbm, project_hbm, inverse_hbm, out,
    rhs, interp, interp_t, butterfly, inverse,
    weight_high, weight_low, turned_high, turned_low, inverse_high, inverse_low,
    leaf, leaf_in, far_out, far_in, up, up_wide_in, up_out, up_in, down_wide_out, down_wide_in, down_out, down_in, down,
    sweep, sweep_out, sweep_in, step_map, root_map,
    root_part, root_plane, root_mine, root_z, root_piece, root_all,
    back,
    load_sem, leaf_sem, up_sem, down_sem, sweep_sem, step_sem, map_sem, plane_sem, z_sem, spread_sem, back_sem,
):
    width = interp.shape[0]
    slice_cols = leaf.shape[1]
    chunk = slice_cols // CHUNKS
    root_rows = width // n_sub
    piece = slice_cols // n_plane

    box = lax.axis_index("box")
    x = lax.axis_index("sub")
    place = box % n_plane
    z = box // n_plane

    def at_x(k):
        return (box, (x + k) % n_sub)

    def at_place(k):
        return (z * n_plane + (place + k) % n_plane, x)

    def at_z(k):
        return (((z + k) % n_z) * n_plane + place, x)

    def sibling(level):
        bit = 2 ** level
        return (box + (1 - 2 * ((z // bit) % 2)) * bit * n_plane, x)

    def send(source, target, sems, index, device):
        copy = pltpu.make_async_remote_copy(
            src_ref=source, dst_ref=target, send_sem=sems.at[0, index], recv_sem=sems.at[1, index],
            device_id=device, device_id_type=MESH,
        )
        copy.start()
        started.append(copy)
        return copy

    started = []

    barrier = pltpu.get_barrier_semaphore()
    peers = ([at_x(k) for k in range(1, n_sub)] + [at_place(k) for k in range(1, n_plane)]
             + [at_z(k) for k in range(1, n_z)])
    for peer in peers:
        pl.semaphore_signal(barrier, inc=1, device_id=peer, device_id_type=MESH)

    my_rows = pl.ds(pl.multiple_of(x * root_rows, root_rows), root_rows)
    loads = []
    for source, target in (
        (interp_hbm, interp), (rhs_hbm, rhs), (project_hbm.at[my_rows], sweep.at[levels]),
        (butterfly_hbm.at[2], butterfly.at[2]), (butterfly_hbm.at[0], butterfly.at[0]),
        (butterfly_hbm.at[1], butterfly.at[1]), (inverse_hbm, inverse),
    ):
        load = pltpu.make_async_copy(source, target, load_sem.at[len(loads)])
        load.start()
        loads.append(load)

    leaf_order = sorted(range(n_sub), key=lambda k: (k == 0, -min(k, n_sub - k)))
    leaf_copies = {}

    across = n_sub // 2

    def leaf_send(j, k):
        rows = pl.ds(j * chunk, chunk)
        if k == across:
            source, target = far_out.at[rows], far_in.at[rows]
        else:
            source, target = leaf.at[k, rows], leaf_in.at[k, rows]
        leaf_copies[j, k] = send(source, target, leaf_sem, j * n_sub + k, at_x(k))

    loads[0].wait()
    loads[1].wait()
    pl.semaphore_wait(barrier, len(peers))
    interp_value = interp[...]
    for k in leaf_order:
        columns = pl.ds(pl.multiple_of(((x + k) % n_sub) * slice_cols, slice_cols), slice_cols)
        term = dot(rhs[:, columns].T, interp_value, NT)
        if k == across:
            far_out[...] = term.astype(BF16)
        else:
            leaf[k] = term
        if k:
            leaf_send(0, k)
    for j in range(1, CHUNKS):
        for k in leaf_order[:-1]:
            leaf_send(j, k)

    def split_level(level):
        high, low = halves(butterfly[level])
        weight_high[level] = high
        weight_low[level] = low

    def turn_level(level):
        turned_high[level] = weight_high[level].T
        turned_low[level] = weight_low[level].T

    def own(value, level):
        return dot_split(value, weight_high[level, :, :width], weight_low[level, :, :width], NN)

    def cross(value, level):
        return dot_split(value, weight_high[level, :, width:], weight_low[level, :, width:], NN)

    def own_turned(value, level):
        return dot_split(value, turned_high[level, :width], turned_low[level, :width], NN)

    def cross_turned(value, level):
        return dot_split(value, turned_high[level, width:], turned_low[level, width:], NN)

    sweep_copies = {}

    def sweep_send(level):
        sweep_out[level] = cross(sweep[level + 1], level)
        sweep_copies[level] = send(
            sweep_out.at[level], sweep_in.at[level], sweep_sem, level, sibling(level))
        sweep[level] = own(sweep[level + 1], level)

    def sweep_take(level):
        sweep_copies[level].wait_recv()
        sweep[level] = sweep[level] + sweep_in[level]
        if level > 0:
            sweep_send(level - 1)

    def gather(level, target, sems):
        target[my_rows] = sweep[level]
        return [send(sweep.at[level], target.at[my_rows], sems, k, at_x(k)) for k in range(1, n_sub)]

    loads[2].wait()
    loads[3].wait()
    split_level(2)
    sweep_send(levels - 1)
    for position, level in ((4, 0), (5, 1)):
        loads[position].wait()
        split_level(level)
        turn_level(level)
    turn_level(levels - 1)
    loads[6].wait()
    inverse_high[...], inverse_low[...] = halves(inverse[...].T)
    interp_t[...] = interp_value.T
    live = lax.broadcasted_iota(jnp.int32, (chunk, width), 1) < count_ref[0]

    up_copies = {}

    def rows_of(j):
        return pl.ds(j * chunk, chunk)

    def up_send(level, j):
        rows = rows_of(j)
        if level == 0:
            source, target = up.at[0, rows], up_wide_in.at[rows]
        else:
            up_out[level, rows] = up[level, rows].astype(BF16)
            source, target = up_out.at[level, rows], up_in.at[level, rows]
        up_copies[level, j] = send(source, target, up_sem, level * CHUNKS + j, sibling(level))

    def up_start(j):
        rows = rows_of(j)
        total = leaf[0, rows]
        for k in leaf_order[:-1][::-1]:
            leaf_copies[j, k].wait_recv()
            total = total + (far_in[rows].astype(F32) if k == across else leaf_in[k, rows])
        up[0, rows] = jnp.where(live, total, 0.0)
        up_send(0, j)

    def up_step(level, j):
        rows = rows_of(j)
        up_copies[level, j].wait_recv()
        arrived = up_in[level, rows] if level else up_wide_in[rows]
        up[level + 1, rows] = up[level + 1, rows] + cross_turned(arrived, level)
        if level + 1 < levels:
            up_send(level + 1, j)
        else:
            down_send(up[levels, rows], level, j)

    def up_own(level):
        up[level + 1] = own_turned(up[level], level)

    down_copies = {}

    def down_send(value, level, j):
        rows = rows_of(j)
        if level == 0:
            down_wide_out[rows] = cross(value, level)
            source, target = down_wide_out.at[rows], down_wide_in.at[rows]
        else:
            down_out[level, rows] = cross(value, level).astype(BF16)
            source, target = down_out.at[level, rows], down_in.at[level, rows]
        down_copies[level, j] = send(source, target, down_sem, level * CHUNKS + j, sibling(level))

    def down_value(level, j):
        rows = rows_of(j)
        down_copies[level, j].wait_recv()
        arrived = down_in[level, rows].astype(F32) if level else down_wide_in[rows]
        return down[level, rows] + arrived

    def down_step(level, j):
        value = down_value(level, j)
        down[level, rows_of(j)] = value
        down_send(value, level - 1, j)

    def every(step, level, part=range(CHUNKS)):
        for j in part:
            step(level, j)

    for j in range(CHUNKS):
        up_start(j)
    up_own(0)
    sweep_take(2)
    step_copies = gather(2, step_map, step_sem)
    every(up_step, 0)
    up_own(1)
    every(up_step, 1)

    for copy in step_copies:
        copy.wait_recv()
    step_high, step_low = halves(step_map[...].T)
    root_part[...] = dot_split(up[levels - 1], step_high, step_low, NN)

    def piece_of(k):
        return pl.ds(pl.multiple_of(((place + k) % n_plane) * piece, piece), piece)

    plane_copies = [
        send(root_part.at[piece_of(k)], root_plane.at[k], plane_sem, k, at_place(k)) for k in range(1, n_plane)]
    up_own(2)
    sweep_take(1)
    every(up_step, 2)
    total = root_part[piece_of(0)]
    for k, copy in enumerate(plane_copies, 1):
        copy.wait_recv()
        total = total + root_plane[k]
    root_mine[...] = total
    z_copies = [send(root_mine, root_z.at[k], z_sem, k, at_z(k)) for k in range(1, n_z)]
    down[2] = own(up[levels], 2)
    sweep_take(0)
    map_copies = gather(0, root_map, map_sem)
    every(down_step, 2, range(CHUNKS // 2))
    for k, copy in enumerate(z_copies, 1):
        copy.wait_recv()
        total = total + root_z[k]
    padded = jnp.concatenate([total, jnp.zeros_like(total)], axis=0)
    solved = dot_split(padded, inverse_high[...], inverse_low[...], NN)[:piece]
    root_piece[...] = solved
    root_all[piece_of(0)] = solved
    spread_copies = [
        send(root_piece, root_all.at[piece_of(0)], spread_sem, k, at_place(k)) for k in range(1, n_plane)]
    every(down_step, 2, range(CHUNKS // 2, CHUNKS))
    down[1] = own(down[2], 1)
    every(down_step, 1)
    down[0] = own(down[1], 0)
    for copy in map_copies:
        copy.wait_recv()
    map_high, map_low = halves(root_map[...])
    for copy in spread_copies:
        copy.wait_recv()
    root_term = dot_split(root_all[...], map_high, map_low, NN)

    back_copies = {}
    for j in range(CHUNKS):
        value = down_value(0, j) - root_term[j * chunk:(j + 1) * chunk]
        spot = pl.ds(pl.multiple_of(x * slice_cols + j * chunk, chunk), chunk)
        back[spot] = jnp.where(live, value, 0.0).astype(BF16)
        for k in leaf_order[:-1]:
            back_copies[j, k] = send(back.at[spot], back.at[spot], back_sem, j * n_sub + k, at_x(k))

    for k in (0, *leaf_order[:-1][::-1]):
        columns = pl.ds(pl.multiple_of(((x + n_sub - k) % n_sub) * slice_cols, slice_cols), slice_cols)
        if k:
            for j in range(CHUNKS):
                back_copies[j, k].wait_recv()
        out[:, columns] = rhs[:, columns].astype(F32) - dot(interp_t[...], back[columns], NT)

    for copy in started:
        copy.wait_send()


def local(n_plane, n_z, n_sub, rhs_points, interp, skel_count, butterfly, project, root_inverse):
    points, columns = rhs_points.shape
    width = interp.shape[0]
    levels = butterfly.shape[0]
    slice_cols = columns // n_sub
    piece = slice_cols // n_plane
    root_rows = width // n_sub
    vmem = pltpu.VMEM
    pair = lambda count: pltpu.SemaphoreType.DMA((2, count))
    scratch = [
        vmem((points, columns), BF16), vmem((width, points), BF16), vmem((points, width), BF16),
        vmem(butterfly.shape, F32), vmem((width, width), F32),
        vmem(butterfly.shape, BF16), vmem(butterfly.shape, BF16),
        vmem((levels, 2 * width, width), BF16), vmem((levels, 2 * width, width), BF16),
        vmem((width, width), BF16), vmem((width, width), BF16),
        vmem((n_sub, slice_cols, width), F32), vmem((n_sub, slice_cols, width), F32),
        vmem((slice_cols, width), BF16), vmem((slice_cols, width), BF16),
        vmem((levels + 1, slice_cols, width), F32), vmem((slice_cols, width), F32),
        vmem((levels, slice_cols, width), BF16), vmem((levels, slice_cols, width), BF16),
        vmem((slice_cols, width), F32), vmem((slice_cols, width), F32),
        vmem((levels, slice_cols, width), BF16), vmem((levels, slice_cols, width), BF16),
        vmem((levels, slice_cols, width), F32),
        vmem((levels + 1, root_rows, width), F32), vmem((levels, root_rows, width), F32),
        vmem((levels, root_rows, width), F32), vmem((width, width), F32), vmem((width, width), F32),
        vmem((slice_cols, width), F32), vmem((n_plane, piece, width), F32),
        vmem((piece, width), F32), vmem((n_z, piece, width), F32), vmem((piece, width), F32),
        vmem((slice_cols, width), F32),
        vmem((columns, width), BF16),
        pltpu.SemaphoreType.DMA((7,)),
        pair(CHUNKS * n_sub), pair(levels * CHUNKS), pair(levels * CHUNKS), pair(levels), pair(n_sub), pair(n_sub),
        pair(n_plane), pair(n_z), pair(n_plane), pair(CHUNKS * n_sub),
    ]
    in_hbm = lambda array: pltpu.with_memory_space_constraint(array, pltpu.HBM)
    hbm = pl.BlockSpec(memory_space=pl.ANY)
    return pl.pallas_call(
        functools.partial(kernel, n_plane, n_z, n_sub, levels),
        out_shape=pltpu.VMEM((points, columns), F32),
        in_specs=[hbm, hbm, pl.BlockSpec(memory_space=pltpu.SMEM), hbm, hbm, hbm],
        out_specs=pl.BlockSpec(memory_space=pltpu.VMEM),
        scratch_shapes=scratch,
        compiler_params=pltpu.CompilerParams(
            collective_id=0, has_side_effects=True, vmem_limit_bytes=40 * 2**20),
    )(in_hbm(rhs_points), in_hbm(interp), skel_count, in_hbm(butterfly), in_hbm(project), in_hbm(root_inverse))


def solution(mesh):
    n_box, n_sub = mesh.shape["box"], mesh.shape["sub"]
    n_z = 8
    in_specs = (
        P(("box", "sub"), None),
        P(("box", "sub"), None),
        P("box"),
        P(None, "box", None),
        P("box", None),
        P(),
    )
    out_specs = P(("box", "sub"), None)
    return jax.shard_map(
        functools.partial(local, n_box // n_z, n_z, n_sub),
        mesh=mesh, in_specs=in_specs, out_specs=out_specs, check_vma=False)
```
